32 devices in a mesh: dp: 4 (over y, x), fsdp: 8 (over z, core).
Axes of the slice: x: 2, y: 2, z: 4, core: 2. Of those that a mesh axis runs over, the one named last changes fastest.
Arguments:
- tokens: bfloat16 [32, 1024, 1024], P(('dp', 'fsdp')), may hold values from -6 to 6
- lengths: int32 [32], P(('dp', 'fsdp')), may hold values from 300 to 1024, as said below
- cotangent: bfloat16 [32, 1024, 1024], P(('dp', 'fsdp')), may hold values from -6 to 6
- w_query: bfloat16 [1024, 1024], P(('dp', 'fsdp')), may hold values from -0.1875 to 0.1875
- w_key: bfloat16 [1024, 1024], P(('dp', 'fsdp')), may hold values from -0.1875 to 0.1875
- w_value: bfloat16 [1024, 1024], P(('dp', 'fsdp')), may hold values from -0.1875 to 0.1875
- w_gate: bfloat16 [1024, 1024], P(('dp', 'fsdp')), may hold values from -0.1875 to 0.1875
- w_out: bfloat16 [1024, 1024], P(('dp', 'fsdp')), may hold values from -0.25 to 0.25
- out_gain: bfloat16 [1024], P(('dp', 'fsdp')), may hold values from 0.099609375 to 1.8984375
- w_first: bfloat16 [1024, 2816], P(('dp', 'fsdp')), may hold values from -0.1875 to 0.1875
- w_second: bfloat16 [1024, 2816], P(('dp', 'fsdp')), may hold values from -0.1875 to 0.1875
- w_down: bfloat16 [2816, 1024], P(('dp', 'fsdp')), may hold values from -0.109375 to 0.109375
Outputs:
- layer_out: bfloat16 [32, 1024, 1024], P(('dp', 'fsdp'))
- input_grad: bfloat16 [32, 1024, 1024], P(('dp', 'fsdp'))
- grad_query: float32 [1024, 1024], P(('dp', 'fsdp'))
- grad_key: float32 [1024, 1024], P(('dp', 'fsdp'))
- grad_value: float32 [1024, 1024], P(('dp', 'fsdp'))
- grad_gate: float32 [1024, 1024], P(('dp', 'fsdp'))
- grad_out: float32 [1024, 1024], P(('dp', 'fsdp'))
- grad_gain: float32 [1024], P(('dp', 'fsdp'))
- grad_first: float32 [1024, 2816], P(('dp', 'fsdp'))
- grad_second: float32 [1024, 2816], P(('dp', 'fsdp'))
- grad_down: float32 [2816, 1024], P(('dp', 'fsdp'))
The draws below stay inside these ranges and needn't reach their ends.
Inputs may be any that keep to these rules, and one draw needn't show every extreme that they name: Slot s holds one sequence in its first lengths[s] positions and padding after it; some slot is exactly 1024 tokens long and some other exactly 300.
All inputs are finite; a program needn't handle non-finite values.
Results may differ from the reference program's by a relative error of at most 0.014.
Values may be sent and summed in bfloat16 or wider, within the bound.
A program may use at most 256 MiB of HBM per device.

```python
import math
import jax
import jax.numpy as jnp
from jax import lax

D = 1024
HEADS = 16
HEAD_DIM = 64
FF = 2816
BLOCK = 64
SLOT = 1024
MIN_LEN = 300
SLOTS = 32


def draw_lengths(key, part):
    key = jax.random.fold_in(key, 7)
    first_key, second_key = jax.random.split(key)
    drawn = jax.random.randint(first_key, (SLOTS,), MIN_LEN, SLOT + 1)
    order = jax.random.permutation(second_key, SLOTS)
    drawn = jnp.where(order == 0, SLOT, drawn)
    drawn = jnp.where(order == 1, MIN_LEN, drawn)
    return drawn.astype(jnp.int32)


def spiked(array, rng, source, target, parts, factor):
    def block_of(axis_at):
        return (jnp.arange(array.shape[axis_at]) // (array.shape[axis_at] // parts)).reshape((-1,) + (1,) * (array.ndim - 1 - axis_at))

    one_side = jax.random.permutation(rng, parts)[block_of(target)]
    second = (block_of(target) + parts // 2) % parts
    return jnp.where((block_of(source) == one_side) | (block_of(source) == second), factor * array, array)


def steps_of(stream_key, dims, shards, low, high):
    gain = 1.0
    for position, shards_of in shards:
        draws = jax.random.uniform(jax.random.fold_in(jax.random.fold_in(stream_key, 6), position), (shards_of,), jnp.float32, low / len(shards), high / len(shards))
        gain = gain * jnp.repeat(jnp.exp(draws), dims[position] // shards_of).reshape((-1,) + (1,) * (len(dims) - 1 - position))
    return gain


def centred(rng, dims, scale, bound, cuts=(), kind=jnp.bfloat16):
    array = jax.random.normal(rng, dims, jnp.float32) * scale
    if len(cuts) > 0:
        array = steps_of(rng, dims, cuts, -0.22, 0.18) * array
    return jnp.clip(array, min=-bound, max=bound).astype(kind)


def gaussian_with(own_key, dims, width, reach, cuts, heavy, kind=jnp.bfloat16):
    array = width * jax.random.normal(own_key, dims, jnp.float32)
    if cuts:
        array = array * steps_of(own_key, dims, cuts, -0.22, 0.18)
    return jnp.clip(spiked(array, jax.random.fold_in(own_key, 3), *heavy), -reach, reach).astype(kind)


def setup_inputs(seed: int = 0) -> dict:
    keys = jax.random.split(jax.random.key(seed), 13)
    tokens = gaussian_with(keys[0], (SLOTS, SLOT, D), 1.0, 6.0, ((0, 32),), (0, 2, 32, 2.75))
    lengths = draw_lengths(jax.random.fold_in(keys[12], 71), 0)
    cotangent = centred(keys[2], (SLOTS, SLOT, D), 1.0, 6.0, ((0, 32),))
    w_query = centred(keys[3], (D, D), D ** -0.5, 0.1875, ((0, 32),))
    w_key = centred(keys[4], (D, D), D ** -0.5, 0.1875, ((0, 32),))
    w_value = centred(keys[5], (D, D), D ** -0.5, 0.1875, ((0, 32),))
    w_gate = centred(keys[6], (D, D), D ** -0.5, 0.1875, ((0, 32),))
    w_out = centred(keys[7], (D, D), (D // 2) ** -0.5, 0.25, ((0, 32),))
    out_gain = jnp.clip(1.0 + 0.18 * jax.random.normal(keys[8], (D,), jnp.float32), 0.099609375, 1.8984375).astype(jnp.bfloat16)
    w_first = centred(keys[9], (D, FF), D ** -0.5, 0.1875, ((0, 32),))
    w_second = centred(keys[10], (D, FF), D ** -0.5, 0.1875, ((0, 32),))
    w_down = centred(keys[11], (FF, D), FF ** -0.5, 0.109375, ((0, 32),))
    return dict(tokens=tokens, lengths=lengths, cotangent=cotangent, w_query=w_query, w_key=w_key, w_value=w_value, w_gate=w_gate, w_out=w_out, out_gain=out_gain, w_first=w_first, w_second=w_second, w_down=w_down)


@jax.custom_vjp
def low(v):
    return lax.optimization_barrier(v.astype(jnp.bfloat16)).astype(jnp.float32)

@jax.custom_vjp
def low_back(v):
    return v

def low_keep(v):
    return (low(v), None)

def low_pass(kept, grad):
    return (grad,)

def back_keep(v):
    return (v, None)

def back_low(kept, grad):
    return (low(grad),)
low.defvjp(low_keep, low_pass)
low_back.defvjp(back_keep, back_low)
epsilon = 1e-06
masked_score = -1e+30
highest = lax.Precision.HIGHEST

def matmul(left_rows, right_rows):
    return jnp.dot(left_rows, right_rows, precision=highest, preferred_element_type=jnp.float32)

def normalize(values):
    return values * lax.rsqrt(lax.optimization_barrier(jnp.mean(values * values, axis=-1, keepdims=True)) + epsilon)

def split_heads(row_block):
    row_count = row_block.shape[0]
    return row_block.reshape(row_count // BLOCK, BLOCK, HEADS, HEAD_DIM)

def attend(query_rows, key_rows, value_rows):
    scores = jnp.einsum('bihd,bjhd->bhij', split_heads(query_rows), split_heads(key_rows), precision=highest) * HEAD_DIM ** (-0.5)
    scores = low_back(scores)
    causal = jnp.arange(BLOCK)[:, None] >= jnp.arange(BLOCK)[None, :]
    scores = jnp.where(causal, scores, masked_score)
    probs_low = low(jax.nn.softmax(scores, axis=-1))
    head_mix = jnp.einsum('bhij,bjhd->bihd', probs_low, split_heads(value_rows), precision=highest)
    return head_mix.reshape(query_rows.shape)

def forward(inputs, live_rows, w_query, w_key, w_value, w_gate, w_out, out_gain, w_first, w_second, w_down):
    first_in = low(normalize(inputs))
    query_rows = low_back(low(matmul(first_in, w_query)))
    key_rows = low_back(low(matmul(first_in, w_key)))
    value_rows = low_back(low(matmul(first_in, w_value)))
    gate_pre = low_back(matmul(first_in, w_gate))
    head_mix = low_back(attend(query_rows, key_rows, value_rows))
    branch_in = low(normalize(head_mix) * out_gain * jax.nn.silu(gate_pre))
    middle = inputs + live_rows * low_back(matmul(branch_in, w_out))
    second_in = low(normalize(middle))
    first_proj = low_back(matmul(second_in, w_first))
    second_proj = low_back(matmul(second_in, w_second))
    hidden = low(first_proj * second_proj)
    return middle + live_rows * low_back(matmul(hidden, w_down))

def reference(tokens, lengths, cotangent, w_query, w_key, w_value, w_gate, w_out, out_gain, w_first, w_second, w_down):
    weights = tuple((matrix.astype(jnp.float32) for matrix in (w_query, w_key, w_value, w_gate, w_out, out_gain, w_first, w_second, w_down)))
    group_size = math.gcd(SLOTS, max(1, 4096 // SLOT))
    blocks = SLOTS // group_size
    places = jnp.arange(SLOT, dtype=jnp.int32)
    live_all = (places[None, :] < lengths.astype(jnp.int32)[:, None]).astype(jnp.float32)

    def one_group(carried, slices_in):
        token_block, live_block, cot_block = slices_in
        inputs = token_block.reshape(group_size * SLOT, D).astype(jnp.float32)
        live_rows = live_block.reshape(group_size * SLOT, 1)

        def forward_rows(layer_in, *params):
            return forward(layer_in, live_rows, *params)
        final_rows, pullback = jax.vjp(forward_rows, inputs, *weights)
        gradients = pullback(cot_block.reshape(group_size * SLOT, D).astype(jnp.float32))
        summed = tuple((before + piece_grad for before, piece_grad in zip(carried, gradients[1:])))
        shaped_out = final_rows.astype(jnp.bfloat16).reshape(group_size, SLOT, D)
        shaped_grad = gradients[0].astype(jnp.bfloat16).reshape(group_size, SLOT, D)
        return (summed, (shaped_out, shaped_grad))
    initial = tuple((jnp.zeros(matrix.shape, jnp.float32) for matrix in weights))
    totals, (out_blocks, grad_blocks) = lax.scan(one_group, initial, (tokens.reshape(blocks, group_size, SLOT, D), live_all.reshape(blocks, group_size, SLOT), cotangent.reshape(blocks, group_size, SLOT, D)))
    return (out_blocks.reshape(SLOTS, SLOT, D), grad_blocks.reshape(SLOTS, SLOT, D), totals[0], totals[1], totals[2], totals[3], totals[4], totals[5], totals[6], totals[7], totals[8])
```

```python
import functools

import jax
import jax.numpy as jnp
from jax import lax
from jax.experimental import pallas as pl
from jax.experimental.pallas import tpu as pltpu
from jax.sharding import PartitionSpec as P

HEADS = 16
HEAD_DIM = 64
BLOCK = 64


epsilon = 1e-06
masked_score = -1e30


def normalize(values):
    inv_rms = lax.rsqrt(jnp.mean(values * values, axis=-1, keepdims=True) + epsilon)
    return (values * inv_rms, inv_rms)


def norm_back(normed, inv_rms, upstream):
    return inv_rms * (upstream - normed * jnp.mean(upstream * normed, axis=-1, keepdims=True))


def project(left_rows, right_rows):
    return jnp.dot(left_rows, right_rows, preferred_element_type=jnp.float32)


def project_back(upstream, weight):
    return lax.dot_general(
        upstream, weight, (((1,), (1,)), ((), ())), preferred_element_type=jnp.float32
    )


def weight_grad(inputs, upstream):
    return lax.dot_general(
        inputs, upstream, (((0,), (0,)), ((), ())), preferred_element_type=jnp.float32
    )


def split_heads(row_block):
    row_count = row_block.shape[0]
    return row_block.reshape(row_count // BLOCK, BLOCK, HEADS, HEAD_DIM)


def block_scores(query_blocks, key_blocks):
    scores = jnp.einsum(
        "bihd,bjhd->bhij", query_blocks, key_blocks, preferred_element_type=jnp.float32
    ) * HEAD_DIM ** (-0.5)
    causal = lax.broadcasted_iota(jnp.int32, (BLOCK, BLOCK), 0) >= lax.broadcasted_iota(
        jnp.int32, (BLOCK, BLOCK), 1
    )
    return jnp.where(causal, scores, masked_score)


def attend(query_rows, key_rows, value_rows):
    scores = block_scores(split_heads(query_rows), split_heads(key_rows))
    row_max = jnp.max(scores, axis=-1, keepdims=True)
    exp_scores = jnp.exp(scores - row_max)
    row_total = jnp.sum(exp_scores, axis=-1, keepdims=True)
    probs_low = (exp_scores / row_total).astype(jnp.bfloat16)
    head_mix = jnp.einsum(
        "bhij,bjhd->bihd", probs_low, split_heads(value_rows), preferred_element_type=jnp.float32
    )
    return (head_mix.reshape(query_rows.shape[0], -1), row_max + jnp.log(row_total))


def attend_back(query_rows, key_rows, value_rows, logsum, grad_mix):
    query_blocks = split_heads(query_rows)
    key_blocks = split_heads(key_rows)
    value_blocks = split_heads(value_rows)
    grad_blocks = split_heads(grad_mix)
    probs = jnp.exp(block_scores(query_blocks, key_blocks) - logsum)
    probs_low = probs.astype(jnp.bfloat16)
    grad_probs = jnp.einsum(
        "bihd,bjhd->bhij", grad_blocks, value_blocks, preferred_element_type=jnp.float32
    )
    grad_values = jnp.einsum(
        "bhij,bihd->bjhd", probs_low, grad_blocks, preferred_element_type=jnp.float32
    )
    grad_scores = (
        probs * (grad_probs - jnp.sum(grad_probs * probs, axis=-1, keepdims=True))
    ).astype(jnp.bfloat16)
    scale_factor = HEAD_DIM ** (-0.5)
    grad_queries = (
        jnp.einsum("bhij,bjhd->bihd", grad_scores, key_blocks, preferred_element_type=jnp.float32)
        * scale_factor
    )
    grad_keys = (
        jnp.einsum("bhij,bihd->bjhd", grad_scores, query_blocks, preferred_element_type=jnp.float32)
        * scale_factor
    )
    row_count = query_rows.shape[0]
    return (
        grad_queries.reshape(row_count, -1).astype(jnp.bfloat16),
        grad_keys.reshape(row_count, -1).astype(jnp.bfloat16),
        grad_values.reshape(row_count, -1).astype(jnp.bfloat16),
    )


def ffn_sums(second_in, hidden, grad_first_proj, grad_second_proj, grad_branch):
    both_proj = jnp.concatenate([grad_first_proj, grad_second_proj], axis=1)
    inner_shard = lax.psum_scatter(
        weight_grad(second_in, both_proj), ("dp", "fsdp"), scatter_dimension=0, tiled=True
    )
    down_shard = lax.psum_scatter(
        weight_grad(hidden, grad_branch), ("dp", "fsdp"), scatter_dimension=0, tiled=True
    )
    ff_width = grad_first_proj.shape[1]
    return (inner_shard[:, :ff_width], inner_shard[:, ff_width:], down_shard)


def general_body(
    tokens,
    lengths,
    cotangent,
    w_query,
    w_key,
    w_value,
    w_gate,
    w_out,
    out_gain,
    w_first,
    w_second,
    w_down,
):
    slot_count, slot_len, feature_width = tokens.shape
    row_count = slot_count * slot_len
    places = lax.broadcasted_iota(jnp.int32, (slot_count, slot_len), 1)
    live_rows = (places < lengths[:, None]).astype(jnp.float32).reshape(row_count, 1)
    attn_full = (
        lax.all_gather(w_query, ("dp", "fsdp"), axis=0, tiled=True),
        lax.all_gather(w_key, ("dp", "fsdp"), axis=0, tiled=True),
        lax.all_gather(w_value, ("dp", "fsdp"), axis=0, tiled=True),
        lax.all_gather(w_gate, ("dp", "fsdp"), axis=0, tiled=True),
        lax.all_gather(w_out, ("dp", "fsdp"), axis=0, tiled=True),
        lax.all_gather(out_gain, ("dp", "fsdp"), axis=0, tiled=True),
    )
    ffn_full = (
        lax.all_gather(w_first, ("dp", "fsdp"), axis=0, tiled=True),
        lax.all_gather(w_second, ("dp", "fsdp"), axis=0, tiled=True),
        lax.all_gather(w_down, ("dp", "fsdp"), axis=0, tiled=True),
    )
    query_full, key_full, value_full, gate_full, out_full, gain_full = attn_full
    first_full, second_full, down_full = ffn_full
    inputs = tokens.reshape(row_count, feature_width).astype(jnp.float32)
    normed_in, inv_in = normalize(inputs)
    first_in = normed_in.astype(jnp.bfloat16)
    query_rows = project(first_in, query_full).astype(jnp.bfloat16)
    key_rows = project(first_in, key_full).astype(jnp.bfloat16)
    value_rows = project(first_in, value_full).astype(jnp.bfloat16)
    gate_pre = project(first_in, gate_full)
    head_mix, logsum = attend(query_rows, key_rows, value_rows)
    normed_mix, inv_mix = normalize(head_mix)
    gain_rows = gain_full.astype(jnp.float32)
    gate_act = jax.nn.silu(gate_pre)
    scaled_mix = normed_mix * gain_rows
    branch_in = (scaled_mix * gate_act).astype(jnp.bfloat16)
    middle = inputs + live_rows * project(branch_in, out_full)
    normed_mid, inv_mid = normalize(middle)
    second_in = normed_mid.astype(jnp.bfloat16)
    first_proj = project(second_in, first_full)
    second_proj = project(second_in, second_full)
    hidden = (first_proj * second_proj).astype(jnp.bfloat16)
    final_rows = middle + live_rows * project(hidden, down_full)
    layer_out = final_rows.astype(jnp.bfloat16).reshape(tokens.shape)
    first_back, second_back, down_back = (
        lax.all_gather(w_first, ("dp", "fsdp"), axis=0, tiled=True),
        lax.all_gather(w_second, ("dp", "fsdp"), axis=0, tiled=True),
        lax.all_gather(w_down, ("dp", "fsdp"), axis=0, tiled=True),
    )
    query_back, key_back, value_back, gate_back, out_back, gain_back = (
        lax.all_gather(w_query, ("dp", "fsdp"), axis=0, tiled=True),
        lax.all_gather(w_key, ("dp", "fsdp"), axis=0, tiled=True),
        lax.all_gather(w_value, ("dp", "fsdp"), axis=0, tiled=True),
        lax.all_gather(w_gate, ("dp", "fsdp"), axis=0, tiled=True),
        lax.all_gather(w_out, ("dp", "fsdp"), axis=0, tiled=True),
        lax.all_gather(out_gain, ("dp", "fsdp"), axis=0, tiled=True),
    )
    gain_used = gain_back.astype(jnp.float32)
    grad_final = cotangent.reshape(row_count, feature_width).astype(jnp.float32)
    grad_branch = (live_rows * grad_final).astype(jnp.bfloat16)
    grad_hidden = project_back(grad_branch, down_back)
    grad_first_proj = (grad_hidden * second_proj).astype(jnp.bfloat16)
    grad_second_proj = (grad_hidden * first_proj).astype(jnp.bfloat16)
    grad_normed_mid = project_back(grad_first_proj, first_back) + project_back(
        grad_second_proj, second_back
    )
    grad_middle = grad_final + norm_back(normed_mid, inv_mid, grad_normed_mid)
    grad_attn_out = (live_rows * grad_middle).astype(jnp.bfloat16)
    grad_branch_in = project_back(grad_attn_out, out_back)
    gain_terms = grad_branch_in * gate_act * normed_mix
    sigmoid_gate = jax.nn.sigmoid(gate_pre)
    grad_gate_pre = (
        grad_branch_in * scaled_mix * sigmoid_gate * (1.0 + gate_pre * (1.0 - sigmoid_gate))
    ).astype(jnp.bfloat16)
    grad_scaled = grad_branch_in * gate_act * gain_used
    grad_mix = norm_back(normed_mix, inv_mix, grad_scaled).astype(jnp.bfloat16)
    grad_queries, grad_keys, grad_values = attend_back(
        query_rows, key_rows, value_rows, logsum, grad_mix
    )
    grad_normed_in = (
        project_back(grad_queries, query_back)
        + project_back(grad_keys, key_back)
        + project_back(grad_values, value_back)
        + project_back(grad_gate_pre, gate_back)
    )
    grad_inputs = grad_middle + norm_back(normed_in, inv_in, grad_normed_in)
    input_grad = grad_inputs.astype(jnp.bfloat16).reshape(tokens.shape)
    ffn_shards = ffn_sums(second_in, hidden, grad_first_proj, grad_second_proj, grad_branch)
    four_grads = jnp.concatenate([grad_queries, grad_keys, grad_values, grad_gate_pre], axis=1)
    from_input = weight_grad(first_in, four_grads)
    from_branch = weight_grad(branch_in, grad_attn_out)
    gain_part = jnp.sum(gain_terms, axis=0)[:, None]
    attn_shard = lax.psum_scatter(
        jnp.concatenate([from_input, from_branch, gain_part], axis=1),
        ("dp", "fsdp"),
        scatter_dimension=0,
        tiled=True,
    )
    shard_query = attn_shard[:, 0:feature_width]
    shard_key = attn_shard[:, feature_width : 2 * feature_width]
    shard_value = attn_shard[:, 2 * feature_width : 3 * feature_width]
    shard_gate = attn_shard[:, 3 * feature_width : 4 * feature_width]
    shard_out = attn_shard[:, 4 * feature_width : 5 * feature_width]
    shard_gain = attn_shard[:, 5 * feature_width]
    shard_first, shard_second, shard_down = ffn_shards
    return (
        layer_out,
        input_grad,
        shard_query,
        shard_key,
        shard_value,
        shard_gate,
        shard_out,
        shard_gain,
        shard_first,
        shard_second,
        shard_down,
    )


MESH = pl.DeviceIdType.MESH
f32 = jnp.float32
bf16 = jnp.bfloat16


class Place:
    def __init__(self):
        dp, fs = lax.axis_index("dp"), lax.axis_index("fsdp")
        z, c = lax.div(fs, 2), lax.rem(fs, 2)
        self.dp, self.fs, self.z, self.c = dp, fs, z, c
        self.nx = dp + 1 - 2 * lax.rem(dp, 2)
        self.ny = lax.rem(dp + 2, 4)
        self.dg = lax.rem(self.nx + 2, 4)
        self.zp = [lax.rem(z + k, 4) for k in (1, 2, 3)]
        self.sib = (dp, z * 2 + 1 - c)
        self.zdev = [(dp, zz * 2 + c) for zz in self.zp]
        self.xdev, self.ydev = (self.nx, fs), (self.ny, fs)
        self.peers = [self.sib, self.xdev, self.ydev] + self.zdev

    def barrier(self):
        bar = pltpu.get_barrier_semaphore()
        for d in self.peers:
            pl.semaphore_signal(bar, inc=1, device_id=d, device_id_type=MESH)
        pl.semaphore_wait(bar, 6)


class Gather:
    def __init__(self, here, shards, outs, ssem, rsem, lsem):
        self.h, self.shards, self.outs = here, shards, outs
        self.ssem, self.rsem, self.lsem = ssem, rsem, lsem
        self.sends = []

    def rc(self, i, k, src, dst, dev):
        return pltpu.make_async_remote_copy(
            src_ref=src, dst_ref=dst, send_sem=self.ssem.at[i, k], recv_sem=self.rsem.at[i, k],
            device_id=dev, device_id_type=MESH,
        )

    def go(self, m):
        m.start()
        self.sends.append(m)

    def own(self, i):
        h = self.h
        return pltpu.make_async_copy(self.shards[i], self.outs[i].at[h.dp, h.z, h.c], self.lsem.at[i])

    def zmsg(self, i, k):
        h = self.h
        return self.rc(i, k, self.shards[i], self.outs[i].at[h.dp, h.z, h.c], h.zdev[k])

    def col(self, i, k, yx, dev):
        r = self.outs[i].at[yx, :, self.h.c]
        return self.rc(i, k, r, r, dev)

    def half(self, i, k, yx, lo, dev):
        r = self.outs[i].at[yx, lo : lo + 2, self.h.c]
        return self.rc(i, k, r, r, dev)

    def step0(self, i):
        self.own(i).start()
        for k in range(3):
            self.go(self.zmsg(i, k))

    def step1(self, i):
        h = self.h
        self.own(i).wait()
        for k in range(3):
            self.zmsg(i, k).wait_recv()
        self.go(self.col(i, 3, h.dp, h.xdev))
        self.go(self.col(i, 4, h.dp, h.ydev))
        self.go(self.col(i, 7, h.dp, h.sib))

    def step2(self, i):
        h = self.h
        self.col(i, 3, h.dp, h.xdev).wait_recv()
        self.go(self.half(i, 6, h.nx, 2, h.ydev))
        self.go(self.col(i, 8, h.nx, h.sib))
        self.col(i, 4, h.dp, h.ydev).wait_recv()
        self.go(self.half(i, 5, h.ny, 0, h.xdev))
        self.go(self.col(i, 9, h.ny, h.sib))

    def step3(self, i):
        h = self.h
        self.half(i, 5, h.ny, 0, h.xdev).wait_recv()
        self.half(i, 6, h.nx, 2, h.ydev).wait_recv()
        self.go(self.col(i, 10, h.dg, h.sib))

    def step4(self, i):
        h = self.h
        for k in (7, 8, 9, 10):
            self.col(i, k, h.dp, h.sib).wait_recv()

    def finish(self):
        for m in self.sends:
            m.wait_send()


def gather_kernel(n, *refs):
    here = Place()
    here.barrier()
    ag = Gather(here, refs[:n], refs[n : 2 * n], *refs[2 * n :])
    stages = ((0, ag.step0), (1, ag.step1), (2, ag.step2), (3, ag.step3), (4, ag.step4))
    for t in range(n + 4):
        for off, f in stages:
            if 0 <= t - off < n:
                f(t - off)
    ag.finish()


def gather(shards):
    n = len(shards)
    hbm = pl.BlockSpec(memory_space=pl.ANY)
    return pl.pallas_call(
        functools.partial(gather_kernel, n),
        out_shape=[jax.ShapeDtypeStruct((4, 4, 2) + s.shape, s.dtype) for s in shards],
        in_specs=[hbm] * n,
        out_specs=[hbm] * n,
        scratch_shapes=[
            pltpu.SemaphoreType.DMA((n, 11)), pltpu.SemaphoreType.DMA((n, 11)), pltpu.SemaphoreType.DMA((n,)),
        ],
        compiler_params=pltpu.CompilerParams(collective_id=0, has_side_effects=True),
    )(*shards)


class Scatter:
    def __init__(self, here, items, bufs, ssem, rsem, lsem, free):
        self.h, self.items, self.bufs = here, items, bufs
        self.ssem, self.rsem, self.lsem, self.free = ssem, rsem, lsem, free
        self.sends = {}

    def rc(self, i, k, src, dst, dev):
        return pltpu.make_async_remote_copy(
            src_ref=src, dst_ref=dst, send_sem=self.ssem.at[i, k], recv_sem=self.rsem.at[i, k],
            device_id=dev, device_id_type=MESH,
        )

    def go(self, i, *moves):
        for m in moves:
            m.start()
            self.sends.setdefault(i, []).append(m)

    def views(self, i):
        it = self.items[i]
        return it, self.bufs[it["cls"]], it["slot"], it["w"]

    def m_sib(self, i):
        it, b, s, w = self.views(i)
        src = it["g"].at[:, :, 1 - self.h.c, :, pl.ds(it["c0"], w)]
        return self.rc(i, 0, src, b["r1"].at[s, :, :, :, 0:w], self.h.sib)

    def m_load(self, i):
        it, b, s, w = self.views(i)
        src = it["g"].at[:, :, self.h.c, :, pl.ds(it["c0"], w)]
        return pltpu.make_async_copy(src, b["p"].at[s, :, :, :, 0:w], self.lsem.at[i])

    def m_dx(self, i):
        it, b, s, w = self.views(i)
        return self.rc(i, 1, b["p"].at[s, self.h.dg, 0:2, :, 0:w], b["rd"].at[s, 0, :, :, 0:w], self.h.xdev)

    def m_dy(self, i):
        it, b, s, w = self.views(i)
        return self.rc(i, 2, b["p"].at[s, self.h.dg, 2:4, :, 0:w], b["rd"].at[s, 1, :, :, 0:w], self.h.ydev)

    def m_x(self, i):
        it, b, s, w = self.views(i)
        return self.rc(i, 3, b["p"].at[s, self.h.nx, :, :, 0:w], b["rxy"].at[s, 0, :, :, 0:w], self.h.xdev)

    def m_y(self, i):
        it, b, s, w = self.views(i)
        return self.rc(i, 4, b["p"].at[s, self.h.ny, :, :, 0:w], b["rxy"].at[s, 1, :, :, 0:w], self.h.ydev)

    def m_z(self, i, k):
        it, b, s, w = self.views(i)
        return self.rc(
            i, 5 + k, b["p"].at[s, self.h.dp, self.h.zp[k], :, 0:w], b["rz"].at[s, k, :, 0:w], self.h.zdev[k]
        )

    def step0(self, i):
        it = self.items[i]
        if it["wait_free"] is not None:
            for m in self.sends.pop(it["wait_free"]):
                m.wait_send()
            for k in range(6):
                pl.semaphore_wait(self.free.at[k], 1)
        self.m_load(i).start()
        self.go(i, self.m_sib(i))

    def step1(self, i):
        it, b, s, w = self.views(i)
        p, r, dg = b["p"], b["r1"], self.h.dg
        self.m_load(i).wait()
        self.m_sib(i).wait_recv()

        def far(j, _):
            p[s, dg, j, :, 0:w] = p[s, dg, j, :, 0:w] + r[s, dg, j, :, 0:w]
            return 0

        lax.fori_loop(0, 4, far, 0)
        self.go(i, self.m_dx(i), self.m_dy(i))

        def near(j, _):
            a, q = lax.rem(dg + 1 + lax.div(j, 4), 4), lax.rem(j, 4)
            p[s, a, q, :, 0:w] = p[s, a, q, :, 0:w] + r[s, a, q, :, 0:w]
            return 0

        lax.fori_loop(0, 12, near, 0)

    def step2(self, i):
        it, b, s, w = self.views(i)
        p, rd, nx, ny = b["p"], b["rd"], self.h.nx, self.h.ny
        self.m_dx(i).wait_recv()

        def to_y(j, _):
            p[s, ny, j, :, 0:w] = p[s, ny, j, :, 0:w] + rd[s, 0, j, :, 0:w]
            return 0

        lax.fori_loop(0, 2, to_y, 0)
        self.go(i, self.m_y(i))
        self.m_dy(i).wait_recv()

        def to_x(j, _):
            p[s, nx, 2 + j, :, 0:w] = p[s, nx, 2 + j, :, 0:w] + rd[s, 1, j, :, 0:w]
            return 0

        lax.fori_loop(0, 2, to_x, 0)
        self.go(i, self.m_x(i))

    def step3(self, i):
        it, b, s, w = self.views(i)
        p, rxy, dp = b["p"], b["rxy"], self.h.dp
        self.m_x(i).wait_recv()
        self.m_y(i).wait_recv()

        def own(j, _):
            both = rxy[s, 0, j, :, 0:w].astype(f32) + rxy[s, 1, j, :, 0:w].astype(f32)
            p[s, dp, j, :, 0:w] = (p[s, dp, j, :, 0:w].astype(f32) + both).astype(p.dtype)
            return 0

        lax.fori_loop(0, 4, own, 0)
        self.go(i, *[self.m_z(i, k) for k in range(3)])

    def step4(self, i):
        it, b, s, w = self.views(i)
        p, rz = b["p"], b["rz"]
        for k in range(3):
            self.m_z(i, k).wait_recv()
        total = p[s, self.h.dp, self.h.z, :, 0:w].astype(f32)
        for k in range(3):
            total = total + rz[s, k, :, 0:w].astype(f32)
        it["out"][:, it["oc"] : it["oc"] + w] = total
        if it["signal_free"]:
            for k, d in enumerate(self.h.peers):
                pl.semaphore_signal(self.free.at[k if k < 3 else 8 - k], inc=1, device_id=d, device_id_type=MESH)

    def finish(self):
        for i in list(self.sends):
            for m in self.sends.pop(i):
                m.wait_send()


def scatter_plan(specs, ring):
    items, by_class = [], {}
    for gi, c0, w, cls in specs:
        mine = by_class.setdefault(cls, [])
        it = dict(gi=gi, c0=c0, w=w, cls=cls, oc=c0, slot=len(mine) % ring[cls], wait_free=None, signal_free=False)
        if len(mine) >= ring[cls]:
            it["wait_free"] = mine[-ring[cls]]
            items[it["wait_free"]]["signal_free"] = True
        mine.append(len(items))
        items.append(it)
    return items


SCATTER_BUFFERS = ("p", "r1", "rd", "rxy", "rz")


def scatter_scratch(slots, r, w, dt):
    return [
        pltpu.VMEM((slots, 4, 4, r, w), dt), pltpu.VMEM((slots, 4, 4, r, w), dt), pltpu.VMEM((slots, 2, 2, r, w), dt),
        pltpu.VMEM((slots, 2, 4, r, w), dt), pltpu.VMEM((slots, 3, r, w), dt),
    ]


def scatter_kernel(items, ng, classes, *refs):
    gs, outs, rest = refs[:ng], refs[ng : 2 * ng], list(refs[2 * ng :])
    bufs = {}
    for cls in classes:
        bufs[cls] = dict(zip(SCATTER_BUFFERS, rest[:5]))
        rest = rest[5:]
    here = Place()
    here.barrier()
    items = [dict(it, g=gs[it["gi"]], out=outs[it["gi"]]) for it in items]
    rs = Scatter(here, items, bufs, *rest)
    n = len(items)
    for t in range(n + 4):
        for off, f in enumerate((rs.step0, rs.step1, rs.step2, rs.step3, rs.step4)):
            if 0 <= t - off < n:
                f(t - off)
    rs.finish()


def reduce_scatter(gs, specs, ring, shapes):
    items = scatter_plan(specs, ring)
    n, classes, scratch = len(items), list(ring), []
    for cls in classes:
        scratch += scatter_scratch(ring[cls], *shapes[cls])
    scratch += [
        pltpu.SemaphoreType.DMA((n, 8)), pltpu.SemaphoreType.DMA((n, 8)), pltpu.SemaphoreType.DMA((n,)),
        pltpu.SemaphoreType.REGULAR((6,)),
    ]
    return pl.pallas_call(
        functools.partial(scatter_kernel, items, len(gs), classes),
        out_shape=[jax.ShapeDtypeStruct(g.shape[3:], f32) for g in gs],
        in_specs=[pl.BlockSpec(memory_space=pl.ANY)] * len(gs),
        out_specs=[pl.BlockSpec(memory_space=pltpu.VMEM)] * len(gs),
        scratch_shapes=scratch,
        compiler_params=pltpu.CompilerParams(collective_id=1, has_side_effects=True, vmem_limit_bytes=58 * 2**20),
    )(*gs)


def blocks(grad):
    return grad.reshape((4, 4, 2, grad.shape[0] // 32, grad.shape[1]))


def column_parts(width, part):
    return [(c0, min(part, width - c0)) for c0 in range(0, width, part)]


def slice_body(
    tokens, lengths, cotangent, w_query, w_key, w_value, w_gate, w_out, out_gain, w_first, w_second, w_down,
):
    slot_count, slot_len, feature_width = tokens.shape
    row_count = slot_count * slot_len
    ff_width = w_first.shape[1]
    places = lax.broadcasted_iota(jnp.int32, (slot_count, slot_len), 1)
    live_rows = (places < lengths[:, None]).astype(f32).reshape(row_count, 1)
    me = lax.axis_index("dp") * 8 + lax.axis_index("fsdp")
    lane = lax.broadcasted_iota(jnp.int32, (16, 128), 1)
    gain_block = jnp.where(lax.div(lane, 32) == lax.rem(me, 4), jnp.tile(out_gain, 4)[None, :], 0)
    full = gather((w_query, w_key, w_value, w_gate, gain_block, w_out, w_first, w_second, w_down))
    gain_full = full[4].reshape(8, 4, 16, 128)[:, :, 0].sum(axis=1).reshape(feature_width)
    query_full, key_full, value_full, gate_full, _, out_full, first_full, second_full, down_full = [
        w.reshape(-1, w.shape[-1]) for w in full
    ]
    inputs = tokens.reshape(row_count, feature_width).astype(f32)
    normed_in, inv_in = normalize(inputs)
    first_in = normed_in.astype(bf16)
    query_rows = project(first_in, query_full).astype(bf16)
    key_rows = project(first_in, key_full).astype(bf16)
    value_rows = project(first_in, value_full).astype(bf16)
    gate_pre = project(first_in, gate_full)
    head_mix, logsum = attend(query_rows, key_rows, value_rows)
    normed_mix, inv_mix = normalize(head_mix)
    gain_rows = gain_full.astype(f32)
    gate_act = jax.nn.silu(gate_pre)
    scaled_mix = normed_mix * gain_rows
    branch_in = (scaled_mix * gate_act).astype(bf16)
    middle = inputs + live_rows * project(branch_in, out_full)
    normed_mid, inv_mid = normalize(middle)
    second_in = normed_mid.astype(bf16)
    first_proj = project(second_in, first_full)
    second_proj = project(second_in, second_full)
    hidden = (first_proj * second_proj).astype(bf16)
    final_rows = middle + live_rows * project(hidden, down_full)
    layer_out = final_rows.astype(bf16).reshape(tokens.shape)
    grad_final = cotangent.reshape(row_count, feature_width).astype(f32)
    grad_branch = (live_rows * grad_final).astype(bf16)
    grad_hidden = project_back(grad_branch, down_full)
    grad_first_proj = (grad_hidden * second_proj).astype(bf16)
    grad_second_proj = (grad_hidden * first_proj).astype(bf16)
    grad_normed_mid = project_back(grad_first_proj, first_full) + project_back(grad_second_proj, second_full)
    grad_middle = grad_final + norm_back(normed_mid, inv_mid, grad_normed_mid)
    grad_attn_out = (live_rows * grad_middle).astype(bf16)
    grad_branch_in = project_back(grad_attn_out, out_full)
    gain_terms = grad_branch_in * gate_act * normed_mix
    sigmoid_gate = jax.nn.sigmoid(gate_pre)
    grad_gate_pre = (
        grad_branch_in * scaled_mix * sigmoid_gate * (1.0 + gate_pre * (1.0 - sigmoid_gate))
    ).astype(bf16)
    grad_scaled = grad_branch_in * gate_act * gain_rows
    grad_mix = norm_back(normed_mix, inv_mix, grad_scaled).astype(bf16)
    grad_queries, grad_keys, grad_values = attend_back(query_rows, key_rows, value_rows, logsum, grad_mix)
    grad_normed_in = (
        project_back(grad_queries, query_full) + project_back(grad_keys, key_full)
        + project_back(grad_values, value_full) + project_back(grad_gate_pre, gate_full)
    )
    grad_inputs = grad_middle + norm_back(normed_in, inv_in, grad_normed_in)
    input_grad = grad_inputs.astype(bf16).reshape(tokens.shape)
    gain_part = gain_terms.reshape(row_count // 8, 8, feature_width).sum(axis=0)
    gain_blocks = jnp.repeat(gain_part.reshape(8, 8, 128).transpose(1, 0, 2), 4, axis=0).reshape(4, 4, 2, 8, 128)
    gs = [blocks(weight_grad(a, b).astype(bf16)) for a, b in (
        (hidden, grad_branch), (second_in, grad_first_proj), (second_in, grad_second_proj),
        (branch_in, grad_attn_out), (first_in, grad_gate_pre), (first_in, grad_queries),
        (first_in, grad_keys), (first_in, grad_values),
    )] + [gain_blocks]
    specs = [(0, c0, w, "down") for c0, w in column_parts(feature_width, 512)]
    for g in (1, 2):
        specs += [(g, c0, w, "in") for c0, w in column_parts(ff_width, 1024)]
    specs += [(g, 0, feature_width, "in") for g in (3, 4, 5, 6, 7)] + [(8, 0, 128, "gain")]
    down, first, second, out, gate, query, key, value, gain = reduce_scatter(
        gs, specs, {"down": 2, "in": 5, "gain": 1},
        {"down": (w_down.shape[0], 512, bf16), "in": (w_query.shape[0], 1024, bf16), "gain": (8, 128, f32)},
    )
    gain = lax.dynamic_slice(gain.sum(axis=0), (lax.rem(me, 4) * 32,), (32,))
    return layer_out, input_grad, query, key, value, gate, out, gain, first, second, down


def solution(mesh):
    fits = mesh.shape["dp"] == 4 and mesh.shape["fsdp"] == 8
    return jax.shard_map(
        slice_body if fits else general_body,
        mesh=mesh,
        in_specs=(
            P(("dp", "fsdp"), None, None),
            P(("dp", "fsdp")),
            P(("dp", "fsdp"), None, None),
            P(("dp", "fsdp"), None),
            P(("dp", "fsdp"), None),
            P(("dp", "fsdp"), None),
            P(("dp", "fsdp"), None),
            P(("dp", "fsdp"), None),
            P(("dp", "fsdp")),
            P(("dp", "fsdp"), None),
            P(("dp", "fsdp"), None),
            P(("dp", "fsdp"), None),
        ),
        out_specs=(
            P(("dp", "fsdp"), None, None),
            P(("dp", "fsdp"), None, None),
            P(("dp", "fsdp"), None),
            P(("dp", "fsdp"), None),
            P(("dp", "fsdp"), None),
            P(("dp", "fsdp"), None),
            P(("dp", "fsdp"), None),
            P(("dp", "fsdp")),
            P(("dp", "fsdp"), None),
            P(("dp", "fsdp"), None),
            P(("dp", "fsdp"), None),
        ),
        check_vma=False,
    )
```

```python
import functools
from types import SimpleNamespace

import jax
import jax.numpy as jnp
from jax import lax
from jax.experimental import pallas as pl
from jax.experimental.pallas import tpu as pltpu
from jax.sharding import PartitionSpec as P

AXES = ("dp", "fsdp")
HEADS = 16
HEAD_DIM = 64
BLOCK = 64


epsilon = 1e-06
masked_score = -1e30


def normalize(values):
    inv_rms = lax.rsqrt(jnp.mean(values * values, axis=-1, keepdims=True) + epsilon)
    return (values * inv_rms, inv_rms)


def norm_back(normed, inv_rms, upstream):
    return inv_rms * (upstream - normed * jnp.mean(upstream * normed, axis=-1, keepdims=True))


def project(left_rows, right_rows):
    return jnp.dot(left_rows, right_rows, preferred_element_type=jnp.float32)


def project_back(upstream, weight):
    return lax.dot_general(
        upstream, weight, (((1,), (1,)), ((), ())), preferred_element_type=jnp.float32
    )


def weight_grad(inputs, upstream):
    return lax.dot_general(
        inputs, upstream, (((0,), (0,)), ((), ())), preferred_element_type=jnp.float32
    )


def split_heads(row_block):
    row_count = row_block.shape[0]
    return row_block.reshape(row_count // BLOCK, BLOCK, HEADS, HEAD_DIM)


def block_scores(query_blocks, key_blocks):
    scores = jnp.einsum(
        "bihd,bjhd->bhij", query_blocks, key_blocks, preferred_element_type=jnp.float32
    ) * HEAD_DIM ** (-0.5)
    causal = lax.broadcasted_iota(jnp.int32, (BLOCK, BLOCK), 0) >= lax.broadcasted_iota(
        jnp.int32, (BLOCK, BLOCK), 1
    )
    return jnp.where(causal, scores, masked_score)


def attend(query_rows, key_rows, value_rows):
    scores = block_scores(split_heads(query_rows), split_heads(key_rows))
    row_max = jnp.max(scores, axis=-1, keepdims=True)
    exp_scores = jnp.exp(scores - row_max)
    row_total = jnp.sum(exp_scores, axis=-1, keepdims=True)
    probs_low = (exp_scores / row_total).astype(jnp.bfloat16)
    head_mix = jnp.einsum(
        "bhij,bjhd->bihd", probs_low, split_heads(value_rows), preferred_element_type=jnp.float32
    )
    return (head_mix.reshape(query_rows.shape[0], -1), row_max + jnp.log(row_total))


def attend_back(query_rows, key_rows, value_rows, logsum, grad_mix):
    query_blocks = split_heads(query_rows)
    key_blocks = split_heads(key_rows)
    value_blocks = split_heads(value_rows)
    grad_blocks = split_heads(grad_mix)
    probs = jnp.exp(block_scores(query_blocks, key_blocks) - logsum)
    probs_low = probs.astype(jnp.bfloat16)
    grad_probs = jnp.einsum(
        "bihd,bjhd->bhij", grad_blocks, value_blocks, preferred_element_type=jnp.float32
    )
    grad_values = jnp.einsum(
        "bhij,bihd->bjhd", probs_low, grad_blocks, preferred_element_type=jnp.float32
    )
    grad_scores = (
        probs * (grad_probs - jnp.sum(grad_probs * probs, axis=-1, keepdims=True))
    ).astype(jnp.bfloat16)
    scale_factor = HEAD_DIM ** (-0.5)
    grad_queries = (
        jnp.einsum("bhij,bjhd->bihd", grad_scores, key_blocks, preferred_element_type=jnp.float32)
        * scale_factor
    )
    grad_keys = (
        jnp.einsum("bhij,bihd->bjhd", grad_scores, query_blocks, preferred_element_type=jnp.float32)
        * scale_factor
    )
    row_count = query_rows.shape[0]
    return (
        grad_queries.reshape(row_count, -1).astype(jnp.bfloat16),
        grad_keys.reshape(row_count, -1).astype(jnp.bfloat16),
        grad_values.reshape(row_count, -1).astype(jnp.bfloat16),
    )


def ffn_sums(second_in, hidden, grad_first_proj, grad_second_proj, grad_branch):
    both_proj = jnp.concatenate([grad_first_proj, grad_second_proj], axis=1)
    inner_shard = lax.psum_scatter(
        weight_grad(second_in, both_proj), AXES, scatter_dimension=0, tiled=True
    )
    down_shard = lax.psum_scatter(
        weight_grad(hidden, grad_branch), AXES, scatter_dimension=0, tiled=True
    )
    ff_width = grad_first_proj.shape[1]
    return (inner_shard[:, :ff_width], inner_shard[:, ff_width:], down_shard)


def general_body(
    tokens,
    lengths,
    cotangent,
    w_query,
    w_key,
    w_value,
    w_gate,
    w_out,
    out_gain,
    w_first,
    w_second,
    w_down,
):
    slot_count, slot_len, feature_width = tokens.shape
    row_count = slot_count * slot_len
    places = lax.broadcasted_iota(jnp.int32, (slot_count, slot_len), 1)
    live_rows = (places < lengths[:, None]).astype(jnp.float32).reshape(row_count, 1)
    attn_full = (
        lax.all_gather(w_query, AXES, axis=0, tiled=True),
        lax.all_gather(w_key, AXES, axis=0, tiled=True),
        lax.all_gather(w_value, AXES, axis=0, tiled=True),
        lax.all_gather(w_gate, AXES, axis=0, tiled=True),
        lax.all_gather(w_out, AXES, axis=0, tiled=True),
        lax.all_gather(out_gain, AXES, axis=0, tiled=True),
    )
    ffn_full = (
        lax.all_gather(w_first, AXES, axis=0, tiled=True),
        lax.all_gather(w_second, AXES, axis=0, tiled=True),
        lax.all_gather(w_down, AXES, axis=0, tiled=True),
    )
    query_full, key_full, value_full, gate_full, out_full, gain_full = attn_full
    first_full, second_full, down_full = ffn_full
    inputs = tokens.reshape(row_count, feature_width).astype(jnp.float32)
    normed_in, inv_in = normalize(inputs)
    first_in = normed_in.astype(jnp.bfloat16)
    query_rows = project(first_in, query_full).astype(jnp.bfloat16)
    key_rows = project(first_in, key_full).astype(jnp.bfloat16)
    value_rows = project(first_in, value_full).astype(jnp.bfloat16)
    gate_pre = project(first_in, gate_full)
    head_mix, logsum = attend(query_rows, key_rows, value_rows)
    normed_mix, inv_mix = normalize(head_mix)
    gain_rows = gain_full.astype(jnp.float32)
    gate_act = jax.nn.silu(gate_pre)
    scaled_mix = normed_mix * gain_rows
    branch_in = (scaled_mix * gate_act).astype(jnp.bfloat16)
    middle = inputs + live_rows * project(branch_in, out_full)
    normed_mid, inv_mid = normalize(middle)
    second_in = normed_mid.astype(jnp.bfloat16)
    first_proj = project(second_in, first_full)
    second_proj = project(second_in, second_full)
    hidden = (first_proj * second_proj).astype(jnp.bfloat16)
    final_rows = middle + live_rows * project(hidden, down_full)
    layer_out = final_rows.astype(jnp.bfloat16).reshape(tokens.shape)
    first_back, second_back, down_back = (
        lax.all_gather(w_first, AXES, axis=0, tiled=True),
        lax.all_gather(w_second, AXES, axis=0, tiled=True),
        lax.all_gather(w_down, AXES, axis=0, tiled=True),
    )
    query_back, key_back, value_back, gate_back, out_back, gain_back = (
        lax.all_gather(w_query, AXES, axis=0, tiled=True),
        lax.all_gather(w_key, AXES, axis=0, tiled=True),
        lax.all_gather(w_value, AXES, axis=0, tiled=True),
        lax.all_gather(w_gate, AXES, axis=0, tiled=True),
        lax.all_gather(w_out, AXES, axis=0, tiled=True),
        lax.all_gather(out_gain, AXES, axis=0, tiled=True),
    )
    gain_used = gain_back.astype(jnp.float32)
    grad_final = cotangent.reshape(row_count, feature_width).astype(jnp.float32)
    grad_branch = (live_rows * grad_final).astype(jnp.bfloat16)
    grad_hidden = project_back(grad_branch, down_back)
    grad_first_proj = (grad_hidden * second_proj).astype(jnp.bfloat16)
    grad_second_proj = (grad_hidden * first_proj).astype(jnp.bfloat16)
    grad_normed_mid = project_back(grad_first_proj, first_back) + project_back(
        grad_second_proj, second_back
    )
    grad_middle = grad_final + norm_back(normed_mid, inv_mid, grad_normed_mid)
    grad_attn_out = (live_rows * grad_middle).astype(jnp.bfloat16)
    grad_branch_in = project_back(grad_attn_out, out_back)
    gain_terms = grad_branch_in * gate_act * normed_mix
    sigmoid_gate = jax.nn.sigmoid(gate_pre)
    grad_gate_pre = (
        grad_branch_in * scaled_mix * sigmoid_gate * (1.0 + gate_pre * (1.0 - sigmoid_gate))
    ).astype(jnp.bfloat16)
    grad_scaled = grad_branch_in * gate_act * gain_used
    grad_mix = norm_back(normed_mix, inv_mix, grad_scaled).astype(jnp.bfloat16)
    grad_queries, grad_keys, grad_values = attend_back(
        query_rows, key_rows, value_rows, logsum, grad_mix
    )
    grad_normed_in = (
        project_back(grad_queries, query_back)
        + project_back(grad_keys, key_back)
        + project_back(grad_values, value_back)
        + project_back(grad_gate_pre, gate_back)
    )
    grad_inputs = grad_middle + norm_back(normed_in, inv_in, grad_normed_in)
    input_grad = grad_inputs.astype(jnp.bfloat16).reshape(tokens.shape)
    ffn_shards = ffn_sums(second_in, hidden, grad_first_proj, grad_second_proj, grad_branch)
    four_grads = jnp.concatenate([grad_queries, grad_keys, grad_values, grad_gate_pre], axis=1)
    from_input = weight_grad(first_in, four_grads)
    from_branch = weight_grad(branch_in, grad_attn_out)
    gain_part = jnp.sum(gain_terms, axis=0)[:, None]
    attn_shard = lax.psum_scatter(
        jnp.concatenate([from_input, from_branch, gain_part], axis=1),
        AXES,
        scatter_dimension=0,
        tiled=True,
    )
    shard_query = attn_shard[:, 0:feature_width]
    shard_key = attn_shard[:, feature_width : 2 * feature_width]
    shard_value = attn_shard[:, 2 * feature_width : 3 * feature_width]
    shard_gate = attn_shard[:, 3 * feature_width : 4 * feature_width]
    shard_out = attn_shard[:, 4 * feature_width : 5 * feature_width]
    shard_gain = attn_shard[:, 5 * feature_width]
    shard_first, shard_second, shard_down = ffn_shards
    return (
        layer_out,
        input_grad,
        shard_query,
        shard_key,
        shard_value,
        shard_gate,
        shard_out,
        shard_gain,
        shard_first,
        shard_second,
        shard_down,
    )


MESH = pl.DeviceIdType.MESH
f32 = jnp.float32
bf16 = jnp.bfloat16
QUERY, KEY, VALUE, GATE, GAIN, OUT, FIRST, SECOND, DOWN = range(9)
DOWN_PARTIAL = "down_partial"


def bind(trees, refs):
    fields = {}
    for tree in trees:
        leaves, form = jax.tree.flatten(tree)
        fields |= jax.tree.unflatten(form, refs[: len(leaves)])
        refs = refs[len(leaves) :]
    return SimpleNamespace(**fields)


class Place:
    def __init__(self):
        dp, fs = lax.axis_index(AXES[0]), lax.axis_index(AXES[1])
        z, c = lax.div(fs, 2), lax.rem(fs, 2)
        self.dp, self.fs, self.z, self.c = dp, fs, z, c
        self.nx = dp + 1 - 2 * lax.rem(dp, 2)
        self.ny = lax.rem(dp + 2, 4)
        self.dg = lax.rem(self.nx + 2, 4)
        self.zp = [lax.rem(z + k, 4) for k in (1, 2, 3)]
        self.sib = (dp, z * 2 + 1 - c)
        self.zdev = [(dp, zz * 2 + c) for zz in self.zp]
        self.xdev, self.ydev = (self.nx, fs), (self.ny, fs)
        self.peers = [self.sib, self.xdev, self.ydev] + self.zdev

    def barrier(self):
        bar = pltpu.get_barrier_semaphore()
        for d in self.peers:
            pl.semaphore_signal(bar, inc=1, device_id=d, device_id_type=MESH)
        pl.semaphore_wait(bar, 6)


class Gather:
    def __init__(self, here, items, shards, outs, ssem, rsem, lsem):
        self.h, self.items, self.shards, self.outs = here, items, shards, outs
        self.ssem, self.rsem, self.lsem = ssem, rsem, lsem
        self.sends = []

    def rc(self, i, k, src, dst, dev):
        return pltpu.make_async_remote_copy(
            src_ref=src, dst_ref=dst, send_sem=self.ssem.at[i, k], recv_sem=self.rsem.at[i, k],
            device_id=dev, device_id_type=MESH,
        )

    def go(self, m):
        m.start()
        self.sends.append(m)

    def shard(self, i):
        m, c0, w = self.items[i]
        return self.shards[m].at[:, pl.ds(c0, w)]

    def block(self, i, yx, z):
        m, c0, w = self.items[i]
        return self.outs[m].at[yx, z, self.h.c, :, pl.ds(c0, w)]

    def own(self, i):
        return pltpu.make_async_copy(self.shard(i), self.block(i, self.h.dp, self.h.z), self.lsem.at[i])

    def zmsg(self, i, k):
        return self.rc(i, k, self.shard(i), self.block(i, self.h.dp, self.h.z), self.h.zdev[k])

    def col(self, i, k, yx, dev):
        r = self.block(i, yx, slice(None))
        return self.rc(i, k, r, r, dev)

    def half(self, i, k, yx, lo, dev):
        r = self.block(i, yx, slice(lo, lo + 2))
        return self.rc(i, k, r, r, dev)

    def step0(self, i):
        self.own(i).start()
        for k in range(3):
            self.go(self.zmsg(i, k))

    def step1(self, i):
        h = self.h
        self.own(i).wait()
        for k in range(3):
            self.zmsg(i, k).wait_recv()
        self.go(self.col(i, 3, h.dp, h.xdev))
        self.go(self.col(i, 4, h.dp, h.ydev))
        self.go(self.col(i, 7, h.dp, h.sib))

    def step2(self, i):
        h = self.h
        self.col(i, 3, h.dp, h.xdev).wait_recv()
        self.go(self.half(i, 6, h.nx, 2, h.ydev))
        self.go(self.col(i, 8, h.nx, h.sib))
        self.col(i, 4, h.dp, h.ydev).wait_recv()
        self.go(self.half(i, 5, h.ny, 0, h.xdev))
        self.go(self.col(i, 9, h.ny, h.sib))

    def step3(self, i):
        h = self.h
        self.half(i, 5, h.ny, 0, h.xdev).wait_recv()
        self.half(i, 6, h.nx, 2, h.ydev).wait_recv()
        self.go(self.col(i, 10, h.dg, h.sib))

    def step4(self, i):
        h = self.h
        for k in (7, 8, 9, 10):
            self.col(i, k, h.dp, h.sib).wait_recv()

    def finish(self):
        for m in self.sends:
            m.wait_send()


def column_parts(width, part):
    return [(c0, min(part, width - c0)) for c0 in range(0, width, part)]


def dot_nn(a, b):
    return jnp.dot(a, b, preferred_element_type=f32)


def dot_nt(a, b):
    return lax.dot_general(a, b, (((1,), (1,)), ((), ())), preferred_element_type=f32)


def dot_tn(a, b):
    return lax.dot_general(a, b, (((0,), (0,)), ((), ())), preferred_element_type=f32)


def tiles(count, body):
    def step(i, carry):
        body(i)
        return carry

    lax.fori_loop(0, count, step, 0)


def rows_of(i, size):
    return pl.ds(pl.multiple_of(i * size, size), size)


def rms_inv(values):
    return lax.rsqrt(jnp.mean(values * values, axis=-1, keepdims=True) + epsilon)


QUAD = 4 * HEAD_DIM


def quad_mask():
    shape = (QUAD, QUAD)
    row = lax.div(lax.broadcasted_iota(jnp.int32, shape, 0), HEAD_DIM)
    return row == lax.div(lax.broadcasted_iota(jnp.int32, shape, 1), HEAD_DIM)


def spread_heads(rows, mask):
    tall = jnp.concatenate([rows] * 4, axis=0)
    return jnp.where(mask, tall, jnp.zeros_like(tall))


def per_head(values, reduce, fill):
    halves = []
    for k in range(2):
        part = values[:, 128 * k : 128 * (k + 1)]
        low = lax.broadcasted_iota(jnp.int32, part.shape, 1) < HEAD_DIM
        first = reduce(jnp.where(low, part, fill), axis=-1, keepdims=True)
        second = reduce(jnp.where(low, fill, part), axis=-1, keepdims=True)
        halves.append(jnp.where(low, first, second))
    return jnp.concatenate(halves, axis=1)


def attend_blocks(b, q, k, v, probs, mix):
    mask = quad_mask()
    place = lax.broadcasted_iota(jnp.int32, (BLOCK, QUAD), 0)
    causal = place >= lax.rem(lax.broadcasted_iota(jnp.int32, (BLOCK, QUAD), 1), HEAD_DIM)
    at = [
        (rows_of(2 * b + n, BLOCK), slice(QUAD * g, QUAD * (g + 1))) for n in range(2) for g in range(HEADS // 4)
    ]
    scores = [
        jnp.where(causal, dot_nt(q[i], spread_heads(k[i], mask)) * HEAD_DIM ** (-0.5), masked_score) for i in at
    ]
    tops = [per_head(s, jnp.max, masked_score) for s in scores]
    terms = [jnp.exp(s - m) for s, m in zip(scores, tops)]
    totals = [per_head(t, jnp.sum, 0.0) for t in terms]
    lows = [(t / n).astype(bf16) for t, n in zip(terms, totals)]
    mixes = [dot_nn(p, spread_heads(v[i], mask)) for i, p in zip(at, lows)]
    for i, p, m in zip(at, lows, mixes):
        probs[i] = p
        mix[i] = m


def attend_blocks_back(b, q, k, v, probs, grad_mix, dq, dk, dv):
    mask = quad_mask()
    scale = HEAD_DIM ** (-0.5)
    low = lax.broadcasted_iota(jnp.int32, (BLOCK, 128), 1) < HEAD_DIM

    def own_head(wide):
        return jnp.concatenate(
            [
                jnp.where(low, wide[0:64, 0:128], wide[64:128, 0:128]),
                jnp.where(low, wide[128:192, 128:256], wide[192:256, 128:256]),
            ],
            axis=1,
        )

    at = [
        (rows_of(2 * b + n, BLOCK), slice(QUAD * g, QUAD * (g + 1))) for n in range(2) for g in range(HEADS // 4)
    ]
    dps = [dot_nt(grad_mix[i], spread_heads(v[i], mask)) for i in at]
    dvs = [own_head(dot_tn(probs[i], grad_mix[i])) for i in at]
    ps = [probs[i].astype(f32) for i in at]
    means = [per_head(dp * p, jnp.sum, 0.0) for dp, p in zip(dps, ps)]
    dss = [(p * (dp - m)).astype(bf16) for p, dp, m in zip(ps, dps, means)]
    dqs = [dot_nn(ds, spread_heads(k[i], mask)) * scale for i, ds in zip(at, dss)]
    dks = [own_head(dot_tn(ds, q[i])) * scale for i, ds in zip(at, dss)]
    for i, a, c, d in zip(at, dqs, dks, dvs):
        dq[i] = a.astype(bf16)
        dk[i] = c.astype(bf16)
        dv[i] = d.astype(bf16)


class Saves:
    def __init__(self, sems):
        self.sems, self.count, self.open = sems, 0, {}

    def start(self, name, src, dst):
        m = pltpu.make_async_copy(src, dst, self.sems.at[self.count])
        self.count += 1
        m.start()
        self.open[name] = m

    def wait(self, *names):
        for name in names:
            if name in self.open:
                self.open.pop(name).wait()

    def finish(self):
        self.wait(*list(self.open))


FORWARD_COPIES = 64
X, DF, A1, Q, K, V, PB, GP, H, O, Y, A2, GAINS, SLABS = range(10, 24)


def forward_kernel(items, trees, *refs):
    ref = bind(trees, refs)
    rows, width = ref.tokens.shape
    ff = ref.shards[FIRST].shape[1]
    parts = column_parts(ff, width)
    x, a1, q, k, v, pb, h, a2, e0, e1, e2, df = [ref.page.at[i] for i in range(12)]
    weight = [ref.weight.at[i] for i in range(4)]
    hidden, first, second = (e0, e1, e2), (q, k, v), (pb, h, x)
    wide = ref.wide
    gate_rows, mix_rows, mid_rows = [pl.ds(rows * i, rows) for i in range(3)]
    gp, o, y = wide.at[gate_rows], wide.at[mix_rows], wide.at[mid_rows]
    here = Place()
    here.barrier()
    ag = Gather(here, items, ref.shards, ref.full, ref.ssem, ref.rsem, ref.lsem)
    cp = Saves(ref.csem)
    size = 128
    live_len = ref.lengths[0]

    def live(i, n):
        return lax.broadcasted_iota(jnp.int32, (n, 1), 0) + i * n < live_len

    def spread(values):
        return jnp.broadcast_to(values, (values.shape[0], 128))

    cp.start(X, ref.tokens, x)
    cp.start(DF, ref.cotangent, df)

    def norm_in():
        cp.wait(X)

        def tile(i):
            r = rows_of(i, size)
            t = x[r, :].astype(f32)
            inv = rms_inv(t)
            a1[r, :] = (t * inv).astype(bf16)
            ref.inv_in[r, :] = spread(inv)

        tiles(rows // size, tile)
        cp.start(A1, a1, ref.save_a1)

    def mask_df():
        cp.wait(DF)

        def tile(i):
            r = rows_of(i, size)
            df[r, :] = jnp.where(live(i, size), df[r, :], jnp.zeros((), bf16))

        tiles(rows // size, tile)

    def load(slot, m, c0=0, w=None):
        src = ref.full[m]
        w = src.shape[-1] if w is None else w
        cp.start(slot, src.at[:, :, :, :, pl.ds(c0, w)], weight[slot].at[:, :, :, :, pl.ds(0, w)])

    def matrix(slot, w=None):
        w = width if w is None else w
        return weight[slot][:, :, :, :, 0:w].reshape(width, w)

    def projected(slot, dst, name=None, kept=None):
        def run():
            cp.wait(slot)

            def tile(i):
                r = rows_of(i, rows // 2)
                dst[r, :] = dot_nn(a1[r, :], matrix(slot)).astype(dst.dtype)

            tiles(2, tile)
            if kept is not None:
                cp.start(name, dst, kept)

        return run

    def gate_low():
        def tile(i):
            r = rows_of(i, size)
            e0[r, :] = gp[r, :].astype(bf16)

        tiles(rows // size, tile)
        cp.start(GP, e0, ref.save_gp)

    def attention(n, count):
        def run():
            tiles(count, lambda b: attend_blocks(b + n * count, q, k, v, pb, o))

        return run

    def mixed():
        cp.start(PB, pb, ref.save_pb)
        cp.wait(GAINS)
        gains = ref.gain
        gain = jnp.concatenate(
            [
                sum(gains[g, j, cc, 0:1, :].astype(f32) for j in (2 * half, 2 * half + 1) for cc in range(2))
                for g in range(4)
                for half in range(2)
            ],
            axis=1,
        )

        def tile(i):
            r = rows_of(i, size)
            t, z = o[r, :], gp[r, :]
            inv = rms_inv(t)
            h[r, :] = (t * inv * gain * (z * jax.nn.sigmoid(z))).astype(bf16)
            e1[r, :] = t.astype(bf16)
            ref.inv_mix[r, :] = spread(inv)

        tiles(rows // size, tile)
        cp.start(H, h, ref.save_h)
        cp.start(O, e1, ref.save_o)

    def middle(slot):
        def run():
            cp.wait(slot)

            def tile(i):
                r = rows_of(i, rows // 2)
                y[r, :] = dot_nn(h[r, :], matrix(slot))

            tiles(2, tile)

            def norm(i):
                r = rows_of(i, size)
                t = x[r, :].astype(f32) + jnp.where(live(i, size), y[r, :], 0.0)
                inv = rms_inv(t)
                y[r, :] = t
                a2[r, :] = (t * inv).astype(bf16)
                ref.inv_mid[r, :] = spread(inv)

            tiles(rows // size, norm)
            cp.start(Y, y, ref.save_y)
            cp.start(A2, a2, ref.save_a2)

        return run

    def gated(j, s1, s2, half):
        c0, w = parts[j]
        saved = ((first[j], ref.save_g1), (second[j], ref.save_g2), (hidden[j], ref.save_e))

        def run():
            if half == 0:
                cp.wait(s1, s2, Q, K, V, PB, H, GP, O)
            r = pl.ds(half * (rows // 2), rows // 2)
            up = dot_nn(a2[r, :], matrix(s1, w))
            first[j][r, 0:w] = up.astype(bf16)
            other = dot_nn(a2[r, :], matrix(s2, w))
            second[j][r, 0:w] = other.astype(bf16)
            hidden[j][r, 0:w] = (up * other).astype(bf16)
            if half == 1:
                for n, (page, kept) in enumerate(saved):
                    cp.start((j, n), page.at[:, 0:w], kept.at[:, pl.ds(c0, w)])

        return run

    def down_grad(j, c0, w):
        def run():
            if j == 2:
                cp.wait(Y)
            wide[pl.ds(parts[j][0] + c0, w), :] = dot_tn(hidden[j][:, c0 : c0 + w], df[...])

        return run

    def down_slabs():
        slabs = ref.slabs
        n = slabs.shape[1]

        def tile(d):
            slabs[d] = wide[pl.ds(pl.multiple_of(d * n, 8), n), :].astype(bf16)

        tiles(slabs.shape[0], tile)
        cp.start(SLABS, slabs, ref.down_partial)

    work = [((), norm_in), ((), mask_df)]
    work += [((0,), projected(0, q, Q, ref.save_q)), ((1,), projected(1, k, K, ref.save_k)), ((2,), projected(2, v, V, ref.save_v))]
    work += [((), attention(n, 2)) for n in range(rows // BLOCK // 4)]
    work += [((3,), projected(3, gp)), ((), gate_low), ((4,), mixed), ((5,), middle(0))]
    slots = ((1, 2), (3, 0), (1, 2))
    for j, (s1, s2) in enumerate(slots):
        work += [((6 + 2 * j, 7 + 2 * j), gated(j, s1, s2, half)) for half in range(2)]
    for j, (c0, w) in enumerate(parts):
        step = 512 if w % 512 == 0 else w // 2
        work += [((), down_grad(j, n * step, step)) for n in range(w // step)]
    work += [((), down_slabs)]
    loads = {0: (0, QUERY), 1: (1, KEY), 2: (2, VALUE), 3: (3, GATE), 5: (0, OUT)}
    for j, (s1, s2) in enumerate(slots):
        loads[6 + 2 * j] = (s1, FIRST) + parts[j]
        loads[7 + 2 * j] = (s2, SECOND) + parts[j]
    readers = {i: sum(i in needs for needs, _ in work) for i in range(len(items))}
    ready, waiting, held = set(), [], {}

    def try_loads():
        while waiting:
            i = waiting[0]
            slot = loads[i][0]
            if slot in held and readers[held[slot]]:
                return
            held[slot] = i
            load(*loads[i])
            ready.add(i)
            waiting.pop(0)

    def completed(i):
        if i in loads:
            waiting.append(i)
            try_loads()
        elif i == 4:
            cp.start(GAINS, ref.full[GAIN], ref.gain)
            ready.add(i)

    def run_one():
        if work and all(i in ready for i in work[0][0]):
            needs, f = work.pop(0)
            f()
            for i in needs:
                readers[i] -= 1
            try_loads()

    n = len(items)
    stages = ((0, ag.step0), (1, ag.step1), (2, ag.step2), (3, ag.step3), (4, ag.step4))
    for t in range(n + 4):
        for off, f in stages:
            if 0 <= t - off < n:
                f(t - off)
                if off == 4:
                    completed(t - off)
            if t > 0:
                run_one()
    while work:
        run_one()
    ag.finish()
    cp.start(X, ref.inv_in, ref.save_inv_in)
    cp.start(PB, ref.inv_mix, ref.save_inv_mix)
    cp.start(Y, ref.inv_mid, ref.save_inv_mid)
    cp.finish()


def forward(tokens, lengths, cotangent, shards):
    rows, width = tokens.shape
    ff = shards[FIRST].shape[1]
    parts = column_parts(ff, width)
    items = [(m, 0, shards[m].shape[1]) for m in (QUERY, KEY, VALUE, GATE, GAIN, OUT)]
    items += [(m, c0, w) for c0, w in parts for m in (FIRST, SECOND)]
    items += [(DOWN, c0, w) for c0, w in column_parts(width, 256)]
    n = len(items)
    page, row = jax.ShapeDtypeStruct((rows, width), bf16), jax.ShapeDtypeStruct((rows, 128), f32)
    wide = jax.ShapeDtypeStruct((rows, ff), bf16)
    saves = dict(
        save_a1=page, save_q=page, save_k=page, save_v=page, save_pb=page, save_gp=page, save_o=page, save_h=page,
        save_a2=page, save_g1=wide, save_g2=wide, save_e=wide, save_y=jax.ShapeDtypeStruct((rows, width), f32),
        save_inv_in=row, save_inv_mix=row, save_inv_mid=row,
    )
    slab = (32,) + shards[DOWN].shape
    saves[DOWN_PARTIAL] = jax.ShapeDtypeStruct(slab, bf16)
    outs = dict(full=[jax.ShapeDtypeStruct((4, 4, 2) + s.shape, bf16) for s in shards])
    inv = pltpu.VMEM((rows, 128), f32)
    scratch = dict(
        page=pltpu.VMEM((12, rows, width), bf16),
        weight=pltpu.VMEM((4, 4, 4, 2, shards[QUERY].shape[0], width), bf16),
        wide=pltpu.VMEM((3 * rows, width), f32),
        slabs=pltpu.VMEM(slab, bf16),
        gain=pltpu.VMEM((4, 4, 2) + shards[GAIN].shape, bf16),
        inv_in=inv, inv_mix=inv, inv_mid=inv,
        ssem=pltpu.SemaphoreType.DMA((n, 11)),
        rsem=pltpu.SemaphoreType.DMA((n, 11)),
        lsem=pltpu.SemaphoreType.DMA((n,)),
        csem=pltpu.SemaphoreType.DMA((FORWARD_COPIES,)),
    )
    ins = dict(cotangent=cotangent, shards=list(shards), tokens=tokens)
    hbm = pl.BlockSpec(memory_space=pl.ANY)
    leaves = jax.tree.leaves
    got = pl.pallas_call(
        functools.partial(forward_kernel, items, (dict(lengths=0), ins, outs, saves, scratch)),
        out_shape=leaves(outs) + leaves(saves),
        in_specs=[pl.BlockSpec(memory_space=pltpu.SMEM)] + [hbm] * len(leaves(ins)),
        out_specs=[hbm] * len(leaves(outs) + leaves(saves)),
        scratch_shapes=leaves(scratch),
        compiler_params=pltpu.CompilerParams(
            collective_id=0, has_side_effects=True, vmem_limit_bytes=62 * 2**20
        ),
    )(lengths, *leaves(ins))
    full = got[: len(shards)]
    return full, jax.tree.unflatten(jax.tree.structure(saves), got[len(shards) :])


class Timeline:
    def __init__(self, steps, work, window, given, after):
        self.steps, self.work, self.window, self.after = steps, list(work), window, after
        self.made = set(given)
        self.at = [0] * len(steps)
        self.when = [0.0] * len(steps)
        self.free = {}
        self.now = 0.0
        self.done = set()
        self.log = []

    def next_steps(self):
        started = 0
        for i, at in enumerate(self.at):
            if at == 0:
                if i in self.made and started < self.window and self.after[i] <= self.done:
                    yield i
                return
            if at < len(self.steps[i]):
                started += at < 2
                yield i

    def step(self, i):
        run, link, link_us, core_us = self.steps[i][self.at[i]]
        self.now = max(self.now, self.when[i])
        run(i)
        self.now += core_us
        begin = max(self.now, self.free.get(link, 0.0))
        if link:
            self.free[link] = begin + link_us
        self.when[i] = begin + link_us + (1.5 if link else 0.0)
        self.at[i] += 1
        if self.at[i] == len(self.steps[i]):
            self.done.add(i)
        self.log.append((round(self.now, 1), "step", i, self.at[i] - 1))

    def run(self):
        while True:
            steps = list(self.next_steps())
            ready = [i for i in steps if self.when[i] <= self.now]
            if ready:
                self.step(ready[0])
            elif self.work and all(n in self.done for n in self.work[0][2]):
                run, core_us, _, gives = self.work.pop(0)
                run()
                self.now += core_us
                if gives is not None:
                    self.made.add(gives)
                    self.when[gives] = self.now
                self.log.append((round(self.now, 1), "work", getattr(run, "__name__", "")))
            elif steps:
                self.step(min(steps, key=lambda i: self.when[i]))
            else:
                return


class Scatter:
    def __init__(self, here, items, bufs, ssem, rsem, lsem, free):
        self.h, self.items, self.bufs = here, items, bufs
        self.ssem, self.rsem, self.lsem, self.free = ssem, rsem, lsem, free
        self.sends = {}

    def rc(self, i, k, src, dst, dev):
        return pltpu.make_async_remote_copy(
            src_ref=src, dst_ref=dst, send_sem=self.ssem.at[i, k], recv_sem=self.rsem.at[i, k],
            device_id=dev, device_id_type=MESH,
        )

    def go(self, i, *moves):
        for m in moves:
            m.start()
            self.sends.setdefault(i, []).append(m)

    def views(self, i):
        it = self.items[i]
        return it, self.bufs[it.cls], it.slot, it.w

    def mine(self, i, yx, z):
        it, b, s, w = self.views(i)
        if b.p is not None:
            return b.p.at[s, yx, z, :, 0:w]
        return b.g.at[s, yx, z, self.h.c, :, 0:w]

    def m_sib(self, i):
        it, b, s, w = self.views(i)
        if b.p is not None:
            src = it.src.at[:, :, 1 - self.h.c, :, pl.ds(it.c0, w)]
        else:
            src = b.g.at[s, :, :, 1 - self.h.c, :, 0:w]
        return self.rc(i, 0, src, b.r1.at[s, :, :, :, 0:w], self.h.sib)

    def m_load(self, i):
        it, b, s, w = self.views(i)
        src = it.src.at[:, :, self.h.c, :, pl.ds(it.c0, w)]
        return pltpu.make_async_copy(src, b.p.at[s, :, :, :, 0:w], self.lsem.at[i])

    def m_dx(self, i):
        it, b, s, w = self.views(i)
        return self.rc(i, 1, self.mine(i, self.h.dg, slice(0, 2)), b.rd.at[s, 0, :, :, 0:w], self.h.xdev)

    def m_dy(self, i):
        it, b, s, w = self.views(i)
        return self.rc(i, 2, self.mine(i, self.h.dg, slice(2, 4)), b.rd.at[s, 1, :, :, 0:w], self.h.ydev)

    def m_x(self, i):
        it, b, s, w = self.views(i)
        return self.rc(i, 3, self.mine(i, self.h.nx, slice(None)), b.rxy.at[s, 0, :, :, 0:w], self.h.xdev)

    def m_y(self, i):
        it, b, s, w = self.views(i)
        return self.rc(i, 4, self.mine(i, self.h.ny, slice(None)), b.rxy.at[s, 1, :, :, 0:w], self.h.ydev)

    def m_z(self, i, k):
        it, b, s, w = self.views(i)
        return self.rc(i, 5 + k, self.mine(i, self.h.dp, self.h.zp[k]), b.rz.at[s, k, :, 0:w], self.h.zdev[k])

    def add(self, i, yx, z, *terms):
        p = self.mine(i, yx, z)
        total = p[...].astype(f32)
        for t in terms:
            total = total + t[...].astype(f32)
        p[...] = total.astype(p.dtype)

    def release(self, i):
        for m in self.sends.pop(i):
            m.wait_send()

    def step0(self, i):
        it, b, s, w = self.views(i)
        if it.before is not None:
            if b.p is not None:
                self.release(it.before)
            for k in range(6):
                pl.semaphore_wait(self.free.at[it.cls, k], 1)
        if b.p is not None:
            self.m_load(i).start()
        self.go(i, self.m_sib(i))

    def step1(self, i):
        it, b, s, w = self.views(i)
        r, dg = b.r1, self.h.dg
        if b.p is not None:
            self.m_load(i).wait()
        self.m_sib(i).wait_recv()
        tiles(4, lambda j: self.add(i, dg, j, r.at[s, dg, j, :, 0:w]))
        self.go(i, self.m_dx(i), self.m_dy(i))

        def near(j):
            a, q = lax.rem(dg + 1 + lax.div(j, 4), 4), lax.rem(j, 4)
            self.add(i, a, q, r.at[s, a, q, :, 0:w])

        tiles(12, near)

    def step2(self, i):
        it, b, s, w = self.views(i)
        rd, nx, ny = b.rd, self.h.nx, self.h.ny
        self.m_dx(i).wait_recv()
        tiles(2, lambda j: self.add(i, ny, j, rd.at[s, 0, j, :, 0:w]))
        self.go(i, self.m_y(i))
        self.m_dy(i).wait_recv()
        tiles(2, lambda j: self.add(i, nx, 2 + j, rd.at[s, 1, j, :, 0:w]))
        self.go(i, self.m_x(i))

    def step3(self, i):
        it, b, s, w = self.views(i)
        rxy, dp = b.rxy, self.h.dp
        self.m_x(i).wait_recv()
        self.m_y(i).wait_recv()
        tiles(4, lambda j: self.add(i, dp, j, rxy.at[s, 0, j, :, 0:w], rxy.at[s, 1, j, :, 0:w]))
        self.go(i, *[self.m_z(i, k) for k in range(3)])

    def step4(self, i):
        it, b, s, w = self.views(i)
        rz = b.rz
        for k in range(3):
            self.m_z(i, k).wait_recv()
        total = self.mine(i, self.h.dp, self.h.z)[...].astype(f32)
        for k in range(3):
            total = total + rz[s, k, :, 0:w].astype(f32)
        it.out[:, pl.ds(it.c0, w)] = total
        if it.reused:
            for k, d in enumerate(self.h.peers):
                pl.semaphore_signal(
                    self.free.at[it.cls, k if k < 3 else 8 - k], inc=1, device_id=d, device_id_type=MESH
                )

    def finish(self):
        for i in list(self.sends):
            self.release(i)


def scatter_plan(specs, ring):
    items, by_class = [], {}
    for m, c0, w, cls in specs:
        mine = by_class.setdefault(cls, [])
        it = SimpleNamespace(m=m, c0=c0, w=w, cls=cls, slot=len(mine) % ring[cls], before=None, reused=False)
        if len(mine) >= ring[cls]:
            it.before = mine[-ring[cls]]
            items[it.before].reused = True
        mine.append(len(items))
        items.append(it)
    return items


def scatter_scratch(held, slots, r, w, dt):
    return dict(
        g=pltpu.VMEM((slots, 4, 4, 2, r, w) if held else (8, 128), dt),
        p=pltpu.VMEM((8, 128) if held else (slots, 4, 4, r, w), dt),
        r1=pltpu.VMEM((slots, 4, 4, r, w), dt),
        rd=pltpu.VMEM((slots, 2, 2, r, w), dt),
        rxy=pltpu.VMEM((slots, 2, 4, r, w), dt),
        rz=pltpu.VMEM((slots, 3, r, w), dt),
    )


BACKWARD_COPIES = 64


def backward_kernel(items, trees, *refs):
    ref = bind(trees, refs)
    rows, width = ref.cotangent.shape
    ff = ref.full[FIRST].shape[1]
    parts = column_parts(ff, width)
    page = [ref.page.at[i] for i in range(12)]
    acc, other = ref.wide.at[0], ref.wide.at[1]
    here = Place()
    here.barrier()
    bufs = [SimpleNamespace(**b) for b in ref.rings]
    bufs[DOWN_RING].g = bufs[IN_RING].p = bufs[GAIN_RING].p = None
    items = [SimpleNamespace(**vars(it), out=ref.grads[it.m], src=ref.down_partial) for it in items]
    rs = Scatter(here, items, bufs, ref.ssem, ref.rsem, ref.lsem, ref.free)
    cp = Saves(ref.csem)
    size, half_rows = 128, rows // 2
    live_len = ref.lengths[0]
    index = {(it.m, it.c0): i for i, it in enumerate(items)}

    def live(first, n):
        return lax.broadcasted_iota(jnp.int32, (n, 1), 0) + first < live_len

    def load(n, src, c0=None, w=None, by_row=False):
        dst = page[n]
        if c0 is not None:
            if by_row:
                src, dst = src.at[pl.ds(c0, w)], dst.at[pl.ds(0, w)]
            else:
                src, dst = src.at[:, pl.ds(c0, w)], dst.at[:, pl.ds(0, w)]
        cp.start(n, src, dst)

    def halves(f):
        return [functools.partial(f, pl.ds(half_rows * n, half_rows)) for n in range(2)]

    work = []

    def piece(cost, f, needs=(), gives=None):
        work.append((f, cost, needs, gives))

    def grad_item(m, c0, w, left, right):
        i = index[m, c0]
        it = items[i]
        g = bufs[it.cls].g

        def half(n):
            def run():
                if n == 0:
                    if it.before is not None:
                        rs.release(it.before)
                    left_wait = [k for k in range(12) if page[k] is left or page[k] is right]
                    cp.wait(*left_wait)
                cols = slice(n * (width // 2), (n + 1) * (width // 2))
                got = dot_tn(left[:, cols], right[:, 0:w]).astype(bf16)
                g[it.slot, 2 * n : 2 * n + 2, :, :, :, 0:w] = got.reshape((2,) + g.shape[2:5] + (w,))

            return run

        needs = () if it.before is None else (it.before,)
        piece(1.25, half(0), needs)
        piece(1.25, half(1), (), i)

    load(0, ref.cotangent)
    load(2, ref.full[DOWN], *parts[0], by_row=True)
    load(4, ref.save_g2, *parts[0])
    load(3, ref.save_g1, *parts[0])
    load(1, ref.save_a2)
    load(5, ref.full[FIRST], *parts[0])
    load(6, ref.full[SECOND], *parts[0])
    load(9, ref.save_h)
    load(10, ref.full[OUT])
    load(11, ref.save_gp)
    cp.start(12, ref.save_inv_in, ref.inv_in)
    cp.start(13, ref.save_inv_mix, ref.inv_mix)
    cp.start(14, ref.save_inv_mid, ref.inv_mid)
    cp.start(15, ref.full_gain, ref.gain)

    def hidden_back(j, n):
        c0, w = parts[j]

        def run():
            cp.wait(0, 2, 3, 4)
            r = pl.ds(half_rows * n, half_rows)
            de = dot_nt(page[0][r, :], page[2][0:w, :])
            de = jnp.where(live(half_rows * n, half_rows), de, 0.0)
            page[7][r, 0:w] = (de * page[4][r, 0:w].astype(f32)).astype(bf16)
            page[8][r, 0:w] = (de * page[3][r, 0:w].astype(f32)).astype(bf16)
            if n == 1:
                if j + 1 < len(parts):
                    load(2, ref.full[DOWN], *parts[j + 1], by_row=True)
                    load(3, ref.save_g1, *parts[j + 1])
                    load(4, ref.save_g2, *parts[j + 1])
                else:
                    load(3, ref.save_o)

        return run

    def mid_back(j, n):
        c0, w = parts[j]

        def run():
            cp.wait(5, 6)
            r = pl.ds(half_rows * n, half_rows)
            part = dot_nt(page[7][r, 0:w], page[5][:, 0:w]) + dot_nt(page[8][r, 0:w], page[6][:, 0:w])
            acc[r, :] = part if j == 0 else acc[r, :] + part
            if n == 1:
                if j + 1 < len(parts):
                    load(5, ref.full[FIRST], *parts[j + 1])
                    load(6, ref.full[SECOND], *parts[j + 1])
                else:
                    load(6, ref.save_a1)
                    load(7, ref.save_q)
                    load(8, ref.save_k)

        return run

    for j, (c0, w) in enumerate(parts):
        for n in range(2):
            piece(1.7, hidden_back(j, n))
        grad_item(FIRST, c0, w, page[1], page[7])
        grad_item(SECOND, c0, w, page[1], page[8])
        for n in range(2):
            piece(2.6, mid_back(j, n))

    def middle_back():
        cp.wait(14, 1, 0)

        def tile(i):
            r = rows_of(i, size)
            up, n2 = acc[r, :], page[1][r, :].astype(f32)
            mean = jnp.mean(up * n2, axis=-1, keepdims=True)
            dy = page[0][r, :].astype(f32) + ref.inv_mid[r, 0:1] * (up - n2 * mean)
            acc[r, :] = dy
            page[2][r, :] = jnp.where(live(i * size, size), dy, 0.0).astype(bf16)

        tiles(rows // size, tile)
        load(0, ref.full[GATE])

    piece(3.0, middle_back)
    grad_item(OUT, 0, width, page[9], page[2])

    def branch_back():
        cp.wait(10)

        def tile(i):
            r = rows_of(i, half_rows)
            other[r, :] = dot_nt(page[2][r, :], page[10][...])

        tiles(2, tile)
        load(9, ref.save_v)
        load(10, ref.save_pb)

    piece(2.4, branch_back)

    def mix_back(first, count):
        def run():
            cp.wait(15, 13, 3, 11)
            gains = ref.gain
            gain = jnp.concatenate(
                [
                    sum(gains[g, j, cc, 0:1, :].astype(f32) for j in (2 * half, 2 * half + 1) for cc in range(2))
                    for g in range(4)
                    for half in range(2)
                ],
                axis=1,
            )
            terms = ref.gain_terms
            if first == 0:
                terms[...] = jnp.zeros_like(terms)

            def tile(i):
                r = rows_of(i + first, size)
                inv = ref.inv_mix[r, 0:1]
                up, z = other[r, :], page[11][r, :].astype(f32)
                normed = page[3][r, :].astype(f32) * inv
                sig = jax.nn.sigmoid(z)
                upu = up * (z * sig)
                terms[...] += (upu * normed).reshape(size // 8, 8, width).sum(axis=0)
                page[4][r, :] = (up * normed * gain * sig * (1.0 + z * (1.0 - sig))).astype(bf16)
                dm = upu * gain
                mean = jnp.mean(dm * normed, axis=-1, keepdims=True)
                page[5][r, :] = (inv * (dm - normed * mean)).astype(bf16)

            tiles(count, tile)

        return run

    for n in range(2):
        piece(3.0, mix_back(n * (rows // size // 2), rows // size // 2))

    def gain_item():
        g, terms = bufs[GAIN_RING].g, ref.gain_terms
        for yx in range(4):
            for z in range(4):
                for c in range(2):
                    at = 128 * (2 * yx + z // 2)
                    g[0, yx, z, c] = terms[:, at : at + 128]

    piece(0.3, gain_item, (), index[GAIN, 0])
    grad_item(GATE, 0, width, page[6], page[4])

    def attention_back(n, count):
        def run():
            cp.wait(7, 8, 9, 10)
            q, k, v, pb, do, dq, dk, dv = [page[m] for m in (7, 8, 9, 10, 5, 11, 3, 2)]
            tiles(count, lambda b: attend_blocks_back(b + n * count, q, k, v, pb, do, dq, dk, dv))
            if n == rows // BLOCK // 4 - 1:
                load(7, ref.full[QUERY])
                load(8, ref.full[KEY])
                load(9, ref.full[VALUE])
                load(10, ref.save_e, *parts[0])
                load(5, ref.save_e, *parts[1])
                load(1, ref.save_e, *parts[2])

        return run

    for n in range(rows // BLOCK // 4):
        piece(2.4, attention_back(n, 2))
    grad_item(QUERY, 0, width, page[6], page[11])
    grad_item(KEY, 0, width, page[6], page[3])
    grad_item(VALUE, 0, width, page[6], page[2])

    def input_part(up, w, first, then=None):
        def run():
            cp.wait(w)

            def tile(i):
                r = rows_of(i, half_rows)
                part = dot_nt(page[up][r, :], page[w][...])
                other[r, :] = part if first else other[r, :] + part

            tiles(2, tile)
            if then is not None:
                load(w, ref.full[DOWN], *parts[then], by_row=True)

        return run

    piece(2.4, input_part(4, 0, True))
    for then, (up, w) in enumerate(((11, 7), (3, 8), (2, 9))):
        piece(2.4, input_part(up, w, False, then))

    def input_back():
        cp.wait(12, 6)

        def tile(i):
            r = rows_of(i, size)
            up, n1 = other[r, :], page[6][r, :].astype(f32)
            mean = jnp.mean(up * n1, axis=-1, keepdims=True)
            page[0][r, :] = (acc[r, :] + ref.inv_in[r, 0:1] * (up - n1 * mean)).astype(bf16)

        tiles(rows // size, tile)
        cp.start(0, page[0], ref.input_grad)
        cp.start(16, ref.save_y, acc)

    piece(2.5, input_back)

    def output_part(j, e, w):
        def run():
            cp.wait(e, w)
            n = parts[j][1]

            def tile(i):
                r = rows_of(i, half_rows)
                part = dot_nn(page[e][r, 0:n], page[w][0:n, :])
                other[r, :] = part if j == 0 else other[r, :] + part

            tiles(2, tile)

        return run

    for j, (e, w) in enumerate(((10, 7), (5, 8), (1, 9))):
        piece(2.4, output_part(j, e, w))

    def output():
        cp.wait(16)

        def tile(i):
            r = rows_of(i, size)
            page[4][r, :] = (acc[r, :] + jnp.where(live(i * size, size), other[r, :], 0.0)).astype(bf16)

        tiles(rows // size, tile)
        cp.start(4, page[4], ref.layer_out)

    piece(1.5, output)

    def unit(i):
        it = items[i]
        return it.w * it.out.shape[0] / (32 * 1024)

    steps = []
    for i in range(len(items)):
        u = unit(i)
        steps.append([
            (rs.step0, -i - 1, 1.5 * u, 0.2), (rs.step1, 1, 2.8 * u, 1.0 * u + 0.2),
            (rs.step2, 1, 5.6 * u, 0.4 * u + 0.2), (rs.step3, 2, 5.6 * u, 0.4 * u + 0.2),
            (rs.step4, None, 0.0, 0.2 * u + 0.2),
        ])
    given = [i for i, it in enumerate(items) if it.cls == DOWN_RING]
    after = [set() if it.before is None else {it.before} for it in items]
    order = Timeline(steps, work, 3, given, after)
    order.run()
    rs.finish()
    cp.finish()
    if SHOW_ORDER:
        print(order.log)


SHOW_ORDER = False


DOWN_RING, IN_RING, GAIN_RING = range(3)


def backward(cotangent, lengths, full, got):
    rows, width = cotangent.shape
    flat = [w.reshape(-1, w.shape[-1]) for w in full]
    ff = flat[FIRST].shape[1]
    r_in, r_down = full[QUERY].shape[3], full[DOWN].shape[3]
    parts = column_parts(ff, width)
    specs = [(DOWN, c0, w, DOWN_RING) for c0, w in column_parts(width, 256)]
    specs += [(m, c0, w, IN_RING) for c0, w in parts for m in (FIRST, SECOND)]
    specs += [(OUT, 0, width, IN_RING), (GAIN, 0, 128, GAIN_RING)]
    specs += [(m, 0, width, IN_RING) for m in (GATE, QUERY, KEY, VALUE)]
    slots = (2, 4, 1)
    items = scatter_plan(specs, slots)
    n = len(items)
    ins = dict(cotangent=cotangent, full=flat, full_gain=full[GAIN])
    ins |= {k: a for k, a in got.items() if k != DOWN_PARTIAL}
    ins |= dict(down_partial=got[DOWN_PARTIAL].reshape(full[DOWN].shape))
    shapes = [(r_down if m == DOWN else r_in, flat[m].shape[1]) for m in range(len(full))]
    shapes[GAIN] = (8, 128)
    page = jax.ShapeDtypeStruct((rows, width), bf16)
    outs = dict(layer_out=page, input_grad=page)
    grads = dict(grads=[jax.ShapeDtypeStruct(s, f32) for s in shapes])
    inv = pltpu.VMEM((rows, 128), f32)
    scratch = dict(
        rings=[
            scatter_scratch(False, slots[DOWN_RING], r_down, 256, bf16),
            scatter_scratch(True, slots[IN_RING], r_in, width, bf16),
            scatter_scratch(True, slots[GAIN_RING], 8, 128, f32),
        ],
        page=pltpu.VMEM((12, rows, width), bf16),
        wide=pltpu.VMEM((2, rows, width), f32),
        inv_in=inv, inv_mix=inv, inv_mid=inv,
        gain=pltpu.VMEM(full[GAIN].shape, bf16),
        gain_terms=pltpu.VMEM((8, width), f32),
        ssem=pltpu.SemaphoreType.DMA((n, 8)),
        rsem=pltpu.SemaphoreType.DMA((n, 8)),
        lsem=pltpu.SemaphoreType.DMA((n,)),
        csem=pltpu.SemaphoreType.DMA((BACKWARD_COPIES,)),
        free=pltpu.SemaphoreType.REGULAR((len(slots), 6)),
    )
    hbm, vmem = pl.BlockSpec(memory_space=pl.ANY), pl.BlockSpec(memory_space=pltpu.VMEM)
    leaves = jax.tree.leaves
    out = pl.pallas_call(
        functools.partial(backward_kernel, items, (dict(lengths=0), ins, outs, grads, scratch)),
        out_shape=leaves(outs) + leaves(grads),
        in_specs=[pl.BlockSpec(memory_space=pltpu.SMEM)] + [hbm] * len(leaves(ins)),
        out_specs=[hbm] * len(leaves(outs)) + [vmem] * len(leaves(grads)),
        scratch_shapes=leaves(scratch),
        compiler_params=pltpu.CompilerParams(
            collective_id=1, has_side_effects=True, vmem_limit_bytes=63 * 2**20
        ),
    )(lengths, *leaves(ins))
    return bind((outs, grads), out)


def slice_body(
    tokens, lengths, cotangent, w_query, w_key, w_value, w_gate, w_out, out_gain, w_first, w_second, w_down,
):
    rows, width = tokens.shape[0] * tokens.shape[1], tokens.shape[2]
    me = lax.axis_index(AXES[0]) * 8 + lax.axis_index(AXES[1])
    lane = lax.broadcasted_iota(jnp.int32, (16, 128), 1)
    gain_block = jnp.where(lax.div(lane, 32) == lax.rem(me, 4), jnp.tile(out_gain, 4)[None, :], 0)
    flat_cotangent = cotangent.reshape(rows, width)
    shards = (w_query, w_key, w_value, w_gate, gain_block, w_out, w_first, w_second, w_down)
    full, got = forward(tokens.reshape(rows, width), lengths, flat_cotangent, shards)
    back = backward(flat_cotangent, lengths, full, got)
    grads = back.grads
    gain = lax.dynamic_slice(grads[GAIN].sum(axis=0), (lax.rem(me, 4) * 32,), (32,))
    return (
        back.layer_out.reshape(tokens.shape), back.input_grad.reshape(tokens.shape),
        *[grads[m] for m in (QUERY, KEY, VALUE, GATE, OUT)], gain,
        *[grads[m] for m in (FIRST, SECOND, DOWN)],
    )


def solution(mesh):
    fits = (mesh.shape[AXES[0]], mesh.shape[AXES[1]]) == (4, 8)
    return jax.shard_map(
        slice_body if fits else general_body,
        mesh=mesh,
        in_specs=(
            P(AXES, None, None),
            P(AXES),
            P(AXES, None, None),
            P(AXES, None),
            P(AXES, None),
            P(AXES, None),
            P(AXES, None),
            P(AXES, None),
            P(AXES),
            P(AXES, None),
            P(AXES, None),
            P(AXES, None),
        ),
        out_specs=(
            P(AXES, None, None),
            P(AXES, None, None),
            P(AXES, None),
            P(AXES, None),
            P(AXES, None),
            P(AXES, None),
            P(AXES, None),
            P(AXES),
            P(AXES, None),
            P(AXES, None),
            P(AXES, None),
        ),
        check_vma=False,
    )
```

```python
import functools
from types import SimpleNamespace

import jax
import jax.numpy as jnp
from jax import lax
from jax.experimental import pallas as pl
from jax.experimental.pallas import tpu as pltpu
from jax.sharding import PartitionSpec as P

AXES = ("dp", "fsdp")
HEADS = 16
HEAD_DIM = 64
BLOCK = 64


epsilon = 1e-06
masked_score = -1e30


def normalize(values):
    inv_rms = lax.rsqrt(jnp.mean(values * values, axis=-1, keepdims=True) + epsilon)
    return (values * inv_rms, inv_rms)


def norm_back(normed, inv_rms, upstream):
    return inv_rms * (upstream - normed * jnp.mean(upstream * normed, axis=-1, keepdims=True))


def project(left_rows, right_rows):
    return jnp.dot(left_rows, right_rows, preferred_element_type=jnp.float32)


def project_back(upstream, weight):
    return lax.dot_general(
        upstream, weight, (((1,), (1,)), ((), ())), preferred_element_type=jnp.float32
    )


def weight_grad(inputs, upstream):
    return lax.dot_general(
        inputs, upstream, (((0,), (0,)), ((), ())), preferred_element_type=jnp.float32
    )


def split_heads(row_block):
    row_count = row_block.shape[0]
    return row_block.reshape(row_count // BLOCK, BLOCK, HEADS, HEAD_DIM)


def block_scores(query_blocks, key_blocks):
    scores = jnp.einsum(
        "bihd,bjhd->bhij", query_blocks, key_blocks, preferred_element_type=jnp.float32
    ) * HEAD_DIM ** (-0.5)
    causal = lax.broadcasted_iota(jnp.int32, (BLOCK, BLOCK), 0) >= lax.broadcasted_iota(
        jnp.int32, (BLOCK, BLOCK), 1
    )
    return jnp.where(causal, scores, masked_score)


def attend(query_rows, key_rows, value_rows):
    scores = block_scores(split_heads(query_rows), split_heads(key_rows))
    row_max = jnp.max(scores, axis=-1, keepdims=True)
    exp_scores = jnp.exp(scores - row_max)
    row_total = jnp.sum(exp_scores, axis=-1, keepdims=True)
    probs_low = (exp_scores / row_total).astype(jnp.bfloat16)
    head_mix = jnp.einsum(
        "bhij,bjhd->bihd", probs_low, split_heads(value_rows), preferred_element_type=jnp.float32
    )
    return (head_mix.reshape(query_rows.shape[0], -1), row_max + jnp.log(row_total))


def attend_back(query_rows, key_rows, value_rows, logsum, grad_mix):
    query_blocks = split_heads(query_rows)
    key_blocks = split_heads(key_rows)
    value_blocks = split_heads(value_rows)
    grad_blocks = split_heads(grad_mix)
    probs = jnp.exp(block_scores(query_blocks, key_blocks) - logsum)
    probs_low = probs.astype(jnp.bfloat16)
    grad_probs = jnp.einsum(
        "bihd,bjhd->bhij", grad_blocks, value_blocks, preferred_element_type=jnp.float32
    )
    grad_values = jnp.einsum(
        "bhij,bihd->bjhd", probs_low, grad_blocks, preferred_element_type=jnp.float32
    )
    grad_scores = (
        probs * (grad_probs - jnp.sum(grad_probs * probs, axis=-1, keepdims=True))
    ).astype(jnp.bfloat16)
    scale_factor = HEAD_DIM ** (-0.5)
    grad_queries = (
        jnp.einsum("bhij,bjhd->bihd", grad_scores, key_blocks, preferred_element_type=jnp.float32)
        * scale_factor
    )
    grad_keys = (
        jnp.einsum("bhij,bihd->bjhd", grad_scores, query_blocks, preferred_element_type=jnp.float32)
        * scale_factor
    )
    row_count = query_rows.shape[0]
    return (
        grad_queries.reshape(row_count, -1).astype(jnp.bfloat16),
        grad_keys.reshape(row_count, -1).astype(jnp.bfloat16),
        grad_values.reshape(row_count, -1).astype(jnp.bfloat16),
    )


def ffn_sums(second_in, hidden, grad_first_proj, grad_second_proj, grad_branch):
    both_proj = jnp.concatenate([grad_first_proj, grad_second_proj], axis=1)
    inner_shard = lax.psum_scatter(
        weight_grad(second_in, both_proj), AXES, scatter_dimension=0, tiled=True
    )
    down_shard = lax.psum_scatter(
        weight_grad(hidden, grad_branch), AXES, scatter_dimension=0, tiled=True
    )
    ff_width = grad_first_proj.shape[1]
    return (inner_shard[:, :ff_width], inner_shard[:, ff_width:], down_shard)


def general_body(
    tokens,
    lengths,
    cotangent,
    w_query,
    w_key,
    w_value,
    w_gate,
    w_out,
    out_gain,
    w_first,
    w_second,
    w_down,
):
    slot_count, slot_len, feature_width = tokens.shape
    row_count = slot_count * slot_len
    places = lax.broadcasted_iota(jnp.int32, (slot_count, slot_len), 1)
    live_rows = (places < lengths[:, None]).astype(jnp.float32).reshape(row_count, 1)
    attn_full = (
        lax.all_gather(w_query, AXES, axis=0, tiled=True),
        lax.all_gather(w_key, AXES, axis=0, tiled=True),
        lax.all_gather(w_value, AXES, axis=0, tiled=True),
        lax.all_gather(w_gate, AXES, axis=0, tiled=True),
        lax.all_gather(w_out, AXES, axis=0, tiled=True),
        lax.all_gather(out_gain, AXES, axis=0, tiled=True),
    )
    ffn_full = (
        lax.all_gather(w_first, AXES, axis=0, tiled=True),
        lax.all_gather(w_second, AXES, axis=0, tiled=True),
        lax.all_gather(w_down, AXES, axis=0, tiled=True),
    )
    query_full, key_full, value_full, gate_full, out_full, gain_full = attn_full
    first_full, second_full, down_full = ffn_full
    inputs = tokens.reshape(row_count, feature_width).astype(jnp.float32)
    normed_in, inv_in = normalize(inputs)
    first_in = normed_in.astype(jnp.bfloat16)
    query_rows = project(first_in, query_full).astype(jnp.bfloat16)
    key_rows = project(first_in, key_full).astype(jnp.bfloat16)
    value_rows = project(first_in, value_full).astype(jnp.bfloat16)
    gate_pre = project(first_in, gate_full)
    head_mix, logsum = attend(query_rows, key_rows, value_rows)
    normed_mix, inv_mix = normalize(head_mix)
    gain_rows = gain_full.astype(jnp.float32)
    gate_act = jax.nn.silu(gate_pre)
    scaled_mix = normed_mix * gain_rows
    branch_in = (scaled_mix * gate_act).astype(jnp.bfloat16)
    middle = inputs + live_rows * project(branch_in, out_full)
    normed_mid, inv_mid = normalize(middle)
    second_in = normed_mid.astype(jnp.bfloat16)
    first_proj = project(second_in, first_full)
    second_proj = project(second_in, second_full)
    hidden = (first_proj * second_proj).astype(jnp.bfloat16)
    final_rows = middle + live_rows * project(hidden, down_full)
    layer_out = final_rows.astype(jnp.bfloat16).reshape(tokens.shape)
    first_back, second_back, down_back = (
        lax.all_gather(w_first, AXES, axis=0, tiled=True),
        lax.all_gather(w_second, AXES, axis=0, tiled=True),
        lax.all_gather(w_down, AXES, axis=0, tiled=True),
    )
    query_back, key_back, value_back, gate_back, out_back, gain_back = (
        lax.all_gather(w_query, AXES, axis=0, tiled=True),
        lax.all_gather(w_key, AXES, axis=0, tiled=True),
        lax.all_gather(w_value, AXES, axis=0, tiled=True),
        lax.all_gather(w_gate, AXES, axis=0, tiled=True),
        lax.all_gather(w_out, AXES, axis=0, tiled=True),
        lax.all_gather(out_gain, AXES, axis=0, tiled=True),
    )
    gain_used = gain_back.astype(jnp.float32)
    grad_final = cotangent.reshape(row_count, feature_width).astype(jnp.float32)
    grad_branch = (live_rows * grad_final).astype(jnp.bfloat16)
    grad_hidden = project_back(grad_branch, down_back)
    grad_first_proj = (grad_hidden * second_proj).astype(jnp.bfloat16)
    grad_second_proj = (grad_hidden * first_proj).astype(jnp.bfloat16)
    grad_normed_mid = project_back(grad_first_proj, first_back) + project_back(
        grad_second_proj, second_back
    )
    grad_middle = grad_final + norm_back(normed_mid, inv_mid, grad_normed_mid)
    grad_attn_out = (live_rows * grad_middle).astype(jnp.bfloat16)
    grad_branch_in = project_back(grad_attn_out, out_back)
    gain_terms = grad_branch_in * gate_act * normed_mix
    sigmoid_gate = jax.nn.sigmoid(gate_pre)
    grad_gate_pre = (
        grad_branch_in * scaled_mix * sigmoid_gate * (1.0 + gate_pre * (1.0 - sigmoid_gate))
    ).astype(jnp.bfloat16)
    grad_scaled = grad_branch_in * gate_act * gain_used
    grad_mix = norm_back(normed_mix, inv_mix, grad_scaled).astype(jnp.bfloat16)
    grad_queries, grad_keys, grad_values = attend_back(
        query_rows, key_rows, value_rows, logsum, grad_mix
    )
    grad_normed_in = (
        project_back(grad_queries, query_back)
        + project_back(grad_keys, key_back)
        + project_back(grad_values, value_back)
        + project_back(grad_gate_pre, gate_back)
    )
    grad_inputs = grad_middle + norm_back(normed_in, inv_in, grad_normed_in)
    input_grad = grad_inputs.astype(jnp.bfloat16).reshape(tokens.shape)
    ffn_shards = ffn_sums(second_in, hidden, grad_first_proj, grad_second_proj, grad_branch)
    four_grads = jnp.concatenate([grad_queries, grad_keys, grad_values, grad_gate_pre], axis=1)
    from_input = weight_grad(first_in, four_grads)
    from_branch = weight_grad(branch_in, grad_attn_out)
    gain_part = jnp.sum(gain_terms, axis=0)[:, None]
    attn_shard = lax.psum_scatter(
        jnp.concatenate([from_input, from_branch, gain_part], axis=1),
        AXES,
        scatter_dimension=0,
        tiled=True,
    )
    shard_query = attn_shard[:, 0:feature_width]
    shard_key = attn_shard[:, feature_width : 2 * feature_width]
    shard_value = attn_shard[:, 2 * feature_width : 3 * feature_width]
    shard_gate = attn_shard[:, 3 * feature_width : 4 * feature_width]
    shard_out = attn_shard[:, 4 * feature_width : 5 * feature_width]
    shard_gain = attn_shard[:, 5 * feature_width]
    shard_first, shard_second, shard_down = ffn_shards
    return (
        layer_out,
        input_grad,
        shard_query,
        shard_key,
        shard_value,
        shard_gate,
        shard_out,
        shard_gain,
        shard_first,
        shard_second,
        shard_down,
    )


MESH = pl.DeviceIdType.MESH
f32 = jnp.float32
bf16 = jnp.bfloat16
QUERY, KEY, VALUE, GATE, GAIN, OUT, FIRST, SECOND, DOWN = range(9)
DOWN_PARTIAL = "down_partial"


def bind(trees, refs):
    fields = {}
    for tree in trees:
        leaves, form = jax.tree.flatten(tree)
        fields |= jax.tree.unflatten(form, refs[: len(leaves)])
        refs = refs[len(leaves) :]
    return SimpleNamespace(**fields)


class Place:
    def __init__(self):
        dp, fs = lax.axis_index(AXES[0]), lax.axis_index(AXES[1])
        z, c = lax.div(fs, 2), lax.rem(fs, 2)
        self.dp, self.fs, self.z, self.c = dp, fs, z, c
        self.nx = dp + 1 - 2 * lax.rem(dp, 2)
        self.ny = lax.rem(dp + 2, 4)
        self.dg = lax.rem(self.nx + 2, 4)
        self.zp = [lax.rem(z + k, 4) for k in (1, 2, 3)]
        self.sib = (dp, z * 2 + 1 - c)
        self.zdev = [(dp, zz * 2 + c) for zz in self.zp]
        self.xdev, self.ydev = (self.nx, fs), (self.ny, fs)
        self.peers = [self.sib, self.xdev, self.ydev] + self.zdev
        self.above, self.below, self.always = z < 3, z > 0, None
        self.end = (z == 0) | (z == 3)
        self.middle = (z == 1) | (z == 2)
        self.inward = z + 1 - 2 * lax.rem(z, 2)
        self.inward_dev = (dp, self.inward * 2 + c)

    def barrier(self):
        bar = pltpu.get_barrier_semaphore()
        for d in self.peers:
            pl.semaphore_signal(bar, inc=1, device_id=d, device_id_type=MESH)
        pl.semaphore_wait(bar, 6)


def where_true(cond, run):
    if cond is None:
        run()
    else:
        pl.when(cond)(run)


class Moves:
    def __init__(self, here, ssem, rsem):
        self.h, self.ssem, self.rsem, self.sends = here, ssem, rsem, {}
        self.along_z = ((0, here.above), (1, None), (2, here.below))
        self.from_z = ((0, here.below), (1, None), (2, here.above))

    def rc(self, i, k, src, dst, dev):
        return pltpu.make_async_remote_copy(
            src_ref=src, dst_ref=dst, send_sem=self.ssem.at[i, k], recv_sem=self.rsem.at[i, k],
            device_id=dev, device_id_type=MESH,
        )

    def go(self, i, *moves, cond=None):
        for m in moves:
            where_true(cond, m.start)
            self.sends.setdefault(i, []).append((cond, m))

    def release(self, i):
        for cond, m in self.sends.pop(i, ()):
            where_true(cond, m.wait_send)

    def finish(self):
        for i in list(self.sends):
            self.release(i)


class Gather(Moves):
    def __init__(self, here, items, shards, outs, ssem, rsem, lsem):
        super().__init__(here, ssem, rsem)
        self.items, self.shards, self.outs, self.lsem = items, shards, outs, lsem

    def block(self, i, yx, z, rows=slice(None)):
        m, c0, w, _ = self.items[i]
        return self.outs[m].at[yx, z, self.h.c, rows, pl.ds(c0, w)]

    def shard(self, i):
        m, c0, w, _ = self.items[i]
        return self.shards[m].at[:, pl.ds(c0, w)]

    def same(self, i, k, ref, dev):
        return self.rc(i, k, ref, ref, dev)

    def own(self, i):
        return pltpu.make_async_copy(self.shard(i), self.block(i, self.h.dp, self.h.z), self.lsem.at[i])

    def zmsg(self, i, k, planes):
        h = self.h
        if planes:
            return self.same(i, k, self.block(i, slice(None), h.z), h.zdev[k])
        return self.rc(i, k, self.shard(i), self.block(i, h.dp, h.z), h.zdev[k])

    def relay(self, i, planes):
        h = self.h
        return self.same(i, 11, self.block(i, slice(None) if planes else h.dp, h.zp[1]), h.inward_dev)

    def send_z(self, i, planes):
        for k, cond in self.along_z:
            self.go(i, self.zmsg(i, k, planes), cond=cond)

    def relay_z(self, i, planes):
        self.zmsg(i, 1, planes).wait_recv()
        self.go(i, self.relay(i, planes), cond=self.h.middle)

    def wait_z(self, i, planes):
        where_true(self.h.below, self.zmsg(i, 0, planes).wait_recv)
        where_true(self.h.above, self.zmsg(i, 2, planes).wait_recv)
        where_true(self.h.end, self.relay(i, planes).wait_recv)

    def col(self, i, k, yx, dev):
        return self.same(i, k, self.block(i, yx, slice(None)), dev)

    def half(self, i, k, yx, lo, dev):
        return self.same(i, k, self.block(i, yx, slice(lo, lo + 2)), dev)

    def part(self, i, k, yx, lo, dev):
        n = self.shards[self.items[i][0]].shape[0] // 2
        return self.same(i, k, self.block(i, yx, self.h.z, pl.ds(lo * n, n)), dev)

    def column0(self, i):
        self.own(i).start()
        self.send_z(i, False)

    def column1(self, i):
        self.relay_z(i, False)

    def column2(self, i):
        h = self.h
        self.own(i).wait()
        self.wait_z(i, False)
        self.go(i, self.col(i, 3, h.dp, h.xdev), self.col(i, 4, h.dp, h.ydev), self.col(i, 7, h.dp, h.sib))

    def column3(self, i):
        h = self.h
        self.col(i, 3, h.dp, h.xdev).wait_recv()
        self.go(i, self.half(i, 6, h.nx, 2, h.ydev), self.col(i, 8, h.nx, h.sib))
        self.col(i, 4, h.dp, h.ydev).wait_recv()
        self.go(i, self.half(i, 5, h.ny, 0, h.xdev), self.col(i, 9, h.ny, h.sib))

    def column4(self, i):
        h = self.h
        self.half(i, 5, h.ny, 0, h.xdev).wait_recv()
        self.half(i, 6, h.nx, 2, h.ydev).wait_recv()
        self.go(i, self.col(i, 10, h.dg, h.sib))

    def column5(self, i):
        h = self.h
        for k in (7, 8, 9, 10):
            self.col(i, k, h.dp, h.sib).wait_recv()

    def plane0(self, i):
        h = self.h
        self.own(i).start()
        self.go(
            i, self.rc(i, 3, self.shard(i), self.block(i, h.dp, h.z), h.xdev),
            self.rc(i, 4, self.shard(i), self.block(i, h.dp, h.z), h.ydev),
        )

    def plane1(self, i):
        h = self.h
        self.same(i, 3, self.block(i, h.nx, h.z), h.xdev).wait_recv()
        self.go(i, self.part(i, 6, h.nx, 1, h.ydev))
        self.same(i, 4, self.block(i, h.ny, h.z), h.ydev).wait_recv()
        self.go(i, self.part(i, 5, h.ny, 0, h.xdev))

    def plane2(self, i):
        h = self.h
        self.own(i).wait()
        self.part(i, 5, h.dg, 0, h.xdev).wait_recv()
        self.part(i, 6, h.dg, 1, h.ydev).wait_recv()
        self.send_z(i, True)
        self.go(i, self.same(i, 7, self.block(i, slice(None), h.z), h.sib))

    def plane3(self, i):
        self.relay_z(i, True)

    def plane4(self, i):
        h = self.h
        self.wait_z(i, True)
        self.go(i, *[self.same(i, 8 + k, self.block(i, slice(None), h.zp[k]), h.sib) for k in range(3)])

    def plane5(self, i):
        h = self.h
        for k in (7, 8, 9, 10):
            self.same(i, k, self.block(i, slice(None), h.z), h.sib).wait_recv()

    def timed_steps(self):
        steps = []
        for m, _, w, planes in self.items:
            u = w * self.shards[m].shape[0] / (32 * 1024)
            if planes:
                steps.append([
                    (self.plane0, 1, 1.5 * u, 0.2), (self.plane1, 1, 0.8 * u, 0.2), (self.plane2, 2, 10.0 * u, 0.2),
                    (self.plane3, 2, 8.0 * u, 0.1), (self.plane4, 3, 1.0 * u, 0.1), (self.plane5, None, 0.0, 0.1),
                ])
            else:
                steps.append([
                    (self.column0, 2, 2.5 * u, 0.2), (self.column1, 2, 2.0 * u, 0.1), (self.column2, 1, 5.8 * u, 0.2),
                    (self.column3, 1, 2.9 * u, 0.2), (self.column4, 3, 1.0 * u, 0.1), (self.column5, None, 0.0, 0.1),
                ])
        return steps


class Scatter(Moves):
    def __init__(self, here, items, bufs, before, ssem, rsem, lsem, free):
        super().__init__(here, ssem, rsem)
        self.items, self.bufs, self.before, self.lsem, self.free = items, bufs, before, lsem, free

    def views(self, i):
        it = self.items[i]
        return it, self.bufs[it.cls], it.slot, it.w

    def mine(self, i, yx, z, rows=slice(None)):
        it, b, s, w = self.views(i)
        if b.p is not None:
            return b.p.at[s, yx, z, rows, 0:w]
        return b.g.at[s, yx, z, self.h.c, rows, 0:w]

    def buf(self, i, ref, *at):
        return ref.at[(self.items[i].slot,) + at + (slice(None), slice(0, self.items[i].w))]

    def m_sib(self, i):
        it, b, s, w = self.views(i)
        if b.p is not None:
            src = it.src.at[:, :, 1 - self.h.c, :, pl.ds(it.s0, w)]
        else:
            src = b.g.at[s, :, :, 1 - self.h.c, :, 0:w]
        return self.rc(i, 0, src, self.buf(i, b.r1, slice(None), slice(None)), self.h.sib)

    def m_load(self, i):
        it, b, s, w = self.views(i)
        src = it.src.at[:, :, self.h.c, :, pl.ds(it.s0, w)]
        return pltpu.make_async_copy(src, self.buf(i, b.p, slice(None), slice(None)), self.lsem.at[i])

    def add(self, to, *terms):
        total = to[...].astype(f32)
        for t in terms:
            total = total + t[...].astype(f32)
        to[...] = total.astype(to.dtype)

    def step0(self, i):
        it, b, s, w = self.views(i)
        if it.before is not None:
            self.release(it.before)
            for k in range(6):
                pl.semaphore_wait(self.free.at[it.cls, k], 1)
        self.before(i)
        if b.p is not None:
            self.m_load(i).start()
        self.go(i, self.m_sib(i))

    def wait_halves(self, i):
        if self.bufs[self.items[i].cls].p is not None:
            self.m_load(i).wait()
        self.m_sib(i).wait_recv()

    def last(self, i):
        it = self.items[i]
        if it.reused:
            for k, d in enumerate(self.h.peers):
                pl.semaphore_signal(
                    self.free.at[it.cls, k if k < 3 else 8 - k], inc=1, device_id=d, device_id_type=MESH
                )

    def m_z(self, i, k, yx):
        b = self.bufs[self.items[i].cls]
        more = () if yx is None else (slice(None),)
        yx = self.h.dp if yx is None else yx
        return self.rc(i, 5 + k, self.mine(i, yx, self.h.zp[k]), self.buf(i, b.rz, k, *more), self.h.zdev[k])

    def m_relay(self, i, yx):
        b = self.bufs[self.items[i].cls]
        more = () if yx is None else (slice(None),)
        yx = self.h.dp if yx is None else yx
        return self.rc(i, 8, self.mine(i, yx, 3 - self.h.z), self.buf(i, b.rz, 3, *more), self.h.inward_dev)

    def send_z(self, i, yx=None):
        self.go(i, self.m_relay(i, yx), cond=self.h.end)
        self.go(i, self.m_z(i, 1, yx), cond=self.h.end)
        self.go(i, self.m_z(i, 0, yx), cond=self.h.above)
        self.go(i, self.m_z(i, 2, yx), cond=self.h.below)

    def relay_z(self, i, yx=None):
        def run():
            b = self.bufs[self.items[i].cls]
            self.m_relay(i, yx).wait_recv()
            if yx is None:
                self.add(self.mine(i, self.h.dp, self.h.zp[1]), self.buf(i, b.rz, 3))
            else:
                tiles(4, lambda j: self.add(self.mine(i, j, self.h.zp[1]), self.buf(i, b.rz, 3, j)))

        where_true(self.h.middle, run)
        self.go(i, self.m_z(i, 1, yx), cond=self.h.middle)

    def m_dx(self, i):
        b = self.bufs[self.items[i].cls]
        return self.rc(i, 1, self.mine(i, self.h.dg, slice(0, 2)), self.buf(i, b.rd, 0, slice(None)), self.h.xdev)

    def m_dy(self, i):
        b = self.bufs[self.items[i].cls]
        return self.rc(i, 2, self.mine(i, self.h.dg, slice(2, 4)), self.buf(i, b.rd, 1, slice(None)), self.h.ydev)

    def m_x(self, i):
        b = self.bufs[self.items[i].cls]
        return self.rc(i, 3, self.mine(i, self.h.nx, slice(None)), self.buf(i, b.rxy, 0, slice(None)), self.h.xdev)

    def m_y(self, i):
        b = self.bufs[self.items[i].cls]
        return self.rc(i, 4, self.mine(i, self.h.ny, slice(None)), self.buf(i, b.rxy, 1, slice(None)), self.h.ydev)

    def column1(self, i):
        r, dg = self.bufs[self.items[i].cls].r1, self.h.dg
        self.wait_halves(i)
        tiles(4, lambda j: self.add(self.mine(i, dg, j), self.buf(i, r, dg, j)))
        self.go(i, self.m_dx(i), self.m_dy(i))

        def near(j):
            a, q = lax.rem(dg + 1 + lax.div(j, 4), 4), lax.rem(j, 4)
            self.add(self.mine(i, a, q), self.buf(i, r, a, q))

        tiles(12, near)

    def column2(self, i):
        rd, nx, ny = self.bufs[self.items[i].cls].rd, self.h.nx, self.h.ny
        self.m_dx(i).wait_recv()
        tiles(2, lambda j: self.add(self.mine(i, ny, j), self.buf(i, rd, 0, j)))
        self.go(i, self.m_y(i))
        self.m_dy(i).wait_recv()
        tiles(2, lambda j: self.add(self.mine(i, nx, 2 + j), self.buf(i, rd, 1, j)))
        self.go(i, self.m_x(i))

    def column3(self, i):
        rxy, dp = self.bufs[self.items[i].cls].rxy, self.h.dp
        self.m_x(i).wait_recv()
        self.m_y(i).wait_recv()
        tiles(4, lambda j: self.add(self.mine(i, dp, j), self.buf(i, rxy, 0, j), self.buf(i, rxy, 1, j)))
        self.send_z(i)

    def column4(self, i):
        self.relay_z(i)

    def column5(self, i):
        it, b, s, w = self.views(i)
        cols = pl.ds(it.c0, w)
        self.m_z(i, 1, None).wait_recv()
        it.out[:, cols] = self.mine(i, self.h.dp, self.h.z)[...].astype(f32) + self.buf(i, b.rz, 1)[...].astype(f32)
        for k, cond in self.from_z:
            if cond is not None:

                def more(k=k):
                    self.m_z(i, k, None).wait_recv()
                    it.out[:, cols] += self.buf(i, b.rz, k)[...].astype(f32)

                pl.when(cond)(more)
        self.last(i)

    def plane1(self, i):
        r = self.bufs[self.items[i].cls].r1
        self.wait_halves(i)

        def both(j):
            a, q = lax.div(j, 4), lax.rem(j, 4)
            self.add(self.mine(i, a, q), self.buf(i, r, a, q))

        tiles(16, both)
        self.send_z(i, slice(None))

    def plane2(self, i):
        self.relay_z(i, slice(None))

    def p_d(self, i, n):
        b, h = self.bufs[self.items[i].cls], self.h
        rows = self.items[i].out.shape[0] // 2
        src = self.mine(i, h.dg, h.z, pl.ds(n * rows, rows))
        return self.rc(i, 1 + n, src, self.buf(i, b.rd, n), (h.xdev, h.ydev)[n])

    def p_xy(self, i, n):
        b, h = self.bufs[self.items[i].cls], self.h
        return self.rc(
            i, 3 + n, self.mine(i, (h.nx, h.ny)[n], h.z), self.buf(i, b.rxy, n), (h.xdev, h.ydev)[n]
        )

    def plane3(self, i):
        b, z = self.bufs[self.items[i].cls], self.h.z
        for k, cond in self.from_z:

            def more(k=k):
                self.m_z(i, k, slice(None)).wait_recv()
                tiles(4, lambda j: self.add(self.mine(i, j, z), self.buf(i, b.rz, k, j)))

            where_true(cond, more)
        self.go(i, self.p_d(i, 0), self.p_d(i, 1))

    def plane4(self, i):
        b, h = self.bufs[self.items[i].cls], self.h
        rows = self.items[i].out.shape[0] // 2
        for n, other in ((0, h.ny), (1, h.nx)):
            self.p_d(i, n).wait_recv()
            self.add(self.mine(i, other, h.z, pl.ds(n * rows, rows)), self.buf(i, b.rd, n))
            self.go(i, self.p_xy(i, 1 - n))

    def plane5(self, i):
        it, b, s, w = self.views(i)
        self.p_xy(i, 0).wait_recv()
        self.p_xy(i, 1).wait_recv()
        total = self.mine(i, self.h.dp, self.h.z)[...].astype(f32)
        it.out[:, pl.ds(it.c0, w)] = total + self.buf(i, b.rxy, 0)[...].astype(f32) + self.buf(i, b.rxy, 1)[...].astype(f32)
        self.last(i)

    def timed_steps(self):
        steps = []
        for i, it in enumerate(self.items):
            u = it.w * it.out.shape[0] / (32 * 1024)
            first = (self.step0, -i - 1, 1.5 * u, 0.2)
            if it.cls == PLANE_RING:
                steps.append([
                    first, (self.plane1, 2, 10.0 * u, 0.5 * u + 0.2), (self.plane2, 2, 8.0 * u, 0.1 * u + 0.1),
                    (self.plane3, 1, 0.8 * u, 0.2 * u + 0.2), (self.plane4, 1, 1.5 * u, 0.2),
                    (self.plane5, None, 0.0, 0.2),
                ])
            else:
                steps.append([
                    first, (self.column1, 1, 2.9 * u, 0.4 * u + 0.2), (self.column2, 1, 5.8 * u, 0.2 * u + 0.2),
                    (self.column3, 2, 2.5 * u, 0.2 * u + 0.2), (self.column4, 2, 2.0 * u, 0.1),
                    (self.column5, None, 0.0, 0.2),
                ])
        return steps

    def after(self):
        return [set() if it.before is None else {it.before} for it in self.items]


DOWN_RING, IN_RING, PLANE_RING, GAIN_RING = range(4)


def scatter_plan(specs, ring):
    items, by_class = [], {}
    for m, c0, w, g0, cls in specs:
        mine = by_class.setdefault(cls, [])
        it = SimpleNamespace(m=m, c0=c0, w=w, g0=g0, cls=cls, slot=len(mine) % ring[cls], before=None, reused=False)
        if len(mine) >= ring[cls]:
            it.before = mine[-ring[cls]]
            items[it.before].reused = True
        mine.append(len(items))
        items.append(it)
    return items


def scatter_scratch(cls, slots, r, w, dt):
    held, planes = cls == GAIN_RING, cls == PLANE_RING
    return dict(
        g=pltpu.VMEM((slots, 4, 4, 2, r, w) if held else (8, 128), dt),
        p=pltpu.VMEM((8, 128) if held else (slots, 4, 4, r, w), dt),
        r1=pltpu.VMEM((slots, 4, 4, r, w), dt),
        rd=pltpu.VMEM((slots, 2, r // 2, w) if planes else (slots, 2, 2, r, w), dt),
        rxy=pltpu.VMEM((slots, 2, r, w) if planes else (slots, 2, 4, r, w), dt),
        rz=pltpu.VMEM((slots, 4, 4, r, w) if planes else (slots, 4, r, w), dt),
    )


def ring_buffers(rings):
    bufs = [SimpleNamespace(**b) for b in rings]
    for cls, b in enumerate(bufs):
        if cls == GAIN_RING:
            b.p = None
        else:
            b.g = None
    return bufs


def column_parts(width, part):
    return [(c0, min(part, width - c0)) for c0 in range(0, width, part)]


def dot_nn(a, b):
    return jnp.dot(a, b, preferred_element_type=f32)


def dot_nt(a, b):
    return lax.dot_general(a, b, (((1,), (1,)), ((), ())), preferred_element_type=f32)


def dot_tn(a, b):
    return lax.dot_general(a, b, (((0,), (0,)), ((), ())), preferred_element_type=f32)


def tiles(count, body):
    def step(i, carry):
        body(i)
        return carry

    lax.fori_loop(0, count, step, 0)


def rows_of(i, size):
    return pl.ds(pl.multiple_of(i * size, size), size)


def rms_inv(values):
    return lax.rsqrt(jnp.mean(values * values, axis=-1, keepdims=True) + epsilon)


QUAD = 4 * HEAD_DIM


def quad_mask():
    shape = (QUAD, QUAD)
    row = lax.div(lax.broadcasted_iota(jnp.int32, shape, 0), HEAD_DIM)
    return row == lax.div(lax.broadcasted_iota(jnp.int32, shape, 1), HEAD_DIM)


def spread_heads(rows, mask):
    tall = jnp.concatenate([rows] * 4, axis=0)
    return jnp.where(mask, tall, jnp.zeros_like(tall))


def per_head(values, reduce, fill):
    halves = []
    for k in range(2):
        part = values[:, 128 * k : 128 * (k + 1)]
        low = lax.broadcasted_iota(jnp.int32, part.shape, 1) < HEAD_DIM
        first = reduce(jnp.where(low, part, fill), axis=-1, keepdims=True)
        second = reduce(jnp.where(low, fill, part), axis=-1, keepdims=True)
        halves.append(jnp.where(low, first, second))
    return jnp.concatenate(halves, axis=1)


def attend_blocks(b, q, k, v, probs, mix):
    mask = quad_mask()
    place = lax.broadcasted_iota(jnp.int32, (BLOCK, QUAD), 0)
    causal = place >= lax.rem(lax.broadcasted_iota(jnp.int32, (BLOCK, QUAD), 1), HEAD_DIM)
    at = [
        (rows_of(2 * b + n, BLOCK), slice(QUAD * g, QUAD * (g + 1))) for n in range(2) for g in range(HEADS // 4)
    ]
    scores = [
        jnp.where(causal, dot_nt(q[i], spread_heads(k[i], mask)) * HEAD_DIM ** (-0.5), masked_score) for i in at
    ]
    tops = [per_head(s, jnp.max, masked_score) for s in scores]
    terms = [jnp.exp(s - m) for s, m in zip(scores, tops)]
    totals = [per_head(t, jnp.sum, 0.0) for t in terms]
    lows = [(t / n).astype(bf16) for t, n in zip(terms, totals)]
    mixes = [dot_nn(p, spread_heads(v[i], mask)) for i, p in zip(at, lows)]
    for i, p, m in zip(at, lows, mixes):
        probs[i] = p
        mix[i] = m


def attend_blocks_back(b, q, k, v, probs, grad_mix, dq, dk, dv):
    mask = quad_mask()
    scale = HEAD_DIM ** (-0.5)
    low = lax.broadcasted_iota(jnp.int32, (BLOCK, 128), 1) < HEAD_DIM

    def own_head(wide):
        return jnp.concatenate(
            [
                jnp.where(low, wide[0:64, 0:128], wide[64:128, 0:128]),
                jnp.where(low, wide[128:192, 128:256], wide[192:256, 128:256]),
            ],
            axis=1,
        )

    at = [
        (rows_of(2 * b + n, BLOCK), slice(QUAD * g, QUAD * (g + 1))) for n in range(2) for g in range(HEADS // 4)
    ]
    dps = [dot_nt(grad_mix[i], spread_heads(v[i], mask)) for i in at]
    dvs = [own_head(dot_tn(probs[i], grad_mix[i])) for i in at]
    ps = [probs[i].astype(f32) for i in at]
    means = [per_head(dp * p, jnp.sum, 0.0) for dp, p in zip(dps, ps)]
    dss = [(p * (dp - m)).astype(bf16) for p, dp, m in zip(ps, dps, means)]
    dqs = [dot_nn(ds, spread_heads(k[i], mask)) * scale for i, ds in zip(at, dss)]
    dks = [own_head(dot_tn(ds, q[i])) * scale for i, ds in zip(at, dss)]
    for i, a, c, d in zip(at, dqs, dks, dvs):
        dq[i] = a.astype(bf16)
        dk[i] = c.astype(bf16)
        dv[i] = d.astype(bf16)


class Saves:
    def __init__(self, sems):
        self.sems, self.count, self.open = sems, 0, {}

    def start(self, name, src, dst):
        m = pltpu.make_async_copy(src, dst, self.sems.at[self.count])
        self.count += 1
        m.start()
        self.open[name] = m

    def wait(self, *names):
        for name in names:
            if name in self.open:
                self.open.pop(name).wait()

    def finish(self):
        self.wait(*list(self.open))


FORWARD_COPIES = 64
X, DF, A1, Q, K, V, PB, GP, H, O, Y, A2, GAINS, SLABS = range(10, 24)


def forward_kernel(items, groups, trees, *refs):
    ref = bind(trees, refs)
    rows, width = ref.tokens.shape
    ff = ref.shards[FIRST].shape[1]
    parts = column_parts(ff, width)
    x, a1, q, k, v, pb, h, a2, e0, e1, e2, df = [ref.page.at[i] for i in range(12)]
    weight = [ref.weight.at[i] for i in range(4)]
    hidden, first, second = (e0, e1, e2), (q, k, v), (pb, h, x)
    wide = ref.wide
    gate_rows, mix_rows, mid_rows = [pl.ds(rows * i, rows) for i in range(3)]
    gp, o, y = wide.at[gate_rows], wide.at[mix_rows], wide.at[mid_rows]
    here = Place()
    here.barrier()
    ag = Gather(here, items, ref.shards, ref.full, ref.ssem, ref.rsem, ref.lsem)
    cp = Saves(ref.csem)
    size = 128
    live_len = ref.lengths[0]

    def live(i, n):
        return lax.broadcasted_iota(jnp.int32, (n, 1), 0) + i * n < live_len

    def spread(values):
        return jnp.broadcast_to(values, (values.shape[0], 128))

    cp.start(X, ref.tokens, x)
    cp.start(DF, ref.cotangent, df)

    def norm_in():
        cp.wait(X)

        def tile(i):
            r = rows_of(i, size)
            t = x[r, :].astype(f32)
            inv = rms_inv(t)
            a1[r, :] = (t * inv).astype(bf16)
            ref.inv_in[r, :] = spread(inv)

        tiles(rows // size, tile)
        cp.start(A1, a1, ref.save_a1)

    def mask_df():
        cp.wait(DF)

        def tile(i):
            r = rows_of(i, size)
            df[r, :] = jnp.where(live(i, size), df[r, :], jnp.zeros((), bf16))

        tiles(rows // size, tile)

    def load(slot, m, c0=0, w=None):
        src = ref.full[m]
        w = src.shape[-1] if w is None else w
        cp.start(slot, src.at[:, :, :, :, pl.ds(c0, w)], weight[slot].at[:, :, :, :, pl.ds(0, w)])

    def matrix(slot, w=None):
        w = width if w is None else w
        return weight[slot][:, :, :, :, 0:w].reshape(width, w)

    def projected(slot, dst, name=None, kept=None):
        def run():
            cp.wait(slot)

            def tile(i):
                r = rows_of(i, rows // 2)
                dst[r, :] = dot_nn(a1[r, :], matrix(slot)).astype(dst.dtype)

            tiles(2, tile)
            if kept is not None:
                cp.start(name, dst, kept)

        return run

    def gate_low():
        def tile(i):
            r = rows_of(i, size)
            e0[r, :] = gp[r, :].astype(bf16)

        tiles(rows // size, tile)
        cp.start(GP, e0, ref.save_gp)

    def attention(n, count):
        def run():
            tiles(count, lambda b: attend_blocks(b + n * count, q, k, v, pb, o))

        return run

    def mixed():
        cp.start(PB, pb, ref.save_pb)
        cp.wait(GAINS)
        gains = ref.gain
        gain = jnp.concatenate(
            [
                sum(gains[g, j, cc, 0:1, :].astype(f32) for j in (2 * half, 2 * half + 1) for cc in range(2))
                for g in range(4)
                for half in range(2)
            ],
            axis=1,
        )

        def tile(i):
            r = rows_of(i, size)
            t, z = o[r, :], gp[r, :]
            inv = rms_inv(t)
            h[r, :] = (t * inv * gain * (z * jax.nn.sigmoid(z))).astype(bf16)
            e1[r, :] = t.astype(bf16)
            ref.inv_mix[r, :] = spread(inv)

        tiles(rows // size, tile)
        cp.start(H, h, ref.save_h)
        cp.start(O, e1, ref.save_o)

    def middle(slot):
        def run():
            cp.wait(slot)

            def tile(i):
                r = rows_of(i, rows // 2)
                y[r, :] = dot_nn(h[r, :], matrix(slot))

            tiles(2, tile)

            def norm(i):
                r = rows_of(i, size)
                t = x[r, :].astype(f32) + jnp.where(live(i, size), y[r, :], 0.0)
                inv = rms_inv(t)
                y[r, :] = t
                a2[r, :] = (t * inv).astype(bf16)
                ref.inv_mid[r, :] = spread(inv)

            tiles(rows // size, norm)
            cp.start(Y, y, ref.save_y)
            cp.start(A2, a2, ref.save_a2)

        return run

    def gated(j, s1, s2, half):
        c0, w = parts[j]
        saved = ((first[j], ref.save_g1), (second[j], ref.save_g2), (hidden[j], ref.save_e))

        def run():
            if half == 0:
                cp.wait(s1, s2, Q, K, V, PB, H, GP, O)
            r = pl.ds(half * (rows // 2), rows // 2)
            up = dot_nn(a2[r, :], matrix(s1, w))
            first[j][r, 0:w] = up.astype(bf16)
            other = dot_nn(a2[r, :], matrix(s2, w))
            second[j][r, 0:w] = other.astype(bf16)
            hidden[j][r, 0:w] = (up * other).astype(bf16)
            if half == 1:
                for n, (page, kept) in enumerate(saved):
                    cp.start((j, n), page.at[:, 0:w], kept.at[:, pl.ds(c0, w)])

        return run

    def down_grad(j, c0, w):
        def run():
            if j == 2:
                cp.wait(Y)
            wide[pl.ds(parts[j][0] + c0, w), :] = dot_tn(hidden[j][:, c0 : c0 + w], df[...])

        return run

    def down_slabs():
        slabs = ref.slabs
        n = slabs.shape[1]

        def tile(d):
            slabs[d] = wide[pl.ds(pl.multiple_of(d * n, 8), n), :].astype(bf16)

        tiles(slabs.shape[0], tile)
        cp.start(SLABS, slabs, ref.down_partial)

    work = []

    def piece(cost, f, needs=()):
        work.append((f, cost, needs, ()))

    piece(1.5, norm_in)
    piece(0.5, mask_df)
    piece(2.3, projected(0, q, Q, ref.save_q), (0,))
    piece(2.3, projected(1, k, K, ref.save_k), (1,))
    piece(2.3, projected(2, v, V, ref.save_v), (2,))
    for n in range(rows // BLOCK // 4):
        piece(2.0, attention(n, 2))
    piece(2.3, projected(3, gp), (3,))
    piece(0.5, gate_low)
    piece(1.5, mixed, (4,))
    piece(3.2, middle(0), (5,))
    slots = ((1, 2), (3, 0), (1, 2))
    for j, (s1, s2) in enumerate(slots):
        for half in range(2):
            piece(2.5, gated(j, s1, s2, half), (6 + 2 * j, 7 + 2 * j))
    for j, (c0, w) in enumerate(parts):
        step = 512 if w % 512 == 0 else w // 2
        for n in range(w // step):
            piece(1.2, down_grad(j, n * step, step))
    piece(1.0, down_slabs)
    loads = {0: (0, QUERY), 1: (1, KEY), 2: (2, VALUE), 3: (3, GATE), 5: (0, OUT)}
    for j, (s1, s2) in enumerate(slots):
        loads[6 + 2 * j] = (s1, FIRST) + parts[j]
        loads[7 + 2 * j] = (s2, SECOND) + parts[j]
    readers = [sum(g in p[2] for p in work) for g in range(len(items))]
    ready, waiting, held = set(), [], {}

    def try_loads():
        while waiting:
            i = waiting[0]
            slot = loads[i][0]
            if slot in held and readers[held[slot]]:
                return
            held[slot] = i
            load(*loads[i])
            ready.add(i)
            waiting.pop(0)

    left = [sum(g == n for g in groups) for n in range(len(items))]

    def ended(i):
        group = groups[i]
        left[group] -= 1
        if left[group]:
            return
        if group in loads:
            waiting.append(group)
            try_loads()
        elif group == 4:
            cp.start(GAINS, ref.full[GAIN], ref.gain)
            ready.add(group)

    def reading(f, needs):
        def run():
            f()
            for i in needs:
                readers[i] -= 1
            try_loads()

        return run

    work = [(reading(f, needs), cost, needs, gives) for f, cost, needs, gives in work]
    Timeline(
        ag.timed_steps(), work, 2, range(len(items)), can_run=lambda needs: all(i in ready for i in needs), ended=ended,
    ).run()
    ag.finish()
    cp.start(30, ref.inv_in, ref.save_inv_in)
    cp.start(31, ref.inv_mix, ref.save_inv_mix)
    cp.start(32, ref.inv_mid, ref.save_inv_mid)
    cp.finish()


def forward(tokens, lengths, cotangent, shards):
    rows, width = tokens.shape
    ff = shards[FIRST].shape[1]
    parts = column_parts(ff, width)
    whole = [(m, 0, width) for m in (QUERY, KEY, VALUE, GATE)] + [(GAIN, 0, shards[GAIN].shape[1]), (OUT, 0, width)]
    whole += [(m, c0, w) for c0, w in parts for m in (FIRST, SECOND)]
    pieces = [(m, c0 + d, w, g) for g, (m, c0, n) in enumerate(whole) for d, w in column_parts(n, 512)]
    pieces.sort(key=lambda p: (p[3] if p[3] < 6 else 6 + (p[3] - 6) // 2, p[1]))
    pieces += [(DOWN, c0, w, len(whole)) for c0, w in column_parts(width, 256)]
    items = [(m, c0, w, n % 6 == 0 and m not in (GAIN, DOWN)) for n, (m, c0, w, _) in enumerate(pieces)]
    groups = [p[3] for p in pieces]
    n = len(items)
    page, row = jax.ShapeDtypeStruct((rows, width), bf16), jax.ShapeDtypeStruct((rows, 128), f32)
    wide = jax.ShapeDtypeStruct((rows, ff), bf16)
    saves = dict(
        save_a1=page, save_q=page, save_k=page, save_v=page, save_pb=page, save_gp=page, save_o=page, save_h=page,
        save_a2=page, save_g1=wide, save_g2=wide, save_e=wide, save_y=jax.ShapeDtypeStruct((rows, width), f32),
        save_inv_in=row, save_inv_mix=row, save_inv_mid=row,
    )
    slab = (32,) + shards[DOWN].shape
    saves[DOWN_PARTIAL] = jax.ShapeDtypeStruct(slab, bf16)
    outs = dict(full=[jax.ShapeDtypeStruct((4, 4, 2) + s.shape, bf16) for s in shards])
    inv = pltpu.VMEM((rows, 128), f32)
    scratch = dict(
        page=pltpu.VMEM((12, rows, width), bf16),
        weight=pltpu.VMEM((4, 4, 4, 2, shards[QUERY].shape[0], width), bf16),
        wide=pltpu.VMEM((3 * rows, width), f32),
        slabs=pltpu.VMEM(slab, bf16),
        gain=pltpu.VMEM((4, 4, 2) + shards[GAIN].shape, bf16),
        inv_in=inv, inv_mix=inv, inv_mid=inv,
        ssem=pltpu.SemaphoreType.DMA((n, 12)),
        rsem=pltpu.SemaphoreType.DMA((n, 12)),
        lsem=pltpu.SemaphoreType.DMA((n,)),
        csem=pltpu.SemaphoreType.DMA((FORWARD_COPIES,)),
    )
    ins = dict(cotangent=cotangent, shards=list(shards), tokens=tokens)
    hbm, vmem = pl.BlockSpec(memory_space=pl.ANY), pl.BlockSpec(memory_space=pltpu.VMEM)
    leaves = jax.tree.leaves
    got = pl.pallas_call(
        functools.partial(forward_kernel, items, groups, (dict(lengths=0), ins, outs, saves, scratch)),
        out_shape=leaves(outs) + leaves(saves),
        in_specs=[pl.BlockSpec(memory_space=pltpu.SMEM), hbm] + [vmem] * len(shards) + [hbm],
        out_specs=[hbm] * len(leaves(outs) + leaves(saves)),
        scratch_shapes=leaves(scratch),
        compiler_params=pltpu.CompilerParams(
            collective_id=0, has_side_effects=True, vmem_limit_bytes=62 * 2**20
        ),
    )(lengths, *leaves(ins))
    full = got[: len(shards)]
    return full, jax.tree.unflatten(jax.tree.structure(saves), got[len(shards) :])


class Timeline:
    def __init__(self, steps, work, window, given, after=None, can_run=None, ended=None):
        self.steps, self.work, self.window = steps, list(work), window
        self.after = after or [set()] * len(steps)
        self.can_run = can_run or (lambda needs: all(n in self.done for n in needs))
        self.ended = ended or (lambda i: None)
        self.made = set(given)
        self.at = [0] * len(steps)
        self.when = [0.0] * len(steps)
        self.free = {}
        self.now = 0.0
        self.done = set()

    def next_steps(self):
        started = 0
        for i, at in enumerate(self.at):
            if at == 0:
                if i in self.made and started < self.window and self.after[i] <= self.done:
                    yield i
                return
            if at < len(self.steps[i]):
                started += at < 2
                yield i

    def step(self, i):
        run, link, link_us, core_us = self.steps[i][self.at[i]]
        self.now = max(self.now, self.when[i])
        run(i)
        self.now += core_us
        begin = max(self.now, self.free.get(link, 0.0))
        if link:
            self.free[link] = begin + link_us
        self.when[i] = begin + link_us + (LATENCY if link else 0.0)
        self.at[i] += 1
        if self.at[i] == len(self.steps[i]):
            self.done.add(i)
            self.ended(i)

    def run(self):
        while True:
            steps = list(self.next_steps())
            ready = [i for i in steps if self.when[i] <= self.now]
            if ready:
                self.step(ready[0])
            elif self.work and self.can_run(self.work[0][2]):
                run, core_us, _, gives = self.work.pop(0)
                run()
                self.now += core_us
                for i in gives:
                    self.made.add(i)
                    self.when[i] = self.now + LATENCY
            elif steps:
                self.step(min(steps, key=lambda i: self.when[i]))
            else:
                return


LATENCY = 2.0


BACKWARD_COPIES = 64
PAGES = 9


def backward_kernel(items, trees, *refs):
    ref = bind(trees, refs)
    rows, width = ref.cotangent.shape
    ff = ref.full[FIRST].shape[1]
    parts = column_parts(ff, width)
    page = [ref.page.at[i] for i in range(PAGES)]
    acc, other = ref.wide.at[0], ref.wide.at[1]
    here = Place()
    here.barrier()
    bufs = ring_buffers(ref.rings)
    cp = Saves(ref.csem)
    made = sorted({(it.m, it.g0) for it in items if it.m not in (DOWN, GAIN)})
    items = [
        SimpleNamespace(
            **vars(it), out=ref.grads[it.m], s0=it.c0 - it.g0,
            src=ref.partials[made.index((it.m, it.g0))] if (it.m, it.g0) in made else ref.down_partial,
        )
        for it in items
    ]
    rs = Scatter(here, items, bufs, lambda i: cp.wait((items[i].m, items[i].g0)), ref.ssem, ref.rsem, ref.lsem, ref.free)
    size, half_rows = 128, rows // 2
    live_len = ref.lengths[0]

    def live(first, n):
        return lax.broadcasted_iota(jnp.int32, (n, 1), 0) + first < live_len

    def load(n, src, c0=None, w=None, by_row=False):
        dst = page[n]
        if c0 is not None:
            if by_row:
                src, dst = src.at[pl.ds(c0, w)], dst.at[pl.ds(0, w)]
            else:
                src, dst = src.at[:, pl.ds(c0, w)], dst.at[:, pl.ds(0, w)]
        cp.start(n, src, dst)

    def halves(f):
        return [functools.partial(f, pl.ds(half_rows * n, half_rows)) for n in range(2)]

    work = []

    def piece(cost, f, needs=(), gives=()):
        work.append((f, cost, needs, gives))

    staged = []

    def grad_item(m, c0, w, left, right):
        name = (m, c0)
        slot = len(staged) % 2
        used = staged[-2] if len(staged) > 1 else None
        staged.append(name)
        stage = ref.stage.at[slot]
        gives = [i for i, it in enumerate(items) if (it.m, it.g0) == name]

        def half(n):
            def run():
                if n == 0:
                    cp.wait(*[k for k in range(PAGES) if page[k] is left or page[k] is right], used)
                cols = slice(n * (width // 2), (n + 1) * (width // 2))
                got = dot_tn(left[:, cols], right[:, 0:w]).astype(bf16)
                stage[2 * n : 2 * n + 2, :, :, :, 0:w] = got.reshape((2,) + stage.shape[1:4] + (w,))
                if n == 1:
                    to = ref.partials[made.index(name)]
                    cp.start(name, stage.at[:, :, :, :, 0:w], to.at[:, :, :, :, 0:w])

            return run

        piece(1.15, half(0))
        piece(1.15, half(1), (), gives)

    load(0, ref.cotangent)
    load(2, ref.full[DOWN], *parts[0], by_row=True)
    load(4, ref.save_g2, *parts[0])
    load(3, ref.save_g1, *parts[0])
    load(1, ref.save_a2)
    cp.start(12, ref.save_inv_in, ref.inv_in)
    cp.start(13, ref.save_inv_mix, ref.inv_mix)
    cp.start(14, ref.save_inv_mid, ref.inv_mid)
    cp.start(15, ref.full_gain, ref.gain)

    def hidden_back(j, n):
        c0, w = parts[j]

        def run():
            cp.wait(0, 2, 3, 4)
            if n == 0 and j == 0:
                load(5, ref.full[FIRST], *parts[0])
                load(6, ref.full[SECOND], *parts[0])
            r = pl.ds(half_rows * n, half_rows)
            de = dot_nt(page[0][r, :], page[2][0:w, :])
            de = jnp.where(live(half_rows * n, half_rows), de, 0.0)
            page[7][r, 0:w] = (de * page[4][r, 0:w].astype(f32)).astype(bf16)
            page[8][r, 0:w] = (de * page[3][r, 0:w].astype(f32)).astype(bf16)
            if n == 1:
                if j + 1 < len(parts):
                    load(2, ref.full[DOWN], *parts[j + 1], by_row=True)
                    load(3, ref.save_g1, *parts[j + 1])
                    load(4, ref.save_g2, *parts[j + 1])
                else:
                    load(3, ref.save_o)
                    load(4, ref.save_gp)

        return run

    def mid_back(j, n):
        c0, w = parts[j]

        def run():
            cp.wait(5, 6)
            r = pl.ds(half_rows * n, half_rows)
            part = dot_nt(page[7][r, 0:w], page[5][:, 0:w]) + dot_nt(page[8][r, 0:w], page[6][:, 0:w])
            acc[r, :] = part if j == 0 else acc[r, :] + part
            if n == 1:
                if j + 1 < len(parts):
                    load(5, ref.full[FIRST], *parts[j + 1])
                    load(6, ref.full[SECOND], *parts[j + 1])
                else:
                    load(5, ref.save_h)
                    load(6, ref.full[OUT])
                    load(7, ref.save_q)
                    load(8, ref.save_k)

        return run

    for j, (c0, w) in enumerate(parts):
        for n in range(2):
            piece(1.5, hidden_back(j, n))
        grad_item(FIRST, c0, w, page[1], page[7])
        grad_item(SECOND, c0, w, page[1], page[8])
        for n in range(2):
            piece(2.2, mid_back(j, n))

    def middle_back():
        cp.wait(14, 1, 0)

        def tile(i):
            r = rows_of(i, size)
            up, n2 = acc[r, :], page[1][r, :].astype(f32)
            mean = jnp.mean(up * n2, axis=-1, keepdims=True)
            dy = page[0][r, :].astype(f32) + ref.inv_mid[r, 0:1] * (up - n2 * mean)
            acc[r, :] = dy
            page[2][r, :] = jnp.where(live(i * size, size), dy, 0.0).astype(bf16)

        tiles(rows // size, tile)
        load(1, ref.save_a1)
        load(0, ref.save_v)

    piece(1.5, middle_back)
    grad_item(OUT, 0, width, page[5], page[2])

    def branch_back():
        cp.wait(6)
        load(5, ref.save_pb)

        def tile(i):
            r = rows_of(i, half_rows)
            other[r, :] = dot_nt(page[2][r, :], page[6][...])

        tiles(2, tile)

    piece(2.2, branch_back)

    def mix_back(first, count):
        def run():
            cp.wait(15, 13, 3, 4)
            gains = ref.gain
            gain = jnp.concatenate(
                [
                    sum(gains[g, j, cc, 0:1, :].astype(f32) for j in (2 * half, 2 * half + 1) for cc in range(2))
                    for g in range(4)
                    for half in range(2)
                ],
                axis=1,
            )
            terms = ref.gain_terms
            if first == 0:
                terms[...] = jnp.zeros_like(terms)

            def tile(i):
                r = rows_of(i + first, size)
                inv = ref.inv_mix[r, 0:1]
                up, z = other[r, :], page[4][r, :].astype(f32)
                normed = page[3][r, :].astype(f32) * inv
                sig = jax.nn.sigmoid(z)
                upu = up * (z * sig)
                terms[...] += (upu * normed).reshape(size // 8, 8, width).sum(axis=0)
                page[4][r, :] = (up * normed * gain * sig * (1.0 + z * (1.0 - sig))).astype(bf16)
                dm = upu * gain
                mean = jnp.mean(dm * normed, axis=-1, keepdims=True)
                page[3][r, :] = (inv * (dm - normed * mean)).astype(bf16)

            tiles(count, tile)

        return run

    for n in range(2):
        piece(1.2, mix_back(n * (rows // size // 2), rows // size // 2))

    def gain_item():
        g, terms = bufs[GAIN_RING].g, ref.gain_terms
        for yx in range(4):
            for z in range(4):
                for c in range(2):
                    at = 128 * (2 * yx + z // 2)
                    g[0, yx, z, c] = terms[:, at : at + 128]

    piece(0.3, gain_item, (), [i for i, it in enumerate(items) if it.m == GAIN])
    grad_item(GATE, 0, width, page[1], page[4])

    def attention_back(n, count):
        def run():
            cp.wait(7, 8, 0, 5)
            q, k, v, pb, do, dq, dk, dv = [page[m] for m in (7, 8, 0, 5, 3, 3, 6, 2)]
            tiles(count, lambda b: attend_blocks_back(b + n * count, q, k, v, pb, do, dq, dk, dv))
            if n == rows // BLOCK // 4 - 1:
                load(5, ref.full[GATE])
                load(7, ref.full[QUERY])
                load(8, ref.full[KEY])
                load(0, ref.full[VALUE])

        return run

    for n in range(rows // BLOCK // 4):
        piece(3.5, attention_back(n, 2))
    grad_item(QUERY, 0, width, page[1], page[3])
    grad_item(KEY, 0, width, page[1], page[6])
    grad_item(VALUE, 0, width, page[1], page[2])

    def input_part(up, w, first, loads):
        def run():
            cp.wait(w)

            def tile(i):
                r = rows_of(i, half_rows)
                part = dot_nt(page[up][r, :], page[w][...])
                other[r, :] = part if first else other[r, :] + part

            tiles(2, tile)
            for n, src, at in loads:
                load(n, src, *parts[at], by_row=src is ref.full[DOWN])

        return run

    down, hidden = ref.full[DOWN], ref.save_e
    piece(2.2, input_part(4, 5, True, [(5, hidden, 0)]))
    piece(2.2, input_part(3, 7, False, [(7, down, 0), (3, hidden, 1)]))
    piece(2.2, input_part(6, 8, False, [(8, down, 1), (6, hidden, 2)]))
    piece(2.2, input_part(2, 0, False, [(0, down, 2)]))

    def input_back():
        cp.wait(12, 1)

        def tile(i):
            r = rows_of(i, size)
            up, n1 = other[r, :], page[1][r, :].astype(f32)
            mean = jnp.mean(up * n1, axis=-1, keepdims=True)
            page[4][r, :] = (acc[r, :] + ref.inv_in[r, 0:1] * (up - n1 * mean)).astype(bf16)

        tiles(rows // size, tile)
        cp.start(4, page[4], ref.input_grad)
        cp.start(16, ref.save_y, acc)

    piece(1.5, input_back)

    def output_part(j, e, w):
        def run():
            cp.wait(e, w)
            n = parts[j][1]

            def tile(i):
                r = rows_of(i, half_rows)
                part = dot_nn(page[e][r, 0:n], page[w][0:n, :])
                other[r, :] = part if j == 0 else other[r, :] + part

            tiles(2, tile)

        return run

    for j, (e, w) in enumerate(((5, 7), (3, 8), (6, 0))):
        piece(2.2, output_part(j, e, w))

    def output():
        cp.wait(16)

        def tile(i):
            r = rows_of(i, size)
            page[2][r, :] = (acc[r, :] + jnp.where(live(i * size, size), other[r, :], 0.0)).astype(bf16)

        tiles(rows // size, tile)
        cp.start(2, page[2], ref.layer_out)

    piece(1.0, output)

    given = [i for i, it in enumerate(items) if it.m == DOWN]
    Timeline(rs.timed_steps(), work, 2, given, rs.after()).run()
    rs.finish()
    cp.finish()


def backward(cotangent, lengths, full, got):
    rows, width = cotangent.shape
    flat = [w.reshape(-1, w.shape[-1]) for w in full]
    ff = flat[FIRST].shape[1]
    r_in, r_down = full[QUERY].shape[3], full[DOWN].shape[3]
    parts = column_parts(ff, width)
    made = [(m, c0, w) for c0, w in parts for m in (FIRST, SECOND)] + [(OUT, 0, width)]
    made += [(m, 0, width) for m in (GATE, QUERY, KEY, VALUE)]
    pieces = [(m, c0 + d, w, c0) for m, c0, n in made for d, w in column_parts(n, 512)]
    specs = [(DOWN, c0, w, 0, DOWN_RING) for c0, w in column_parts(width, 256)]
    specs += [p + (PLANE_RING if n % 5 == 2 else IN_RING,) for n, p in enumerate(pieces)]
    specs.insert(len(specs) - 8, (GAIN, 0, 128, 0, GAIN_RING))
    slots = (4, 8, 2, 1)
    items = scatter_plan(specs, slots)
    n = len(items)
    ins = dict(cotangent=cotangent, full=flat, full_gain=full[GAIN])
    ins |= {k: a for k, a in got.items() if k != DOWN_PARTIAL}
    ins |= dict(down_partial=got[DOWN_PARTIAL].reshape(full[DOWN].shape))
    shapes = [(r_down if m == DOWN else r_in, flat[m].shape[1]) for m in range(len(full))]
    shapes[GAIN] = (8, 128)
    page = jax.ShapeDtypeStruct((rows, width), bf16)
    outs = dict(layer_out=page, input_grad=page)
    partial = jax.ShapeDtypeStruct(full[QUERY].shape, bf16)
    outs |= dict(partials=[partial] * len(made))
    grads = dict(grads=[jax.ShapeDtypeStruct(s, f32) for s in shapes])
    inv = pltpu.VMEM((rows, 128), f32)
    scratch = dict(
        rings=[
            scatter_scratch(DOWN_RING, slots[DOWN_RING], r_down, 256, bf16),
            scatter_scratch(IN_RING, slots[IN_RING], r_in, 512, bf16),
            scatter_scratch(PLANE_RING, slots[PLANE_RING], r_in, 512, bf16),
            scatter_scratch(GAIN_RING, slots[GAIN_RING], 8, 128, f32),
        ],
        stage=pltpu.VMEM((2,) + full[QUERY].shape, bf16),
        page=pltpu.VMEM((PAGES, rows, width), bf16),
        wide=pltpu.VMEM((2, rows, width), f32),
        inv_in=inv, inv_mix=inv, inv_mid=inv,
        gain=pltpu.VMEM(full[GAIN].shape, bf16),
        gain_terms=pltpu.VMEM((8, width), f32),
        ssem=pltpu.SemaphoreType.DMA((n, 9)),
        rsem=pltpu.SemaphoreType.DMA((n, 9)),
        lsem=pltpu.SemaphoreType.DMA((n,)),
        csem=pltpu.SemaphoreType.DMA((BACKWARD_COPIES,)),
        free=pltpu.SemaphoreType.REGULAR((len(slots), 6)),
    )
    hbm, vmem = pl.BlockSpec(memory_space=pl.ANY), pl.BlockSpec(memory_space=pltpu.VMEM)
    leaves = jax.tree.leaves
    out = pl.pallas_call(
        functools.partial(backward_kernel, items, (dict(lengths=0), ins, outs, grads, scratch)),
        out_shape=leaves(outs) + leaves(grads),
        in_specs=[pl.BlockSpec(memory_space=pltpu.SMEM)] + [hbm] * len(leaves(ins)),
        out_specs=[hbm] * len(leaves(outs)) + [vmem] * len(leaves(grads)),
        scratch_shapes=leaves(scratch),
        compiler_params=pltpu.CompilerParams(
            collective_id=1, has_side_effects=True, vmem_limit_bytes=63 * 2**20
        ),
    )(lengths, *leaves(ins))
    return bind((outs, grads), out)


def finish_kernel(count, *refs):
    ins, terms, outs, gain = refs[:count], refs[count], refs[count + 1 : 2 * count + 1], refs[2 * count + 1]
    held, (sems,) = refs[2 * count + 2 : -1], refs[-1:]
    reads = [pltpu.make_async_copy(ins[k], held[k], sems.at[0, k]) for k in range(count)]
    writes = [pltpu.make_async_copy(held[k], outs[k], sems.at[1, k]) for k in range(count)]
    for m in reads:
        m.start()
    part = lax.rem(lax.axis_index(AXES[1]), 4)
    row = jnp.sum(terms[...], axis=0, keepdims=True)
    gain[...] = sum(jnp.where(part == k, row[:, 32 * k : 32 * (k + 1)], 0.0) for k in range(4))
    for r, w in zip(reads, writes):
        r.wait()
        w.start()
    for w in writes:
        w.wait()


def finish(arrays, terms):
    count = len(arrays)
    hbm, vmem = pl.BlockSpec(memory_space=pl.ANY), pl.BlockSpec(memory_space=pltpu.VMEM)
    return pl.pallas_call(
        functools.partial(finish_kernel, count),
        out_shape=[jax.ShapeDtypeStruct(a.shape, a.dtype) for a in arrays] + [jax.ShapeDtypeStruct((1, 32), f32)],
        in_specs=[hbm] * count + [vmem],
        out_specs=[hbm] * count + [vmem],
        scratch_shapes=[pltpu.VMEM(a.shape, a.dtype) for a in arrays] + [pltpu.SemaphoreType.DMA((2, count))],
        compiler_params=pltpu.CompilerParams(vmem_limit_bytes=62 * 2**20),
    )(*arrays, terms)


def slice_body(
    tokens, lengths, cotangent, w_query, w_key, w_value, w_gate, w_out, out_gain, w_first, w_second, w_down,
):
    rows, width = tokens.shape[0] * tokens.shape[1], tokens.shape[2]
    me = lax.axis_index(AXES[0]) * 8 + lax.axis_index(AXES[1])
    lane = lax.broadcasted_iota(jnp.int32, (16, 128), 1)
    gain_block = jnp.where(lax.div(lane, 32) == lax.rem(me, 4), jnp.tile(out_gain, 4)[None, :], 0)
    flat_cotangent = cotangent.reshape(rows, width)
    shards = (w_query, w_key, w_value, w_gate, gain_block, w_out, w_first, w_second, w_down)
    full, got = forward(tokens.reshape(rows, width), lengths, flat_cotangent, shards)
    back = backward(flat_cotangent, lengths, full, got)
    kept = [m for m in range(9) if m != GAIN]
    *whole, gain = finish([back.layer_out, back.input_grad] + [back.grads[m] for m in kept], back.grads[GAIN])
    grads = dict(zip(kept, whole[2:]))
    return (
        whole[0].reshape(tokens.shape), whole[1].reshape(tokens.shape),
        *[grads[m] for m in (QUERY, KEY, VALUE, GATE, OUT)], gain.reshape(32),
        *[grads[m] for m in (FIRST, SECOND, DOWN)],
    )


def solution(mesh):
    fits = (mesh.shape[AXES[0]], mesh.shape[AXES[1]]) == (4, 8)
    return jax.shard_map(
        slice_body if fits else general_body,
        mesh=mesh,
        in_specs=(
            P(AXES, None, None),
            P(AXES),
            P(AXES, None, None),
            P(AXES, None),
            P(AXES, None),
            P(AXES, None),
            P(AXES, None),
            P(AXES, None),
            P(AXES),
            P(AXES, None),
            P(AXES, None),
            P(AXES, None),
        ),
        out_specs=(
            P(AXES, None, None),
            P(AXES, None, None),
            P(AXES, None),
            P(AXES, None),
            P(AXES, None),
            P(AXES, None),
            P(AXES, None),
            P(AXES),
            P(AXES, None),
            P(AXES, None),
            P(AXES, None),
        ),
        check_vma=False,
    )
```

```python
import functools
from types import SimpleNamespace

import jax
import jax.numpy as jnp
from jax import lax
from jax.experimental import pallas as pl
from jax.experimental.pallas import tpu as pltpu
from jax.sharding import PartitionSpec as P

AXES = ("dp", "fsdp")
HEADS = 16
HEAD_DIM = 64
BLOCK = 64


epsilon = 1e-06
masked_score = -1e30


def normalize(values):
    inv_rms = lax.rsqrt(jnp.mean(values * values, axis=-1, keepdims=True) + epsilon)
    return (values * inv_rms, inv_rms)


def norm_back(normed, inv_rms, upstream):
    return inv_rms * (upstream - normed * jnp.mean(upstream * normed, axis=-1, keepdims=True))


def project(left_rows, right_rows):
    return jnp.dot(left_rows, right_rows, preferred_element_type=jnp.float32)


def project_back(upstream, weight):
    return lax.dot_general(
        upstream, weight, (((1,), (1,)), ((), ())), preferred_element_type=jnp.float32
    )


def weight_grad(inputs, upstream):
    return lax.dot_general(
        inputs, upstream, (((0,), (0,)), ((), ())), preferred_element_type=jnp.float32
    )


def split_heads(row_block):
    row_count = row_block.shape[0]
    return row_block.reshape(row_count // BLOCK, BLOCK, HEADS, HEAD_DIM)


def block_scores(query_blocks, key_blocks):
    scores = jnp.einsum(
        "bihd,bjhd->bhij", query_blocks, key_blocks, preferred_element_type=jnp.float32
    ) * HEAD_DIM ** (-0.5)
    causal = lax.broadcasted_iota(jnp.int32, (BLOCK, BLOCK), 0) >= lax.broadcasted_iota(
        jnp.int32, (BLOCK, BLOCK), 1
    )
    return jnp.where(causal, scores, masked_score)


def attend(query_rows, key_rows, value_rows):
    scores = block_scores(split_heads(query_rows), split_heads(key_rows))
    row_max = jnp.max(scores, axis=-1, keepdims=True)
    exp_scores = jnp.exp(scores - row_max)
    row_total = jnp.sum(exp_scores, axis=-1, keepdims=True)
    probs_low = (exp_scores / row_total).astype(jnp.bfloat16)
    head_mix = jnp.einsum(
        "bhij,bjhd->bihd", probs_low, split_heads(value_rows), preferred_element_type=jnp.float32
    )
    return (head_mix.reshape(query_rows.shape[0], -1), row_max + jnp.log(row_total))


def attend_back(query_rows, key_rows, value_rows, logsum, grad_mix):
    query_blocks = split_heads(query_rows)
    key_blocks = split_heads(key_rows)
    value_blocks = split_heads(value_rows)
    grad_blocks = split_heads(grad_mix)
    probs = jnp.exp(block_scores(query_blocks, key_blocks) - logsum)
    probs_low = probs.astype(jnp.bfloat16)
    grad_probs = jnp.einsum(
        "bihd,bjhd->bhij", grad_blocks, value_blocks, preferred_element_type=jnp.float32
    )
    grad_values = jnp.einsum(
        "bhij,bihd->bjhd", probs_low, grad_blocks, preferred_element_type=jnp.float32
    )
    grad_scores = (
        probs * (grad_probs - jnp.sum(grad_probs * probs, axis=-1, keepdims=True))
    ).astype(jnp.bfloat16)
    scale_factor = HEAD_DIM ** (-0.5)
    grad_queries = (
        jnp.einsum("bhij,bjhd->bihd", grad_scores, key_blocks, preferred_element_type=jnp.float32)
        * scale_factor
    )
    grad_keys = (
        jnp.einsum("bhij,bihd->bjhd", grad_scores, query_blocks, preferred_element_type=jnp.float32)
        * scale_factor
    )
    row_count = query_rows.shape[0]
    return (
        grad_queries.reshape(row_count, -1).astype(jnp.bfloat16),
        grad_keys.reshape(row_count, -1).astype(jnp.bfloat16),
        grad_values.reshape(row_count, -1).astype(jnp.bfloat16),
    )


def ffn_sums(second_in, hidden, grad_first_proj, grad_second_proj, grad_branch):
    both_proj = jnp.concatenate([grad_first_proj, grad_second_proj], axis=1)
    inner_shard = lax.psum_scatter(
        weight_grad(second_in, both_proj), AXES, scatter_dimension=0, tiled=True
    )
    down_shard = lax.psum_scatter(
        weight_grad(hidden, grad_branch), AXES, scatter_dimension=0, tiled=True
    )
    ff_width = grad_first_proj.shape[1]
    return (inner_shard[:, :ff_width], inner_shard[:, ff_width:], down_shard)


def general_body(
    tokens,
    lengths,
    cotangent,
    w_query,
    w_key,
    w_value,
    w_gate,
    w_out,
    out_gain,
    w_first,
    w_second,
    w_down,
):
    slot_count, slot_len, feature_width = tokens.shape
    row_count = slot_count * slot_len
    places = lax.broadcasted_iota(jnp.int32, (slot_count, slot_len), 1)
    live_rows = (places < lengths[:, None]).astype(jnp.float32).reshape(row_count, 1)
    attn_full = (
        lax.all_gather(w_query, AXES, axis=0, tiled=True),
        lax.all_gather(w_key, AXES, axis=0, tiled=True),
        lax.all_gather(w_value, AXES, axis=0, tiled=True),
        lax.all_gather(w_gate, AXES, axis=0, tiled=True),
        lax.all_gather(w_out, AXES, axis=0, tiled=True),
        lax.all_gather(out_gain, AXES, axis=0, tiled=True),
    )
    ffn_full = (
        lax.all_gather(w_first, AXES, axis=0, tiled=True),
        lax.all_gather(w_second, AXES, axis=0, tiled=True),
        lax.all_gather(w_down, AXES, axis=0, tiled=True),
    )
    query_full, key_full, value_full, gate_full, out_full, gain_full = attn_full
    first_full, second_full, down_full = ffn_full
    inputs = tokens.reshape(row_count, feature_width).astype(jnp.float32)
    normed_in, inv_in = normalize(inputs)
    first_in = normed_in.astype(jnp.bfloat16)
    query_rows = project(first_in, query_full).astype(jnp.bfloat16)
    key_rows = project(first_in, key_full).astype(jnp.bfloat16)
    value_rows = project(first_in, value_full).astype(jnp.bfloat16)
    gate_pre = project(first_in, gate_full)
    head_mix, logsum = attend(query_rows, key_rows, value_rows)
    normed_mix, inv_mix = normalize(head_mix)
    gain_rows = gain_full.astype(jnp.float32)
    gate_act = jax.nn.silu(gate_pre)
    scaled_mix = normed_mix * gain_rows
    branch_in = (scaled_mix * gate_act).astype(jnp.bfloat16)
    middle = inputs + live_rows * project(branch_in, out_full)
    normed_mid, inv_mid = normalize(middle)
    second_in = normed_mid.astype(jnp.bfloat16)
    first_proj = project(second_in, first_full)
    second_proj = project(second_in, second_full)
    hidden = (first_proj * second_proj).astype(jnp.bfloat16)
    final_rows = middle + live_rows * project(hidden, down_full)
    layer_out = final_rows.astype(jnp.bfloat16).reshape(tokens.shape)
    first_back, second_back, down_back = (
        lax.all_gather(w_first, AXES, axis=0, tiled=True),
        lax.all_gather(w_second, AXES, axis=0, tiled=True),
        lax.all_gather(w_down, AXES, axis=0, tiled=True),
    )
    query_back, key_back, value_back, gate_back, out_back, gain_back = (
        lax.all_gather(w_query, AXES, axis=0, tiled=True),
        lax.all_gather(w_key, AXES, axis=0, tiled=True),
        lax.all_gather(w_value, AXES, axis=0, tiled=True),
        lax.all_gather(w_gate, AXES, axis=0, tiled=True),
        lax.all_gather(w_out, AXES, axis=0, tiled=True),
        lax.all_gather(out_gain, AXES, axis=0, tiled=True),
    )
    gain_used = gain_back.astype(jnp.float32)
    grad_final = cotangent.reshape(row_count, feature_width).astype(jnp.float32)
    grad_branch = (live_rows * grad_final).astype(jnp.bfloat16)
    grad_hidden = project_back(grad_branch, down_back)
    grad_first_proj = (grad_hidden * second_proj).astype(jnp.bfloat16)
    grad_second_proj = (grad_hidden * first_proj).astype(jnp.bfloat16)
    grad_normed_mid = project_back(grad_first_proj, first_back) + project_back(
        grad_second_proj, second_back
    )
    grad_middle = grad_final + norm_back(normed_mid, inv_mid, grad_normed_mid)
    grad_attn_out = (live_rows * grad_middle).astype(jnp.bfloat16)
    grad_branch_in = project_back(grad_attn_out, out_back)
    gain_terms = grad_branch_in * gate_act * normed_mix
    sigmoid_gate = jax.nn.sigmoid(gate_pre)
    grad_gate_pre = (
        grad_branch_in * scaled_mix * sigmoid_gate * (1.0 + gate_pre * (1.0 - sigmoid_gate))
    ).astype(jnp.bfloat16)
    grad_scaled = grad_branch_in * gate_act * gain_used
    grad_mix = norm_back(normed_mix, inv_mix, grad_scaled).astype(jnp.bfloat16)
    grad_queries, grad_keys, grad_values = attend_back(
        query_rows, key_rows, value_rows, logsum, grad_mix
    )
    grad_normed_in = (
        project_back(grad_queries, query_back)
        + project_back(grad_keys, key_back)
        + project_back(grad_values, value_back)
        + project_back(grad_gate_pre, gate_back)
    )
    grad_inputs = grad_middle + norm_back(normed_in, inv_in, grad_normed_in)
    input_grad = grad_inputs.astype(jnp.bfloat16).reshape(tokens.shape)
    ffn_shards = ffn_sums(second_in, hidden, grad_first_proj, grad_second_proj, grad_branch)
    four_grads = jnp.concatenate([grad_queries, grad_keys, grad_values, grad_gate_pre], axis=1)
    from_input = weight_grad(first_in, four_grads)
    from_branch = weight_grad(branch_in, grad_attn_out)
    gain_part = jnp.sum(gain_terms, axis=0)[:, None]
    attn_shard = lax.psum_scatter(
        jnp.concatenate([from_input, from_branch, gain_part], axis=1),
        AXES,
        scatter_dimension=0,
        tiled=True,
    )
    shard_query = attn_shard[:, 0:feature_width]
    shard_key = attn_shard[:, feature_width : 2 * feature_width]
    shard_value = attn_shard[:, 2 * feature_width : 3 * feature_width]
    shard_gate = attn_shard[:, 3 * feature_width : 4 * feature_width]
    shard_out = attn_shard[:, 4 * feature_width : 5 * feature_width]
    shard_gain = attn_shard[:, 5 * feature_width]
    shard_first, shard_second, shard_down = ffn_shards
    return (
        layer_out,
        input_grad,
        shard_query,
        shard_key,
        shard_value,
        shard_gate,
        shard_out,
        shard_gain,
        shard_first,
        shard_second,
        shard_down,
    )


MESH = pl.DeviceIdType.MESH
f32 = jnp.float32
bf16 = jnp.bfloat16
QUERY, KEY, VALUE, GATE, GAIN, OUT, FIRST, SECOND, DOWN = range(9)
DOWN_PARTIAL = "down_partial"


def bind(trees, refs):
    fields = {}
    for tree in trees:
        leaves, form = jax.tree.flatten(tree)
        fields |= jax.tree.unflatten(form, refs[: len(leaves)])
        refs = refs[len(leaves) :]
    return SimpleNamespace(**fields)


class Place:
    def __init__(self):
        dp, fs = lax.axis_index(AXES[0]), lax.axis_index(AXES[1])
        z, c = lax.div(fs, 2), lax.rem(fs, 2)
        self.dp, self.fs, self.z, self.c = dp, fs, z, c
        self.nx = dp + 1 - 2 * lax.rem(dp, 2)
        self.ny = lax.rem(dp + 2, 4)
        self.dg = lax.rem(self.nx + 2, 4)
        self.zp = [lax.rem(z + k, 4) for k in (1, 2, 3)]
        self.sib = (dp, z * 2 + 1 - c)
        self.zdev = [(dp, zz * 2 + c) for zz in self.zp]
        self.xdev, self.ydev = (self.nx, fs), (self.ny, fs)
        self.peers = [self.sib, self.xdev, self.ydev] + self.zdev
        self.above, self.below, self.always = z < 3, z > 0, None
        self.end = (z == 0) | (z == 3)
        self.middle = (z == 1) | (z == 2)
        self.inward = z + 1 - 2 * lax.rem(z, 2)
        self.inward_dev = (dp, self.inward * 2 + c)

    def barrier(self):
        bar = pltpu.get_barrier_semaphore()
        for d in self.peers:
            pl.semaphore_signal(bar, inc=1, device_id=d, device_id_type=MESH)
        pl.semaphore_wait(bar, 6)


def where_true(cond, run):
    if cond is None:
        run()
    else:
        pl.when(cond)(run)


class Moves:
    def __init__(self, here, ssem, rsem):
        self.h, self.ssem, self.rsem, self.sends = here, ssem, rsem, {}
        self.along_z = ((0, here.above), (1, None), (2, here.below))
        self.from_z = ((0, here.below), (1, None), (2, here.above))

    def rc(self, i, k, src, dst, dev):
        return pltpu.make_async_remote_copy(
            src_ref=src, dst_ref=dst, send_sem=self.ssem.at[i, k], recv_sem=self.rsem.at[i, k],
            device_id=dev, device_id_type=MESH,
        )

    def go(self, i, *moves, cond=None):
        for m in moves:
            where_true(cond, m.start)
            self.sends.setdefault(i, []).append((cond, m))

    def release(self, i):
        for cond, m in self.sends.pop(i, ()):
            where_true(cond, m.wait_send)

    def finish(self):
        for i in list(self.sends):
            self.release(i)


class Gather(Moves):
    def __init__(self, here, items, shards, outs, ssem, rsem, lsem):
        super().__init__(here, ssem, rsem)
        self.items, self.shards, self.outs, self.lsem = items, shards, outs, lsem

    def block(self, i, yx, z, rows=slice(None)):
        m, c0, w, _ = self.items[i]
        return self.outs[m].at[yx, z, self.h.c, rows, pl.ds(c0, w)]

    def shard(self, i):
        m, c0, w, _ = self.items[i]
        return self.shards[m].at[:, pl.ds(c0, w)]

    def same(self, i, k, ref, dev):
        return self.rc(i, k, ref, ref, dev)

    def own(self, i):
        return pltpu.make_async_copy(self.shard(i), self.block(i, self.h.dp, self.h.z), self.lsem.at[i])

    def zmsg(self, i, k, planes):
        h = self.h
        if planes:
            return self.same(i, k, self.block(i, slice(None), h.z), h.zdev[k])
        return self.rc(i, k, self.shard(i), self.block(i, h.dp, h.z), h.zdev[k])

    def relay(self, i, planes):
        h = self.h
        return self.same(i, 11, self.block(i, slice(None) if planes else h.dp, h.zp[1]), h.inward_dev)

    def send_z(self, i, planes):
        for k, cond in self.along_z:
            self.go(i, self.zmsg(i, k, planes), cond=cond)

    def relay_z(self, i, planes):
        self.zmsg(i, 1, planes).wait_recv()
        self.go(i, self.relay(i, planes), cond=self.h.middle)

    def wait_z(self, i, planes):
        where_true(self.h.below, self.zmsg(i, 0, planes).wait_recv)
        where_true(self.h.above, self.zmsg(i, 2, planes).wait_recv)
        where_true(self.h.end, self.relay(i, planes).wait_recv)

    def col(self, i, k, yx, dev):
        return self.same(i, k, self.block(i, yx, slice(None)), dev)

    def half(self, i, k, yx, lo, dev):
        return self.same(i, k, self.block(i, yx, slice(lo, lo + 2)), dev)

    def part(self, i, k, yx, lo, dev):
        n = self.shards[self.items[i][0]].shape[0] // 2
        return self.same(i, k, self.block(i, yx, self.h.z, pl.ds(lo * n, n)), dev)

    def column0(self, i):
        self.own(i).start()
        self.send_z(i, False)

    def column1(self, i):
        self.relay_z(i, False)

    def column2(self, i):
        h = self.h
        self.own(i).wait()
        self.wait_z(i, False)
        self.go(i, self.col(i, 3, h.dp, h.xdev), self.col(i, 4, h.dp, h.ydev), self.col(i, 7, h.dp, h.sib))

    def column3(self, i):
        h = self.h
        self.col(i, 3, h.dp, h.xdev).wait_recv()
        self.go(i, self.half(i, 6, h.nx, 2, h.ydev), self.col(i, 8, h.nx, h.sib))
        self.col(i, 4, h.dp, h.ydev).wait_recv()
        self.go(i, self.half(i, 5, h.ny, 0, h.xdev), self.col(i, 9, h.ny, h.sib))

    def column4(self, i):
        h = self.h
        self.half(i, 5, h.ny, 0, h.xdev).wait_recv()
        self.half(i, 6, h.nx, 2, h.ydev).wait_recv()
        self.go(i, self.col(i, 10, h.dg, h.sib))

    def column5(self, i):
        h = self.h
        for k in (7, 8, 9, 10):
            self.col(i, k, h.dp, h.sib).wait_recv()

    def plane0(self, i):
        h = self.h
        self.own(i).start()
        self.go(
            i, self.rc(i, 3, self.shard(i), self.block(i, h.dp, h.z), h.xdev),
            self.rc(i, 4, self.shard(i), self.block(i, h.dp, h.z), h.ydev),
        )

    def plane1(self, i):
        h = self.h
        self.same(i, 3, self.block(i, h.nx, h.z), h.xdev).wait_recv()
        self.go(i, self.part(i, 6, h.nx, 1, h.ydev))
        self.same(i, 4, self.block(i, h.ny, h.z), h.ydev).wait_recv()
        self.go(i, self.part(i, 5, h.ny, 0, h.xdev))

    def plane2(self, i):
        h = self.h
        self.own(i).wait()
        self.part(i, 5, h.dg, 0, h.xdev).wait_recv()
        self.part(i, 6, h.dg, 1, h.ydev).wait_recv()
        self.send_z(i, True)
        self.go(i, self.same(i, 7, self.block(i, slice(None), h.z), h.sib))

    def plane3(self, i):
        self.relay_z(i, True)

    def plane4(self, i):
        h = self.h
        self.wait_z(i, True)
        self.go(i, *[self.same(i, 8 + k, self.block(i, slice(None), h.zp[k]), h.sib) for k in range(3)])

    def plane5(self, i):
        h = self.h
        for k in (7, 8, 9, 10):
            self.same(i, k, self.block(i, slice(None), h.z), h.sib).wait_recv()

    def timed_steps(self):
        steps = []
        for m, _, w, planes in self.items:
            u = w * self.shards[m].shape[0] / (32 * 1024)
            if planes:
                steps.append([
                    (self.plane0, 1, 1.5 * u, 0.2), (self.plane1, 1, 0.8 * u, 0.2), (self.plane2, 2, 10.0 * u, 0.2),
                    (self.plane3, 2, 8.0 * u, 0.1), (self.plane4, 3, 1.0 * u, 0.1), (self.plane5, None, 0.0, 0.1),
                ])
            else:
                steps.append([
                    (self.column0, 2, 2.5 * u, 0.2), (self.column1, 2, 2.0 * u, 0.1), (self.column2, 1, 5.8 * u, 0.2),
                    (self.column3, 1, 2.9 * u, 0.2), (self.column4, 3, 1.0 * u, 0.1), (self.column5, None, 0.0, 0.1),
                ])
        return steps


class Scatter(Moves):
    def __init__(self, here, items, bufs, before, ssem, rsem, lsem, free):
        super().__init__(here, ssem, rsem)
        self.items, self.bufs, self.before, self.lsem, self.free = items, bufs, before, lsem, free

    def views(self, i):
        it = self.items[i]
        return it, self.bufs[it.cls], it.slot, it.w

    def mine(self, i, yx, z, rows=slice(None)):
        it, b, s, w = self.views(i)
        if b.p is not None:
            return b.p.at[s, yx, z, rows, 0:w]
        return b.g.at[s, yx, z, self.h.c, rows, 0:w]

    def buf(self, i, ref, *at):
        return ref.at[(self.items[i].slot,) + at + (slice(None), slice(0, self.items[i].w))]

    def m_sib(self, i):
        it, b, s, w = self.views(i)
        if b.p is not None:
            src = it.src.at[:, :, 1 - self.h.c, :, pl.ds(it.s0, w)]
        else:
            src = b.g.at[s, :, :, 1 - self.h.c, :, 0:w]
        return self.rc(i, 0, src, self.buf(i, b.r1, slice(None), slice(None)), self.h.sib)

    def m_load(self, i):
        it, b, s, w = self.views(i)
        src = it.src.at[:, :, self.h.c, :, pl.ds(it.s0, w)]
        return pltpu.make_async_copy(src, self.buf(i, b.p, slice(None), slice(None)), self.lsem.at[i])

    def add(self, to, *terms):
        total = to[...].astype(f32)
        for t in terms:
            total = total + t[...].astype(f32)
        to[...] = total.astype(to.dtype)

    def step0(self, i):
        it, b, s, w = self.views(i)
        if it.before is not None:
            self.release(it.before)
            for k in range(6):
                pl.semaphore_wait(self.free.at[it.cls, k], 1)
        self.before(i)
        if b.p is not None:
            self.m_load(i).start()
        self.go(i, self.m_sib(i))

    def wait_halves(self, i):
        if self.bufs[self.items[i].cls].p is not None:
            self.m_load(i).wait()
        self.m_sib(i).wait_recv()

    def last(self, i):
        it = self.items[i]
        if it.reused:
            for k, d in enumerate(self.h.peers):
                pl.semaphore_signal(
                    self.free.at[it.cls, k if k < 3 else 8 - k], inc=1, device_id=d, device_id_type=MESH
                )

    def m_z(self, i, k, yx):
        b = self.bufs[self.items[i].cls]
        more = () if yx is None else (slice(None),)
        yx = self.h.dp if yx is None else yx
        return self.rc(i, 5 + k, self.mine(i, yx, self.h.zp[k]), self.buf(i, b.rz, k, *more), self.h.zdev[k])

    def m_relay(self, i, yx):
        b = self.bufs[self.items[i].cls]
        more = () if yx is None else (slice(None),)
        yx = self.h.dp if yx is None else yx
        return self.rc(i, 8, self.mine(i, yx, 3 - self.h.z), self.buf(i, b.rz, 3, *more), self.h.inward_dev)

    def send_z(self, i, yx=None):
        self.go(i, self.m_relay(i, yx), cond=self.h.end)
        self.go(i, self.m_z(i, 1, yx), cond=self.h.end)
        self.go(i, self.m_z(i, 0, yx), cond=self.h.above)
        self.go(i, self.m_z(i, 2, yx), cond=self.h.below)

    def relay_z(self, i, yx=None):
        def run():
            b = self.bufs[self.items[i].cls]
            self.m_relay(i, yx).wait_recv()
            if yx is None:
                self.add(self.mine(i, self.h.dp, self.h.zp[1]), self.buf(i, b.rz, 3))
            else:
                tiles(4, lambda j: self.add(self.mine(i, j, self.h.zp[1]), self.buf(i, b.rz, 3, j)))

        where_true(self.h.middle, run)
        self.go(i, self.m_z(i, 1, yx), cond=self.h.middle)

    def m_dx(self, i):
        b = self.bufs[self.items[i].cls]
        return self.rc(i, 1, self.mine(i, self.h.dg, slice(0, 2)), self.buf(i, b.rd, 0, slice(None)), self.h.xdev)

    def m_dy(self, i):
        b = self.bufs[self.items[i].cls]
        return self.rc(i, 2, self.mine(i, self.h.dg, slice(2, 4)), self.buf(i, b.rd, 1, slice(None)), self.h.ydev)

    def m_x(self, i):
        b = self.bufs[self.items[i].cls]
        return self.rc(i, 3, self.mine(i, self.h.nx, slice(None)), self.buf(i, b.rxy, 0, slice(None)), self.h.xdev)

    def m_y(self, i):
        b = self.bufs[self.items[i].cls]
        return self.rc(i, 4, self.mine(i, self.h.ny, slice(None)), self.buf(i, b.rxy, 1, slice(None)), self.h.ydev)

    def column1(self, i):
        r, dg = self.bufs[self.items[i].cls].r1, self.h.dg
        self.wait_halves(i)
        tiles(4, lambda j: self.add(self.mine(i, dg, j), self.buf(i, r, dg, j)))
        self.go(i, self.m_dx(i), self.m_dy(i))

        def near(j):
            a, q = lax.rem(dg + 1 + lax.div(j, 4), 4), lax.rem(j, 4)
            self.add(self.mine(i, a, q), self.buf(i, r, a, q))

        tiles(12, near)

    def column2(self, i):
        rd, nx, ny = self.bufs[self.items[i].cls].rd, self.h.nx, self.h.ny
        self.m_dx(i).wait_recv()
        tiles(2, lambda j: self.add(self.mine(i, ny, j), self.buf(i, rd, 0, j)))
        self.go(i, self.m_y(i))
        self.m_dy(i).wait_recv()
        tiles(2, lambda j: self.add(self.mine(i, nx, 2 + j), self.buf(i, rd, 1, j)))
        self.go(i, self.m_x(i))

    def column3(self, i):
        rxy, dp = self.bufs[self.items[i].cls].rxy, self.h.dp
        self.m_x(i).wait_recv()
        self.m_y(i).wait_recv()
        tiles(4, lambda j: self.add(self.mine(i, dp, j), self.buf(i, rxy, 0, j), self.buf(i, rxy, 1, j)))
        self.send_z(i)

    def column4(self, i):
        self.relay_z(i)

    def column5(self, i):
        it, b, s, w = self.views(i)
        cols = pl.ds(it.c0, w)
        self.m_z(i, 1, None).wait_recv()
        it.out[:, cols] = self.mine(i, self.h.dp, self.h.z)[...].astype(f32) + self.buf(i, b.rz, 1)[...].astype(f32)
        for k, cond in self.from_z:
            if cond is not None:

                def more(k=k):
                    self.m_z(i, k, None).wait_recv()
                    it.out[:, cols] += self.buf(i, b.rz, k)[...].astype(f32)

                pl.when(cond)(more)
        self.last(i)

    def plane1(self, i):
        r = self.bufs[self.items[i].cls].r1
        self.wait_halves(i)

        def both(j):
            a, q = lax.div(j, 4), lax.rem(j, 4)
            self.add(self.mine(i, a, q), self.buf(i, r, a, q))

        tiles(16, both)
        self.send_z(i, slice(None))

    def plane2(self, i):
        self.relay_z(i, slice(None))

    def p_d(self, i, n):
        b, h = self.bufs[self.items[i].cls], self.h
        rows = self.items[i].out.shape[0] // 2
        src = self.mine(i, h.dg, h.z, pl.ds(n * rows, rows))
        return self.rc(i, 1 + n, src, self.buf(i, b.rd, n), (h.xdev, h.ydev)[n])

    def p_xy(self, i, n):
        b, h = self.bufs[self.items[i].cls], self.h
        return self.rc(
            i, 3 + n, self.mine(i, (h.nx, h.ny)[n], h.z), self.buf(i, b.rxy, n), (h.xdev, h.ydev)[n]
        )

    def plane3(self, i):
        b, z = self.bufs[self.items[i].cls], self.h.z
        for k, cond in self.from_z:

            def more(k=k):
                self.m_z(i, k, slice(None)).wait_recv()
                tiles(4, lambda j: self.add(self.mine(i, j, z), self.buf(i, b.rz, k, j)))

            where_true(cond, more)
        self.go(i, self.p_d(i, 0), self.p_d(i, 1))

    def plane4(self, i):
        b, h = self.bufs[self.items[i].cls], self.h
        rows = self.items[i].out.shape[0] // 2
        for n, other in ((0, h.ny), (1, h.nx)):
            self.p_d(i, n).wait_recv()
            self.add(self.mine(i, other, h.z, pl.ds(n * rows, rows)), self.buf(i, b.rd, n))
            self.go(i, self.p_xy(i, 1 - n))

    def plane5(self, i):
        it, b, s, w = self.views(i)
        self.p_xy(i, 0).wait_recv()
        self.p_xy(i, 1).wait_recv()
        total = self.mine(i, self.h.dp, self.h.z)[...].astype(f32)
        it.out[:, pl.ds(it.c0, w)] = total + self.buf(i, b.rxy, 0)[...].astype(f32) + self.buf(i, b.rxy, 1)[...].astype(f32)
        self.last(i)

    def timed_steps(self):
        steps = []
        for i, it in enumerate(self.items):
            u = it.w * it.out.shape[0] / (32 * 1024)
            first = (self.step0, -i - 1, 1.5 * u, 0.2)
            if it.cls == PLANE_RING:
                steps.append([
                    first, (self.plane1, 2, 10.0 * u, 0.5 * u + 0.2), (self.plane2, 2, 8.0 * u, 0.1 * u + 0.1),
                    (self.plane3, 1, 0.8 * u, 0.2 * u + 0.2), (self.plane4, 1, 1.5 * u, 0.2),
                    (self.plane5, None, 0.0, 0.2),
                ])
            else:
                steps.append([
                    first, (self.column1, 1, 2.9 * u, 0.4 * u + 0.2), (self.column2, 1, 5.8 * u, 0.2 * u + 0.2),
                    (self.column3, 2, 2.5 * u, 0.2 * u + 0.2), (self.column4, 2, 2.0 * u, 0.1),
                    (self.column5, None, 0.0, 0.2),
                ])
        return steps

    def after(self):
        return [set() if it.before is None else {it.before} for it in self.items]


DOWN_RING, IN_RING, PLANE_RING, GAIN_RING = range(4)


def scatter_plan(specs, ring):
    items, by_class = [], {}
    for m, c0, w, g0, cls in specs:
        mine = by_class.setdefault(cls, [])
        it = SimpleNamespace(m=m, c0=c0, w=w, g0=g0, cls=cls, slot=len(mine) % ring[cls], before=None, reused=False)
        if len(mine) >= ring[cls]:
            it.before = mine[-ring[cls]]
            items[it.before].reused = True
        mine.append(len(items))
        items.append(it)
    return items


def scatter_scratch(cls, slots, r, w, dt):
    held, planes = cls == GAIN_RING, cls == PLANE_RING
    return dict(
        g=pltpu.VMEM((slots, 4, 4, 2, r, w) if held else (8, 128), dt),
        p=pltpu.VMEM((8, 128) if held else (slots, 4, 4, r, w), dt),
        r1=pltpu.VMEM((slots, 4, 4, r, w), dt),
        rd=pltpu.VMEM((slots, 2, r // 2, w) if planes else (slots, 2, 2, r, w), dt),
        rxy=pltpu.VMEM((slots, 2, r, w) if planes else (slots, 2, 4, r, w), dt),
        rz=pltpu.VMEM((slots, 4, 4, r, w) if planes else (slots, 4, r, w), dt),
    )


def ring_buffers(rings):
    bufs = [SimpleNamespace(**b) for b in rings]
    for cls, b in enumerate(bufs):
        if cls == GAIN_RING:
            b.p = None
        else:
            b.g = None
    return bufs


def column_parts(width, part):
    return [(c0, min(part, width - c0)) for c0 in range(0, width, part)]


def dot_nn(a, b):
    return jnp.dot(a, b, preferred_element_type=f32)


def dot_nt(a, b):
    return lax.dot_general(a, b, (((1,), (1,)), ((), ())), preferred_element_type=f32)


def dot_tn(a, b):
    return lax.dot_general(a, b, (((0,), (0,)), ((), ())), preferred_element_type=f32)


def tiles(count, body):
    def step(i, carry):
        body(i)
        return carry

    lax.fori_loop(0, count, step, 0)


def rows_of(i, size):
    return pl.ds(pl.multiple_of(i * size, size), size)


def rms_inv(values):
    return lax.rsqrt(jnp.mean(values * values, axis=-1, keepdims=True) + epsilon)


QUAD = 4 * HEAD_DIM


def quad_mask():
    shape = (QUAD, QUAD)
    row = lax.div(lax.broadcasted_iota(jnp.int32, shape, 0), HEAD_DIM)
    return row == lax.div(lax.broadcasted_iota(jnp.int32, shape, 1), HEAD_DIM)


def spread_heads(rows, mask):
    tall = jnp.concatenate([rows] * 4, axis=0)
    return jnp.where(mask, tall, jnp.zeros_like(tall))


def per_head(values, reduce, fill):
    halves = []
    for k in range(2):
        part = values[:, 128 * k : 128 * (k + 1)]
        low = lax.broadcasted_iota(jnp.int32, part.shape, 1) < HEAD_DIM
        first = reduce(jnp.where(low, part, fill), axis=-1, keepdims=True)
        second = reduce(jnp.where(low, fill, part), axis=-1, keepdims=True)
        halves.append(jnp.where(low, first, second))
    return jnp.concatenate(halves, axis=1)


def attend_blocks(b, q, k, v, probs, mix):
    mask = quad_mask()
    place = lax.broadcasted_iota(jnp.int32, (BLOCK, QUAD), 0)
    causal = place >= lax.rem(lax.broadcasted_iota(jnp.int32, (BLOCK, QUAD), 1), HEAD_DIM)
    at = [
        (rows_of(2 * b + n, BLOCK), slice(QUAD * g, QUAD * (g + 1))) for n in range(2) for g in range(HEADS // 4)
    ]
    scores = [
        jnp.where(causal, dot_nt(q[i], spread_heads(k[i], mask)) * HEAD_DIM ** (-0.5), masked_score) for i in at
    ]
    tops = [per_head(s, jnp.max, masked_score) for s in scores]
    terms = [jnp.exp(s - m) for s, m in zip(scores, tops)]
    totals = [per_head(t, jnp.sum, 0.0) for t in terms]
    lows = [(t / n).astype(bf16) for t, n in zip(terms, totals)]
    mixes = [dot_nn(p, spread_heads(v[i], mask)) for i, p in zip(at, lows)]
    for i, p, m in zip(at, lows, mixes):
        probs[i] = p
        mix[i] = m


def attend_blocks_back(b, q, k, v, probs, grad_mix, dq, dk, dv):
    mask = quad_mask()
    scale = HEAD_DIM ** (-0.5)
    low = lax.broadcasted_iota(jnp.int32, (BLOCK, 128), 1) < HEAD_DIM

    def own_head(wide):
        return jnp.concatenate(
            [
                jnp.where(low, wide[0:64, 0:128], wide[64:128, 0:128]),
                jnp.where(low, wide[128:192, 128:256], wide[192:256, 128:256]),
            ],
            axis=1,
        )

    at = [
        (rows_of(2 * b + n, BLOCK), slice(QUAD * g, QUAD * (g + 1))) for n in range(2) for g in range(HEADS // 4)
    ]
    dps = [dot_nt(grad_mix[i], spread_heads(v[i], mask)) for i in at]
    dvs = [own_head(dot_tn(probs[i], grad_mix[i])) for i in at]
    ps = [probs[i].astype(f32) for i in at]
    means = [per_head(dp * p, jnp.sum, 0.0) for dp, p in zip(dps, ps)]
    dss = [(p * (dp - m)).astype(bf16) for p, dp, m in zip(ps, dps, means)]
    dqs = [dot_nn(ds, spread_heads(k[i], mask)) * scale for i, ds in zip(at, dss)]
    dks = [own_head(dot_tn(ds, q[i])) * scale for i, ds in zip(at, dss)]
    for i, a, c, d in zip(at, dqs, dks, dvs):
        dq[i] = a.astype(bf16)
        dk[i] = c.astype(bf16)
        dv[i] = d.astype(bf16)


class Saves:
    def __init__(self, sems):
        self.sems, self.count, self.open = sems, 0, {}

    def start(self, name, src, dst):
        m = pltpu.make_async_copy(src, dst, self.sems.at[self.count])
        self.count += 1
        m.start()
        self.open[name] = m

    def wait(self, *names):
        for name in names:
            if name in self.open:
                self.open.pop(name).wait()

    def finish(self):
        self.wait(*list(self.open))


FORWARD_COPIES = 64
FORWARD_MODEL = SimpleNamespace(latency=(4.15, 0.96, 4.12), work=1.21, core=1.91, link=1.05, slack=0.0)
X, DF, A1, Q, K, V, PB, GP, H, O, Y, A2, GAINS, SLABS, INV = range(10, 25)


def forward_kernel(items, groups, trees, *refs):
    ref = bind(trees, refs)
    rows, width = ref.tokens.shape
    ff = ref.shards[FIRST].shape[1]
    parts = column_parts(ff, width)
    x, a1, q, k, v, pb, h, a2, e0, e1, e2, df = [ref.page.at[i] for i in range(12)]
    weight = [ref.weight.at[i] for i in range(4)]
    hidden, first, second = (e0, e1, e2), (q, k, v), (pb, h, x)
    wide = ref.wide
    gate_rows, mix_rows, mid_rows = [pl.ds(rows * i, rows) for i in range(3)]
    gp, o, y = wide.at[gate_rows], wide.at[mix_rows], wide.at[mid_rows]
    here = Place()
    here.barrier()
    ag = Gather(here, items, ref.shards, ref.full, ref.ssem, ref.rsem, ref.lsem)
    cp = Saves(ref.csem)
    size = 128
    lane = lax.broadcasted_iota(jnp.int32, (size, 128), 1)
    live_len = ref.lengths[0]

    def live(i, n):
        return lax.broadcasted_iota(jnp.int32, (n, 1), 0) + i * n < live_len

    def spread(values):
        return jnp.broadcast_to(values, (values.shape[0], 128))

    cp.start(X, ref.tokens, x)
    cp.start(DF, ref.cotangent, df)

    def norm_in():
        cp.wait(X)

        def tile(i):
            r = rows_of(i, size)
            t = x[r, :].astype(f32)
            inv = rms_inv(t)
            a1[r, :] = (t * inv).astype(bf16)
            ref.inv[r, :] = spread(inv)

        tiles(rows // size, tile)
        cp.start(A1, a1, ref.save_a1)

    def mask_df():
        cp.wait(DF)

        def tile(i):
            r = rows_of(i, size)
            df[r, :] = jnp.where(live(i, size), df[r, :], jnp.zeros((), bf16))

        tiles(rows // size, tile)

    def load(slot, m, c0=0, w=None):
        src = ref.full[m]
        w = src.shape[-1] if w is None else w
        cp.start(slot, src.at[:, :, :, :, pl.ds(c0, w)], weight[slot].at[:, :, :, :, pl.ds(0, w)])

    def matrix(slot, w=None):
        w = width if w is None else w
        return weight[slot][:, :, :, :, 0:w].reshape(width, w)

    def projected(slot, dst, name=None, kept=None):
        def run():
            cp.wait(slot)

            def tile(i):
                r = rows_of(i, rows // 2)
                dst[r, :] = dot_nn(a1[r, :], matrix(slot)).astype(dst.dtype)

            tiles(2, tile)
            if kept is not None:
                cp.start(name, dst, kept)

        return run

    def gate_low():
        def tile(i):
            r = rows_of(i, size)
            e0[r, :] = gp[r, :].astype(bf16)

        tiles(rows // size, tile)
        cp.start(GP, e0, ref.save_gp)

    def attention(n, count):
        def run():
            tiles(count, lambda b: attend_blocks(b + n * count, q, k, v, pb, o))

        return run

    def mixed():
        cp.start(PB, pb, ref.save_pb)
        cp.wait(GAINS)
        gains = ref.gain
        gain = jnp.concatenate(
            [
                sum(gains[g, j, cc, 0:1, :].astype(f32) for j in (2 * half, 2 * half + 1) for cc in range(2))
                for g in range(4)
                for half in range(2)
            ],
            axis=1,
        )

        def tile(i):
            r = rows_of(i, size)
            t, z = o[r, :], gp[r, :]
            inv = rms_inv(t)
            h[r, :] = (t * inv * gain * (z * jax.nn.sigmoid(z))).astype(bf16)
            e1[r, :] = t.astype(bf16)
            ref.inv[r, :] = jnp.where(lane == 1, inv, ref.inv[r, :])

        tiles(rows // size, tile)
        cp.start(H, h, ref.save_h)
        cp.start(O, e1, ref.save_o)

    def middle(slot):
        def run():
            cp.wait(slot)

            def tile(i):
                r = rows_of(i, rows // 2)
                y[r, :] = dot_nn(h[r, :], matrix(slot))

            tiles(2, tile)

            def norm(i):
                r = rows_of(i, size)
                t = x[r, :].astype(f32) + jnp.where(live(i, size), y[r, :], 0.0)
                inv = rms_inv(t)
                y[r, :] = t
                a2[r, :] = (t * inv).astype(bf16)
                ref.inv[r, :] = jnp.where(lane == 2, inv, ref.inv[r, :])

            tiles(rows // size, norm)
            cp.start(Y, y, ref.save_y)
            cp.start(A2, a2, ref.save_a2)

        return run

    def gated(j, s1, s2, half):
        c0, w = parts[j]
        saved = ((first[j], ref.save_g1), (second[j], ref.save_g2), (hidden[j], ref.save_e))

        def run():
            if half == 0:
                cp.wait(s1, s2, Q, K, V, PB, H, GP, O)
            r = pl.ds(half * (rows // 2), rows // 2)
            up = dot_nn(a2[r, :], matrix(s1, w))
            first[j][r, 0:w] = up.astype(bf16)
            other = dot_nn(a2[r, :], matrix(s2, w))
            second[j][r, 0:w] = other.astype(bf16)
            hidden[j][r, 0:w] = (up * other).astype(bf16)
            if half == 1:
                for n, (page, kept) in enumerate(saved):
                    cp.start((j, n), page.at[:, 0:w], kept.at[:, pl.ds(c0, w)])

        return run

    def down_grad(j, c0, w):
        def run():
            if j == 2:
                cp.wait(Y)
            wide[pl.ds(parts[j][0] + c0, w), :] = dot_tn(hidden[j][:, c0 : c0 + w], df[...])

        return run

    def down_slabs():
        slabs = ref.slabs
        n = slabs.shape[1]

        def tile(d):
            slabs[d] = wide[pl.ds(pl.multiple_of(d * n, 8), n), :].astype(bf16)

        tiles(slabs.shape[0], tile)
        cp.start(SLABS, slabs, ref.down_partial)

    work = []

    def piece(cost, f, needs=()):
        work.append((f, cost, needs, ()))

    piece(1.5, norm_in)
    piece(0.5, mask_df)
    piece(2.3, projected(0, q, Q, ref.save_q), (0,))
    piece(2.3, projected(1, k, K, ref.save_k), (1,))
    piece(2.3, projected(2, v, V, ref.save_v), (2,))
    for n in range(rows // BLOCK // 4):
        piece(2.0, attention(n, 2))
    piece(2.3, projected(3, gp), (3,))
    piece(0.5, gate_low)
    piece(1.5, mixed, (4,))
    piece(3.2, middle(0), (5,))
    slots = ((1, 2), (3, 0), (1, 2))
    for j, (s1, s2) in enumerate(slots):
        for half in range(2):
            piece(2.5, gated(j, s1, s2, half), (6 + 2 * j, 7 + 2 * j))
    for j, (c0, w) in enumerate(parts):
        step = 512 if w % 512 == 0 else w // 2
        for n in range(w // step):
            piece(1.2, down_grad(j, n * step, step))
    piece(1.0, down_slabs)
    loads = {0: (0, QUERY), 1: (1, KEY), 2: (2, VALUE), 3: (3, GATE), 5: (0, OUT)}
    for j, (s1, s2) in enumerate(slots):
        loads[6 + 2 * j] = (s1, FIRST) + parts[j]
        loads[7 + 2 * j] = (s2, SECOND) + parts[j]
    readers = [sum(g in p[2] for p in work) for g in range(len(items))]
    ready, waiting, held = set(), [], {}

    def try_loads():
        while waiting:
            i = waiting[0]
            slot = loads[i][0]
            if slot in held and readers[held[slot]]:
                return
            held[slot] = i
            load(*loads[i])
            ready.add(i)
            waiting.pop(0)

    left = [sum(g == n for g in groups) for n in range(len(items))]

    def ended(i):
        group = groups[i]
        left[group] -= 1
        if left[group]:
            return
        if group in loads:
            waiting.append(group)
            try_loads()
        elif group == 4:
            cp.start(GAINS, ref.full[GAIN], ref.gain)
            ready.add(group)

    def reading(f, needs):
        def run():
            f()
            for i in needs:
                readers[i] -= 1
            try_loads()

        return run

    work = [(reading(f, needs), cost, needs, gives) for f, cost, needs, gives in work]
    Timeline(
        ag.timed_steps(), work, 3, range(len(items)), FORWARD_MODEL,
        can_run=lambda needs: all(i in ready for i in needs), ended=ended,
    ).run()
    ag.finish()
    cp.start(INV, ref.inv, ref.save_inv)
    cp.finish()


def forward(tokens, lengths, cotangent, shards):
    rows, width = tokens.shape
    ff = shards[FIRST].shape[1]
    parts = column_parts(ff, width)
    whole = [(m, 0, width) for m in (QUERY, KEY, VALUE, GATE)] + [(GAIN, 0, shards[GAIN].shape[1]), (OUT, 0, width)]
    whole += [(m, c0, w) for c0, w in parts for m in (FIRST, SECOND)]
    pieces = [(m, c0 + d, w, g) for g, (m, c0, n) in enumerate(whole) for d, w in column_parts(n, 512)]
    pieces.sort(key=lambda p: (p[3] if p[3] < 6 else 6 + (p[3] - 6) // 2, p[1]))
    pieces += [(DOWN, c0, w, len(whole)) for c0, w in column_parts(width, 256)]
    items = [(m, c0, w, n % 6 == 0 and m not in (GAIN, DOWN)) for n, (m, c0, w, _) in enumerate(pieces)]
    groups = [p[3] for p in pieces]
    n = len(items)
    page, row = jax.ShapeDtypeStruct((rows, width), bf16), jax.ShapeDtypeStruct((rows, 128), f32)
    wide = jax.ShapeDtypeStruct((rows, ff), bf16)
    saves = dict(
        save_a1=page, save_q=page, save_k=page, save_v=page, save_pb=page, save_gp=page, save_o=page, save_h=page,
        save_a2=page, save_g1=wide, save_g2=wide, save_e=wide, save_y=jax.ShapeDtypeStruct((rows, width), f32),
        save_inv=row,
    )
    slab = (32,) + shards[DOWN].shape
    saves[DOWN_PARTIAL] = jax.ShapeDtypeStruct(slab, bf16)
    outs = dict(full=[jax.ShapeDtypeStruct((4, 4, 2) + s.shape, bf16) for s in shards])
    scratch = dict(
        page=pltpu.VMEM((12, rows, width), bf16),
        weight=pltpu.VMEM((4, 4, 4, 2, shards[QUERY].shape[0], width), bf16),
        wide=pltpu.VMEM((3 * rows, width), f32),
        slabs=pltpu.VMEM(slab, bf16),
        gain=pltpu.VMEM((4, 4, 2) + shards[GAIN].shape, bf16),
        inv=pltpu.VMEM((rows, 128), f32),
        ssem=pltpu.SemaphoreType.DMA((n, 12)),
        rsem=pltpu.SemaphoreType.DMA((n, 12)),
        lsem=pltpu.SemaphoreType.DMA((n,)),
        csem=pltpu.SemaphoreType.DMA((FORWARD_COPIES,)),
    )
    ins = dict(cotangent=cotangent, shards=list(shards), tokens=tokens)
    hbm, vmem = pl.BlockSpec(memory_space=pl.ANY), pl.BlockSpec(memory_space=pltpu.VMEM)
    leaves = jax.tree.leaves
    got = pl.pallas_call(
        functools.partial(forward_kernel, items, groups, (dict(lengths=0), ins, outs, saves, scratch)),
        out_shape=leaves(outs) + leaves(saves),
        in_specs=[pl.BlockSpec(memory_space=pltpu.SMEM), hbm] + [vmem] * len(shards) + [hbm],
        out_specs=[hbm] * len(leaves(outs) + leaves(saves)),
        scratch_shapes=leaves(scratch),
        compiler_params=pltpu.CompilerParams(
            collective_id=0, has_side_effects=True, vmem_limit_bytes=62 * 2**20
        ),
    )(lengths, *leaves(ins))
    full = got[: len(shards)]
    return full, jax.tree.unflatten(jax.tree.structure(saves), got[len(shards) :])


class Timeline:
    def __init__(self, steps, work, window, given, model, after=None, can_run=None, ended=None):
        self.steps, self.work, self.window, self.model = steps, list(work), window, model
        self.after = after or [set()] * len(steps)
        self.can_run = can_run or (lambda needs: all(n in self.done for n in needs))
        self.ended = ended or (lambda i: None)
        self.made = set(given)
        self.at = [0] * len(steps)
        self.when = [0.0] * len(steps)
        self.free = {}
        self.now = 3.0
        self.done = set()

    def next_steps(self):
        started = 0
        for i, at in enumerate(self.at):
            if at == 0:
                if i in self.made and started < self.window and self.after[i] <= self.done:
                    yield i
                return
            if at < len(self.steps[i]):
                started += at < 2
                yield i

    def step(self, i):
        run, link, link_us, core_us = self.steps[i][self.at[i]]
        self.now = max(self.now, self.when[i])
        run(i)
        self.now += core_us * self.model.core
        self.when[i] = self.now
        if link:
            sent = max(self.now, self.free.get(link, 0.0)) + link_us * self.model.link
            self.free[link] = sent
            self.when[i] = sent + self.model.latency[link - 1 if link in (1, 2) else 2]
        self.at[i] += 1
        if self.at[i] == len(self.steps[i]):
            self.done.add(i)
            self.ended(i)

    def run(self):
        while True:
            steps = list(self.next_steps())
            ready = [i for i in steps if self.when[i] <= self.now + self.model.slack]
            if ready:
                self.step(ready[0])
            elif self.work and self.can_run(self.work[0][2]):
                run, core_us, _, gives = self.work.pop(0)
                run()
                self.now += core_us * self.model.work
                for i in gives:
                    self.made.add(i)
                    self.when[i] = self.now + self.model.latency[2]
            elif steps:
                self.step(min(steps, key=lambda i: self.when[i]))
            else:
                return


BACKWARD_COPIES = 64
BACKWARD_MODEL = SimpleNamespace(latency=(4.71, 4.18, 2.15), work=1.15, core=1.38, link=1.14, slack=0.0)
PAGES = 9


def backward_kernel(items, trees, *refs):
    ref = bind(trees, refs)
    rows, width = ref.cotangent.shape
    ff = ref.full[FIRST].shape[1]
    parts = column_parts(ff, width)
    page = [ref.page.at[i] for i in range(PAGES)]
    acc, other = ref.wide.at[0], ref.wide.at[1]
    here = Place()
    here.barrier()
    bufs = ring_buffers(ref.rings)
    cp = Saves(ref.csem)
    made = sorted({(it.m, it.g0) for it in items if it.m not in (DOWN, GAIN)})
    items = [
        SimpleNamespace(
            **vars(it), out=ref.grads[it.m], s0=it.c0 - it.g0,
            src=ref.partials[made.index((it.m, it.g0))] if (it.m, it.g0) in made else ref.down_partial,
        )
        for it in items
    ]
    rs = Scatter(here, items, bufs, lambda i: cp.wait((items[i].m, items[i].g0)), ref.ssem, ref.rsem, ref.lsem, ref.free)
    size, half_rows = 128, rows // 2
    live_len = ref.lengths[0]

    def live(first, n):
        return lax.broadcasted_iota(jnp.int32, (n, 1), 0) + first < live_len

    def load(n, src, c0=None, w=None, by_row=False):
        dst = page[n]
        if c0 is not None:
            if by_row:
                src, dst = src.at[pl.ds(c0, w)], dst.at[pl.ds(0, w)]
            else:
                src, dst = src.at[:, pl.ds(c0, w)], dst.at[:, pl.ds(0, w)]
        cp.start(n, src, dst)

    def halves(f):
        return [functools.partial(f, pl.ds(half_rows * n, half_rows)) for n in range(2)]

    work = []

    def piece(cost, f, needs=(), gives=()):
        work.append((f, cost, needs, gives))

    staged = []

    def grad_item(m, c0, w, left, right):
        name = (m, c0)
        slot = len(staged) % 2
        used = staged[-2] if len(staged) > 1 else None
        staged.append(name)
        stage = ref.stage.at[slot]
        gives = [i for i, it in enumerate(items) if (it.m, it.g0) == name]

        def half(n):
            def run():
                if n == 0:
                    cp.wait(*[k for k in range(PAGES) if page[k] is left or page[k] is right], used)
                cols = slice(n * (width // 2), (n + 1) * (width // 2))
                got = dot_tn(left[:, cols], right[:, 0:w]).astype(bf16)
                stage[2 * n : 2 * n + 2, :, :, :, 0:w] = got.reshape((2,) + stage.shape[1:4] + (w,))
                if n == 1:
                    to = ref.partials[made.index(name)]
                    cp.start(name, stage.at[:, :, :, :, 0:w], to.at[:, :, :, :, 0:w])

            return run

        piece(1.15 * w / width, half(0))
        piece(1.15 * w / width, half(1), (), gives)

    load(0, ref.cotangent)
    load(2, ref.full[DOWN], *parts[0], by_row=True)
    load(4, ref.save_g2, *parts[0])
    load(3, ref.save_g1, *parts[0])
    load(1, ref.save_a2)
    cp.start(12, ref.save_inv, ref.inv)
    cp.start(15, ref.full_gain, ref.gain)

    def hidden_back(j, n):
        c0, w = parts[j]

        def run():
            cp.wait(0, 2, 3, 4)
            if n == 0 and j == 0:
                load(5, ref.full[FIRST], *parts[0])
                load(6, ref.full[SECOND], *parts[0])
            r = pl.ds(half_rows * n, half_rows)
            de = dot_nt(page[0][r, :], page[2][0:w, :])
            de = jnp.where(live(half_rows * n, half_rows), de, 0.0)
            page[7][r, 0:w] = (de * page[4][r, 0:w].astype(f32)).astype(bf16)
            page[8][r, 0:w] = (de * page[3][r, 0:w].astype(f32)).astype(bf16)
            if n == 1:
                if j + 1 < len(parts):
                    load(2, ref.full[DOWN], *parts[j + 1], by_row=True)
                    load(3, ref.save_g1, *parts[j + 1])
                    load(4, ref.save_g2, *parts[j + 1])
                else:
                    load(3, ref.save_o)
                    load(4, ref.save_gp)

        return run

    def mid_back(j, n):
        c0, w = parts[j]

        def run():
            cp.wait(5, 6)
            r = pl.ds(half_rows * n, half_rows)
            part = dot_nt(page[7][r, 0:w], page[5][:, 0:w]) + dot_nt(page[8][r, 0:w], page[6][:, 0:w])
            acc[r, :] = part if j == 0 else acc[r, :] + part
            if n == 1:
                if j + 1 < len(parts):
                    load(5, ref.full[FIRST], *parts[j + 1])
                    load(6, ref.full[SECOND], *parts[j + 1])
                else:
                    load(5, ref.save_h)
                    load(6, ref.full[OUT])
                    load(7, ref.save_q)
                    load(8, ref.save_k)

        return run

    for j, (c0, w) in enumerate(parts):
        for n in range(2):
            piece(1.5 * w / width, hidden_back(j, n))
        grad_item(FIRST, c0, w, page[1], page[7])
        grad_item(SECOND, c0, w, page[1], page[8])
        for n in range(2):
            piece(2.2 * w / width, mid_back(j, n))

    def middle_back():
        cp.wait(12, 1, 0)

        def tile(i):
            r = rows_of(i, size)
            up, n2 = acc[r, :], page[1][r, :].astype(f32)
            mean = jnp.mean(up * n2, axis=-1, keepdims=True)
            dy = page[0][r, :].astype(f32) + ref.inv[r, 2:3] * (up - n2 * mean)
            acc[r, :] = dy
            page[2][r, :] = jnp.where(live(i * size, size), dy, 0.0).astype(bf16)

        tiles(rows // size, tile)
        load(1, ref.save_a1)
        load(0, ref.save_v)

    piece(1.5, middle_back)
    grad_item(OUT, 0, width, page[5], page[2])

    def branch_back():
        cp.wait(6)
        load(5, ref.save_pb)

        def tile(i):
            r = rows_of(i, half_rows)
            other[r, :] = dot_nt(page[2][r, :], page[6][...])

        tiles(2, tile)

    piece(2.2, branch_back)

    def mix_back(first, count):
        def run():
            cp.wait(15, 3, 4)
            gains = ref.gain
            gain = jnp.concatenate(
                [
                    sum(gains[g, j, cc, 0:1, :].astype(f32) for j in (2 * half, 2 * half + 1) for cc in range(2))
                    for g in range(4)
                    for half in range(2)
                ],
                axis=1,
            )
            terms = ref.gain_terms
            if first == 0:
                terms[...] = jnp.zeros_like(terms)

            def tile(i):
                r = rows_of(i + first, size)
                inv = ref.inv[r, 1:2]
                up, z = other[r, :], page[4][r, :].astype(f32)
                normed = page[3][r, :].astype(f32) * inv
                sig = jax.nn.sigmoid(z)
                upu = up * (z * sig)
                terms[...] += (upu * normed).reshape(size // 8, 8, width).sum(axis=0)
                page[4][r, :] = (up * normed * gain * sig * (1.0 + z * (1.0 - sig))).astype(bf16)
                dm = upu * gain
                mean = jnp.mean(dm * normed, axis=-1, keepdims=True)
                page[3][r, :] = (inv * (dm - normed * mean)).astype(bf16)

            tiles(count, tile)

        return run

    for n in range(2):
        piece(1.2, mix_back(n * (rows // size // 2), rows // size // 2))

    def gain_item():
        g, terms = bufs[GAIN_RING].g, ref.gain_terms
        for yx in range(4):
            for z in range(4):
                for c in range(2):
                    at = 128 * (2 * yx + z // 2)
                    g[0, yx, z, c] = terms[:, at : at + 128]

    piece(0.3, gain_item, (), [i for i, it in enumerate(items) if it.m == GAIN])
    grad_item(GATE, 0, width, page[1], page[4])

    def attention_back(n, count):
        def run():
            cp.wait(7, 8, 0, 5)
            q, k, v, pb, do, dq, dk, dv = [page[m] for m in (7, 8, 0, 5, 3, 3, 6, 2)]
            tiles(count, lambda b: attend_blocks_back(b + n * count, q, k, v, pb, do, dq, dk, dv))
            if n == rows // BLOCK // 4 - 1:
                load(5, ref.full[GATE])
                load(7, ref.full[QUERY])
                load(8, ref.full[KEY])
                load(0, ref.full[VALUE])

        return run

    for n in range(rows // BLOCK // 4):
        piece(3.5, attention_back(n, 2))
    grad_item(QUERY, 0, width, page[1], page[3])
    grad_item(KEY, 0, width, page[1], page[6])
    grad_item(VALUE, 0, width, page[1], page[2])

    def input_part(up, w, first, loads):
        def run():
            cp.wait(w)

            def tile(i):
                r = rows_of(i, half_rows)
                part = dot_nt(page[up][r, :], page[w][...])
                other[r, :] = part if first else other[r, :] + part

            tiles(2, tile)
            for n, src, at in loads:
                load(n, src, *parts[at], by_row=src is ref.full[DOWN])

        return run

    down, hidden = ref.full[DOWN], ref.save_e
    piece(2.2, input_part(4, 5, True, [(5, hidden, 0)]))
    piece(2.2, input_part(3, 7, False, [(7, down, 0), (3, hidden, 1)]))
    piece(2.2, input_part(6, 8, False, [(8, down, 1), (6, hidden, 2)]))
    piece(2.2, input_part(2, 0, False, [(0, down, 2)]))

    def input_back():
        cp.wait(1)

        def tile(i):
            r = rows_of(i, size)
            up, n1 = other[r, :], page[1][r, :].astype(f32)
            mean = jnp.mean(up * n1, axis=-1, keepdims=True)
            page[4][r, :] = (acc[r, :] + ref.inv[r, 0:1] * (up - n1 * mean)).astype(bf16)

        tiles(rows // size, tile)
        cp.start(4, page[4], ref.input_grad)
        cp.start(16, ref.save_y, acc)

    piece(1.5, input_back)

    def output_part(j, e, w):
        def run():
            cp.wait(e, w)
            n = parts[j][1]

            def tile(i):
                r = rows_of(i, half_rows)
                part = dot_nn(page[e][r, 0:n], page[w][0:n, :])
                other[r, :] = part if j == 0 else other[r, :] + part

            tiles(2, tile)

        return run

    for j, (e, w) in enumerate(((5, 7), (3, 8), (6, 0))):
        piece(2.2, output_part(j, e, w))

    def output():
        cp.wait(16)

        def tile(i):
            r = rows_of(i, size)
            page[2][r, :] = (acc[r, :] + jnp.where(live(i * size, size), other[r, :], 0.0)).astype(bf16)

        tiles(rows // size, tile)
        cp.start(2, page[2], ref.layer_out)

    piece(1.0, output)

    given = [i for i, it in enumerate(items) if it.m == DOWN]
    Timeline(rs.timed_steps(), work, 6, given, BACKWARD_MODEL, rs.after()).run()
    rs.finish()
    cp.finish()


def backward(cotangent, lengths, full, got):
    rows, width = cotangent.shape
    flat = [w.reshape(-1, w.shape[-1]) for w in full]
    ff = flat[FIRST].shape[1]
    r_in, r_down = full[QUERY].shape[3], full[DOWN].shape[3]
    parts = column_parts(ff, width)
    made = [(m, c0, w) for c0, w in parts for m in (FIRST, SECOND)] + [(OUT, 0, width)]
    made += [(m, 0, width) for m in (GATE, QUERY, KEY, VALUE)]
    specs = [(DOWN, c0, w, 0, DOWN_RING) for c0, w in column_parts(width, 256)]
    for n, (m, c0, w) in enumerate(made):
        if m == GATE:
            specs.append((GAIN, 0, 128, 0, GAIN_RING))
        if n in (1, 3, 8):
            specs += [(m, c0, w // 2, c0, PLANE_RING), (m, c0 + w // 2, w // 2, c0, IN_RING)]
        else:
            specs.append((m, c0, w, c0, IN_RING))
    slots = (4, 5, 2, 1)
    items = scatter_plan(specs, slots)
    n = len(items)
    ins = dict(cotangent=cotangent, full=flat, full_gain=full[GAIN])
    ins |= {k: a for k, a in got.items() if k != DOWN_PARTIAL}
    ins |= dict(down_partial=got[DOWN_PARTIAL].reshape(full[DOWN].shape))
    shapes = [(r_down if m == DOWN else r_in, flat[m].shape[1]) for m in range(len(full))]
    shapes[GAIN] = (8, 128)
    page = jax.ShapeDtypeStruct((rows, width), bf16)
    outs = dict(layer_out=page, input_grad=page)
    partial = jax.ShapeDtypeStruct(full[QUERY].shape, bf16)
    outs |= dict(partials=[partial] * len(made))
    grads = dict(grads=[jax.ShapeDtypeStruct(s, f32) for s in shapes])
    scratch = dict(
        rings=[
            scatter_scratch(DOWN_RING, slots[DOWN_RING], r_down, 256, bf16),
            scatter_scratch(IN_RING, slots[IN_RING], r_in, width, bf16),
            scatter_scratch(PLANE_RING, slots[PLANE_RING], r_in, 512, bf16),
            scatter_scratch(GAIN_RING, slots[GAIN_RING], 8, 128, f32),
        ],
        stage=pltpu.VMEM((2,) + full[QUERY].shape, bf16),
        page=pltpu.VMEM((PAGES, rows, width), bf16),
        wide=pltpu.VMEM((2, rows, width), f32),
        inv=pltpu.VMEM((rows, 128), f32),
        gain=pltpu.VMEM(full[GAIN].shape, bf16),
        gain_terms=pltpu.VMEM((8, width), f32),
        ssem=pltpu.SemaphoreType.DMA((n, 9)),
        rsem=pltpu.SemaphoreType.DMA((n, 9)),
        lsem=pltpu.SemaphoreType.DMA((n,)),
        csem=pltpu.SemaphoreType.DMA((BACKWARD_COPIES,)),
        free=pltpu.SemaphoreType.REGULAR((len(slots), 6)),
    )
    hbm, vmem = pl.BlockSpec(memory_space=pl.ANY), pl.BlockSpec(memory_space=pltpu.VMEM)
    leaves = jax.tree.leaves
    out = pl.pallas_call(
        functools.partial(backward_kernel, items, (dict(lengths=0), ins, outs, grads, scratch)),
        out_shape=leaves(outs) + leaves(grads),
        in_specs=[pl.BlockSpec(memory_space=pltpu.SMEM)] + [hbm] * len(leaves(ins)),
        out_specs=[hbm] * len(leaves(outs)) + [vmem] * len(leaves(grads)),
        scratch_shapes=leaves(scratch),
        compiler_params=pltpu.CompilerParams(
            collective_id=1, has_side_effects=True, vmem_limit_bytes=63 * 2**20
        ),
    )(lengths, *leaves(ins))
    return bind((outs, grads), out)


def finish_kernel(count, *refs):
    ins, terms, outs, gain = refs[:count], refs[count], refs[count + 1 : 2 * count + 1], refs[2 * count + 1]
    held, (sems,) = refs[2 * count + 2 : -1], refs[-1:]
    reads = [pltpu.make_async_copy(ins[k], held[k], sems.at[0, k]) for k in range(count)]
    writes = [pltpu.make_async_copy(held[k], outs[k], sems.at[1, k]) for k in range(count)]
    for m in reads:
        m.start()
    part = lax.rem(lax.axis_index(AXES[1]), 4)
    row = jnp.sum(terms[...], axis=0, keepdims=True)
    gain[...] = sum(jnp.where(part == k, row[:, 32 * k : 32 * (k + 1)], 0.0) for k in range(4))
    for r, w in zip(reads, writes):
        r.wait()
        w.start()
    for w in writes:
        w.wait()


def finish(arrays, terms):
    count = len(arrays)
    hbm, vmem = pl.BlockSpec(memory_space=pl.ANY), pl.BlockSpec(memory_space=pltpu.VMEM)
    return pl.pallas_call(
        functools.partial(finish_kernel, count),
        out_shape=[jax.ShapeDtypeStruct(a.shape, a.dtype) for a in arrays] + [jax.ShapeDtypeStruct((1, 32), f32)],
        in_specs=[hbm] * count + [vmem],
        out_specs=[hbm] * count + [vmem],
        scratch_shapes=[pltpu.VMEM(a.shape, a.dtype) for a in arrays] + [pltpu.SemaphoreType.DMA((2, count))],
        compiler_params=pltpu.CompilerParams(vmem_limit_bytes=62 * 2**20),
    )(*arrays, terms)


def slice_body(
    tokens, lengths, cotangent, w_query, w_key, w_value, w_gate, w_out, out_gain, w_first, w_second, w_down,
):
    rows, width = tokens.shape[0] * tokens.shape[1], tokens.shape[2]
    me = lax.axis_index(AXES[0]) * 8 + lax.axis_index(AXES[1])
    lane = lax.broadcasted_iota(jnp.int32, (16, 128), 1)
    gain_block = jnp.where(lax.div(lane, 32) == lax.rem(me, 4), jnp.tile(out_gain, 4)[None, :], 0)
    flat_cotangent = cotangent.reshape(rows, width)
    shards = (w_query, w_key, w_value, w_gate, gain_block, w_out, w_first, w_second, w_down)
    full, got = forward(tokens.reshape(rows, width), lengths, flat_cotangent, shards)
    back = backward(flat_cotangent, lengths, full, got)
    kept = [m for m in range(9) if m != GAIN]
    *whole, gain = finish([back.layer_out, back.input_grad] + [back.grads[m] for m in kept], back.grads[GAIN])
    grads = dict(zip(kept, whole[2:]))
    return (
        whole[0].reshape(tokens.shape), whole[1].reshape(tokens.shape),
        *[grads[m] for m in (QUERY, KEY, VALUE, GATE, OUT)], gain.reshape(32),
        *[grads[m] for m in (FIRST, SECOND, DOWN)],
    )


def solution(mesh):
    fits = (mesh.shape[AXES[0]], mesh.shape[AXES[1]]) == (4, 8)
    return jax.shard_map(
        slice_body if fits else general_body,
        mesh=mesh,
        in_specs=(
            P(AXES, None, None),
            P(AXES),
            P(AXES, None, None),
            P(AXES, None),
            P(AXES, None),
            P(AXES, None),
            P(AXES, None),
            P(AXES, None),
            P(AXES),
            P(AXES, None),
            P(AXES, None),
            P(AXES, None),
        ),
        out_specs=(
            P(AXES, None, None),
            P(AXES, None, None),
            P(AXES, None),
            P(AXES, None),
            P(AXES, None),
            P(AXES, None),
            P(AXES, None),
            P(AXES),
            P(AXES, None),
            P(AXES, None),
            P(AXES, None),
        ),
        check_vma=False,
    )
```

```python
import functools
from types import SimpleNamespace

import jax
import jax.numpy as jnp
from jax import lax
from jax.experimental import pallas as pl
from jax.experimental.pallas import tpu as pltpu
from jax.sharding import PartitionSpec as P

AXES = ("dp", "fsdp")
HEADS = 16
HEAD_DIM = 64
BLOCK = 64


epsilon = 1e-06
masked_score = -1e30


def normalize(values):
    inv_rms = lax.rsqrt(jnp.mean(values * values, axis=-1, keepdims=True) + epsilon)
    return (values * inv_rms, inv_rms)


def norm_back(normed, inv_rms, upstream):
    return inv_rms * (upstream - normed * jnp.mean(upstream * normed, axis=-1, keepdims=True))


def project(left_rows, right_rows):
    return jnp.dot(left_rows, right_rows, preferred_element_type=jnp.float32)


def project_back(upstream, weight):
    return lax.dot_general(
        upstream, weight, (((1,), (1,)), ((), ())), preferred_element_type=jnp.float32
    )


def weight_grad(inputs, upstream):
    return lax.dot_general(
        inputs, upstream, (((0,), (0,)), ((), ())), preferred_element_type=jnp.float32
    )


def split_heads(row_block):
    row_count = row_block.shape[0]
    return row_block.reshape(row_count // BLOCK, BLOCK, HEADS, HEAD_DIM)


def block_scores(query_blocks, key_blocks):
    scores = jnp.einsum(
        "bihd,bjhd->bhij", query_blocks, key_blocks, preferred_element_type=jnp.float32
    ) * HEAD_DIM ** (-0.5)
    causal = lax.broadcasted_iota(jnp.int32, (BLOCK, BLOCK), 0) >= lax.broadcasted_iota(
        jnp.int32, (BLOCK, BLOCK), 1
    )
    return jnp.where(causal, scores, masked_score)


def attend(query_rows, key_rows, value_rows):
    scores = block_scores(split_heads(query_rows), split_heads(key_rows))
    row_max = jnp.max(scores, axis=-1, keepdims=True)
    exp_scores = jnp.exp(scores - row_max)
    row_total = jnp.sum(exp_scores, axis=-1, keepdims=True)
    probs_low = (exp_scores / row_total).astype(jnp.bfloat16)
    head_mix = jnp.einsum(
        "bhij,bjhd->bihd", probs_low, split_heads(value_rows), preferred_element_type=jnp.float32
    )
    return (head_mix.reshape(query_rows.shape[0], -1), row_max + jnp.log(row_total))


def attend_back(query_rows, key_rows, value_rows, logsum, grad_mix):
    query_blocks = split_heads(query_rows)
    key_blocks = split_heads(key_rows)
    value_blocks = split_heads(value_rows)
    grad_blocks = split_heads(grad_mix)
    probs = jnp.exp(block_scores(query_blocks, key_blocks) - logsum)
    probs_low = probs.astype(jnp.bfloat16)
    grad_probs = jnp.einsum(
        "bihd,bjhd->bhij", grad_blocks, value_blocks, preferred_element_type=jnp.float32
    )
    grad_values = jnp.einsum(
        "bhij,bihd->bjhd", probs_low, grad_blocks, preferred_element_type=jnp.float32
    )
    grad_scores = (
        probs * (grad_probs - jnp.sum(grad_probs * probs, axis=-1, keepdims=True))
    ).astype(jnp.bfloat16)
    scale_factor = HEAD_DIM ** (-0.5)
    grad_queries = (
        jnp.einsum("bhij,bjhd->bihd", grad_scores, key_blocks, preferred_element_type=jnp.float32)
        * scale_factor
    )
    grad_keys = (
        jnp.einsum("bhij,bihd->bjhd", grad_scores, query_blocks, preferred_element_type=jnp.float32)
        * scale_factor
    )
    row_count = query_rows.shape[0]
    return (
        grad_queries.reshape(row_count, -1).astype(jnp.bfloat16),
        grad_keys.reshape(row_count, -1).astype(jnp.bfloat16),
        grad_values.reshape(row_count, -1).astype(jnp.bfloat16),
    )


def ffn_sums(second_in, hidden, grad_first_proj, grad_second_proj, grad_branch):
    both_proj = jnp.concatenate([grad_first_proj, grad_second_proj], axis=1)
    inner_shard = lax.psum_scatter(
        weight_grad(second_in, both_proj), AXES, scatter_dimension=0, tiled=True
    )
    down_shard = lax.psum_scatter(
        weight_grad(hidden, grad_branch), AXES, scatter_dimension=0, tiled=True
    )
    ff_width = grad_first_proj.shape[1]
    return (inner_shard[:, :ff_width], inner_shard[:, ff_width:], down_shard)


def general_body(
    tokens,
    lengths,
    cotangent,
    w_query,
    w_key,
    w_value,
    w_gate,
    w_out,
    out_gain,
    w_first,
    w_second,
    w_down,
):
    slot_count, slot_len, feature_width = tokens.shape
    row_count = slot_count * slot_len
    places = lax.broadcasted_iota(jnp.int32, (slot_count, slot_len), 1)
    live_rows = (places < lengths[:, None]).astype(jnp.float32).reshape(row_count, 1)
    attn_full = (
        lax.all_gather(w_query, AXES, axis=0, tiled=True),
        lax.all_gather(w_key, AXES, axis=0, tiled=True),
        lax.all_gather(w_value, AXES, axis=0, tiled=True),
        lax.all_gather(w_gate, AXES, axis=0, tiled=True),
        lax.all_gather(w_out, AXES, axis=0, tiled=True),
        lax.all_gather(out_gain, AXES, axis=0, tiled=True),
    )
    ffn_full = (
        lax.all_gather(w_first, AXES, axis=0, tiled=True),
        lax.all_gather(w_second, AXES, axis=0, tiled=True),
        lax.all_gather(w_down, AXES, axis=0, tiled=True),
    )
    query_full, key_full, value_full, gate_full, out_full, gain_full = attn_full
    first_full, second_full, down_full = ffn_full
    inputs = tokens.reshape(row_count, feature_width).astype(jnp.float32)
    normed_in, inv_in = normalize(inputs)
    first_in = normed_in.astype(jnp.bfloat16)
    query_rows = project(first_in, query_full).astype(jnp.bfloat16)
    key_rows = project(first_in, key_full).astype(jnp.bfloat16)
    value_rows = project(first_in, value_full).astype(jnp.bfloat16)
    gate_pre = project(first_in, gate_full)
    head_mix, logsum = attend(query_rows, key_rows, value_rows)
    normed_mix, inv_mix = normalize(head_mix)
    gain_rows = gain_full.astype(jnp.float32)
    gate_act = jax.nn.silu(gate_pre)
    scaled_mix = normed_mix * gain_rows
    branch_in = (scaled_mix * gate_act).astype(jnp.bfloat16)
    middle = inputs + live_rows * project(branch_in, out_full)
    normed_mid, inv_mid = normalize(middle)
    second_in = normed_mid.astype(jnp.bfloat16)
    first_proj = project(second_in, first_full)
    second_proj = project(second_in, second_full)
    hidden = (first_proj * second_proj).astype(jnp.bfloat16)
    final_rows = middle + live_rows * project(hidden, down_full)
    layer_out = final_rows.astype(jnp.bfloat16).reshape(tokens.shape)
    first_back, second_back, down_back = (
        lax.all_gather(w_first, AXES, axis=0, tiled=True),
        lax.all_gather(w_second, AXES, axis=0, tiled=True),
        lax.all_gather(w_down, AXES, axis=0, tiled=True),
    )
    query_back, key_back, value_back, gate_back, out_back, gain_back = (
        lax.all_gather(w_query, AXES, axis=0, tiled=True),
        lax.all_gather(w_key, AXES, axis=0, tiled=True),
        lax.all_gather(w_value, AXES, axis=0, tiled=True),
        lax.all_gather(w_gate, AXES, axis=0, tiled=True),
        lax.all_gather(w_out, AXES, axis=0, tiled=True),
        lax.all_gather(out_gain, AXES, axis=0, tiled=True),
    )
    gain_used = gain_back.astype(jnp.float32)
    grad_final = cotangent.reshape(row_count, feature_width).astype(jnp.float32)
    grad_branch = (live_rows * grad_final).astype(jnp.bfloat16)
    grad_hidden = project_back(grad_branch, down_back)
    grad_first_proj = (grad_hidden * second_proj).astype(jnp.bfloat16)
    grad_second_proj = (grad_hidden * first_proj).astype(jnp.bfloat16)
    grad_normed_mid = project_back(grad_first_proj, first_back) + project_back(
        grad_second_proj, second_back
    )
    grad_middle = grad_final + norm_back(normed_mid, inv_mid, grad_normed_mid)
    grad_attn_out = (live_rows * grad_middle).astype(jnp.bfloat16)
    grad_branch_in = project_back(grad_attn_out, out_back)
    gain_terms = grad_branch_in * gate_act * normed_mix
    sigmoid_gate = jax.nn.sigmoid(gate_pre)
    grad_gate_pre = (
        grad_branch_in * scaled_mix * sigmoid_gate * (1.0 + gate_pre * (1.0 - sigmoid_gate))
    ).astype(jnp.bfloat16)
    grad_scaled = grad_branch_in * gate_act * gain_used
    grad_mix = norm_back(normed_mix, inv_mix, grad_scaled).astype(jnp.bfloat16)
    grad_queries, grad_keys, grad_values = attend_back(
        query_rows, key_rows, value_rows, logsum, grad_mix
    )
    grad_normed_in = (
        project_back(grad_queries, query_back)
        + project_back(grad_keys, key_back)
        + project_back(grad_values, value_back)
        + project_back(grad_gate_pre, gate_back)
    )
    grad_inputs = grad_middle + norm_back(normed_in, inv_in, grad_normed_in)
    input_grad = grad_inputs.astype(jnp.bfloat16).reshape(tokens.shape)
    ffn_shards = ffn_sums(second_in, hidden, grad_first_proj, grad_second_proj, grad_branch)
    four_grads = jnp.concatenate([grad_queries, grad_keys, grad_values, grad_gate_pre], axis=1)
    from_input = weight_grad(first_in, four_grads)
    from_branch = weight_grad(branch_in, grad_attn_out)
    gain_part = jnp.sum(gain_terms, axis=0)[:, None]
    attn_shard = lax.psum_scatter(
        jnp.concatenate([from_input, from_branch, gain_part], axis=1),
        AXES,
        scatter_dimension=0,
        tiled=True,
    )
    shard_query = attn_shard[:, 0:feature_width]
    shard_key = attn_shard[:, feature_width : 2 * feature_width]
    shard_value = attn_shard[:, 2 * feature_width : 3 * feature_width]
    shard_gate = attn_shard[:, 3 * feature_width : 4 * feature_width]
    shard_out = attn_shard[:, 4 * feature_width : 5 * feature_width]
    shard_gain = attn_shard[:, 5 * feature_width]
    shard_first, shard_second, shard_down = ffn_shards
    return (
        layer_out,
        input_grad,
        shard_query,
        shard_key,
        shard_value,
        shard_gate,
        shard_out,
        shard_gain,
        shard_first,
        shard_second,
        shard_down,
    )


MESH = pl.DeviceIdType.MESH
f32 = jnp.float32
bf16 = jnp.bfloat16
QUERY, KEY, VALUE, GATE, GAIN, OUT, FIRST, SECOND, DOWN = range(9)
DOWN_PARTIAL = "down_partial"


def bind(trees, refs):
    fields = {}
    for tree in trees:
        leaves, form = jax.tree.flatten(tree)
        fields |= jax.tree.unflatten(form, refs[: len(leaves)])
        refs = refs[len(leaves) :]
    return SimpleNamespace(**fields)


class Place:
    def __init__(self):
        dp, fs = lax.axis_index(AXES[0]), lax.axis_index(AXES[1])
        z, c = lax.div(fs, 2), lax.rem(fs, 2)
        self.dp, self.fs, self.z, self.c = dp, fs, z, c
        self.nx = dp + 1 - 2 * lax.rem(dp, 2)
        self.ny = lax.rem(dp + 2, 4)
        self.dg = lax.rem(self.nx + 2, 4)
        self.zp = [lax.rem(z + k, 4) for k in (1, 2, 3)]
        self.sib = (dp, z * 2 + 1 - c)
        self.zdev = [(dp, zz * 2 + c) for zz in self.zp]
        self.xdev, self.ydev = (self.nx, fs), (self.ny, fs)
        self.peers = [self.sib, self.xdev, self.ydev] + self.zdev
        self.above, self.below, self.always = z < 3, z > 0, None
        self.end = (z == 0) | (z == 3)
        self.middle = (z == 1) | (z == 2)
        self.inward = z + 1 - 2 * lax.rem(z, 2)
        self.inward_dev = (dp, self.inward * 2 + c)

    def barrier(self):
        bar = pltpu.get_barrier_semaphore()
        for d in self.peers:
            pl.semaphore_signal(bar, inc=1, device_id=d, device_id_type=MESH)
        pl.semaphore_wait(bar, 6)


def where_true(cond, run):
    if cond is None:
        run()
    else:
        pl.when(cond)(run)


class Moves:
    def __init__(self, here, ssem, rsem):
        self.h, self.ssem, self.rsem, self.sends = here, ssem, rsem, {}
        self.along_z = ((0, here.above), (1, None), (2, here.below))
        self.from_z = ((0, here.below), (1, None), (2, here.above))

    def rc(self, i, k, src, dst, dev):
        return pltpu.make_async_remote_copy(
            src_ref=src, dst_ref=dst, send_sem=self.ssem.at[i, k], recv_sem=self.rsem.at[i, k],
            device_id=dev, device_id_type=MESH,
        )

    def go(self, i, *moves, cond=None):
        for m in moves:
            where_true(cond, m.start)
            self.sends.setdefault(i, []).append((cond, m))

    def release(self, i):
        for cond, m in self.sends.pop(i, ()):
            where_true(cond, m.wait_send)

    def finish(self):
        for i in list(self.sends):
            self.release(i)


class Gather(Moves):
    def __init__(self, here, items, shards, outs, ssem, rsem, lsem):
        super().__init__(here, ssem, rsem)
        self.items, self.shards, self.outs, self.lsem = items, shards, outs, lsem

    def block(self, i, yx, z, rows=slice(None)):
        m, c0, w, _ = self.items[i]
        return self.outs[m].at[yx, z, self.h.c, rows, pl.ds(c0, w)]

    def shard(self, i):
        m, c0, w, _ = self.items[i]
        return self.shards[m].at[:, pl.ds(c0, w)]

    def same(self, i, k, ref, dev):
        return self.rc(i, k, ref, ref, dev)

    def own(self, i):
        return pltpu.make_async_copy(self.shard(i), self.block(i, self.h.dp, self.h.z), self.lsem.at[i])

    def zmsg(self, i, k, planes):
        h = self.h
        if planes:
            return self.same(i, k, self.block(i, slice(None), h.z), h.zdev[k])
        return self.rc(i, k, self.shard(i), self.block(i, h.dp, h.z), h.zdev[k])

    def relay(self, i, planes):
        h = self.h
        return self.same(i, 11, self.block(i, slice(None) if planes else h.dp, h.zp[1]), h.inward_dev)

    def send_z(self, i, planes):
        for k, cond in self.along_z:
            self.go(i, self.zmsg(i, k, planes), cond=cond)

    def relay_z(self, i, planes):
        self.zmsg(i, 1, planes).wait_recv()
        self.go(i, self.relay(i, planes), cond=self.h.middle)

    def wait_z(self, i, planes):
        where_true(self.h.below, self.zmsg(i, 0, planes).wait_recv)
        where_true(self.h.above, self.zmsg(i, 2, planes).wait_recv)
        where_true(self.h.end, self.relay(i, planes).wait_recv)

    def col(self, i, k, yx, dev):
        return self.same(i, k, self.block(i, yx, slice(None)), dev)

    def half(self, i, k, yx, lo, dev):
        return self.same(i, k, self.block(i, yx, slice(lo, lo + 2)), dev)

    def part(self, i, k, yx, lo, dev):
        n = self.shards[self.items[i][0]].shape[0] // 2
        return self.same(i, k, self.block(i, yx, self.h.z, pl.ds(lo * n, n)), dev)

    def column0(self, i):
        self.own(i).start()
        self.send_z(i, False)

    def column1(self, i):
        self.relay_z(i, False)

    def column2(self, i):
        h = self.h
        self.own(i).wait()
        self.wait_z(i, False)
        self.go(i, self.col(i, 3, h.dp, h.xdev), self.col(i, 4, h.dp, h.ydev), self.col(i, 7, h.dp, h.sib))

    def column3(self, i):
        h = self.h
        self.col(i, 3, h.dp, h.xdev).wait_recv()
        self.go(i, self.half(i, 6, h.nx, 2, h.ydev), self.col(i, 8, h.nx, h.sib))
        self.col(i, 4, h.dp, h.ydev).wait_recv()
        self.go(i, self.half(i, 5, h.ny, 0, h.xdev), self.col(i, 9, h.ny, h.sib))

    def column4(self, i):
        h = self.h
        self.half(i, 5, h.ny, 0, h.xdev).wait_recv()
        self.half(i, 6, h.nx, 2, h.ydev).wait_recv()
        self.go(i, self.col(i, 10, h.dg, h.sib))

    def column5(self, i):
        h = self.h
        for k in (7, 8, 9, 10):
            self.col(i, k, h.dp, h.sib).wait_recv()

    def plane0(self, i):
        h = self.h
        self.own(i).start()
        self.go(
            i, self.rc(i, 3, self.shard(i), self.block(i, h.dp, h.z), h.xdev),
            self.rc(i, 4, self.shard(i), self.block(i, h.dp, h.z), h.ydev),
        )

    def plane1(self, i):
        h = self.h
        self.same(i, 3, self.block(i, h.nx, h.z), h.xdev).wait_recv()
        self.go(i, self.part(i, 6, h.nx, 1, h.ydev))
        self.same(i, 4, self.block(i, h.ny, h.z), h.ydev).wait_recv()
        self.go(i, self.part(i, 5, h.ny, 0, h.xdev))

    def plane2(self, i):
        h = self.h
        self.own(i).wait()
        self.part(i, 5, h.dg, 0, h.xdev).wait_recv()
        self.part(i, 6, h.dg, 1, h.ydev).wait_recv()
        self.send_z(i, True)
        self.go(i, self.same(i, 7, self.block(i, slice(None), h.z), h.sib))

    def plane3(self, i):
        self.relay_z(i, True)

    def plane4(self, i):
        h = self.h
        self.wait_z(i, True)
        self.go(i, *[self.same(i, 8 + k, self.block(i, slice(None), h.zp[k]), h.sib) for k in range(3)])

    def plane5(self, i):
        h = self.h
        for k in (7, 8, 9, 10):
            self.same(i, k, self.block(i, slice(None), h.z), h.sib).wait_recv()

    def timed_steps(self):
        steps = []
        for m, _, w, planes in self.items:
            u = w * self.shards[m].shape[0] / (32 * 1024)
            if planes:
                steps.append([
                    (self.plane0, 1, 1.5 * u, 0.2), (self.plane1, 1, 0.8 * u, 0.2), (self.plane2, 2, 10.0 * u, 0.2),
                    (self.plane3, 2, 8.0 * u, 0.1), (self.plane4, 3, 1.0 * u, 0.1), (self.plane5, None, 0.0, 0.1),
                ])
            else:
                steps.append([
                    (self.column0, 2, 2.5 * u, 0.2), (self.column1, 2, 2.0 * u, 0.1), (self.column2, 1, 5.8 * u, 0.2),
                    (self.column3, 1, 2.9 * u, 0.2), (self.column4, 3, 1.0 * u, 0.1), (self.column5, None, 0.0, 0.1),
                ])
        return steps


class Scatter(Moves):
    def __init__(self, here, items, bufs, before, ssem, rsem, lsem, free):
        super().__init__(here, ssem, rsem)
        self.items, self.bufs, self.before, self.lsem, self.free = items, bufs, before, lsem, free

    def views(self, i):
        it = self.items[i]
        return it, self.bufs[it.cls], it.slot, it.w

    def mine(self, i, yx, z, rows=slice(None)):
        it, b, s, w = self.views(i)
        if b.p is not None:
            return b.p.at[s, yx, z, rows, 0:w]
        return b.g.at[s, yx, z, self.h.c, rows, 0:w]

    def buf(self, i, ref, *at):
        return ref.at[(self.items[i].slot,) + at + (slice(None), slice(0, self.items[i].w))]

    def m_sib(self, i):
        it, b, s, w = self.views(i)
        if b.p is not None:
            src = it.src.at[:, :, 1 - self.h.c, :, pl.ds(it.s0, w)]
        else:
            src = b.g.at[s, :, :, 1 - self.h.c, :, 0:w]
        return self.rc(i, 0, src, self.buf(i, b.r1, slice(None), slice(None)), self.h.sib)

    def m_load(self, i):
        it, b, s, w = self.views(i)
        src = it.src.at[:, :, self.h.c, :, pl.ds(it.s0, w)]
        return pltpu.make_async_copy(src, self.buf(i, b.p, slice(None), slice(None)), self.lsem.at[i])

    def add(self, to, *terms):
        total = to[...].astype(f32)
        for t in terms:
            total = total + t[...].astype(f32)
        to[...] = total.astype(to.dtype)

    def step0(self, i):
        it, b, s, w = self.views(i)
        if it.before is not None:
            self.release(it.before)
            for k in range(6):
                pl.semaphore_wait(self.free.at[it.cls, k], 1)
        self.before(i)
        if b.p is not None:
            self.m_load(i).start()
        self.go(i, self.m_sib(i))

    def wait_halves(self, i):
        if self.bufs[self.items[i].cls].p is not None:
            self.m_load(i).wait()
        self.m_sib(i).wait_recv()

    def last(self, i):
        it = self.items[i]
        if it.reused:
            for k, d in enumerate(self.h.peers):
                pl.semaphore_signal(
                    self.free.at[it.cls, k if k < 3 else 8 - k], inc=1, device_id=d, device_id_type=MESH
                )

    def m_z(self, i, k, yx):
        b = self.bufs[self.items[i].cls]
        more = () if yx is None else (slice(None),)
        yx = self.h.dp if yx is None else yx
        return self.rc(i, 5 + k, self.mine(i, yx, self.h.zp[k]), self.buf(i, b.rz, k, *more), self.h.zdev[k])

    def m_relay(self, i, yx):
        b = self.bufs[self.items[i].cls]
        more = () if yx is None else (slice(None),)
        yx = self.h.dp if yx is None else yx
        return self.rc(i, 8, self.mine(i, yx, 3 - self.h.z), self.buf(i, b.rz, 3, *more), self.h.inward_dev)

    def send_z(self, i, yx=None):
        self.go(i, self.m_relay(i, yx), cond=self.h.end)
        self.go(i, self.m_z(i, 1, yx), cond=self.h.end)
        self.go(i, self.m_z(i, 0, yx), cond=self.h.above)
        self.go(i, self.m_z(i, 2, yx), cond=self.h.below)

    def relay_z(self, i, yx=None):
        def run():
            b = self.bufs[self.items[i].cls]
            self.m_relay(i, yx).wait_recv()
            if yx is None:
                self.add(self.mine(i, self.h.dp, self.h.zp[1]), self.buf(i, b.rz, 3))
            else:
                tiles(4, lambda j: self.add(self.mine(i, j, self.h.zp[1]), self.buf(i, b.rz, 3, j)))

        where_true(self.h.middle, run)
        self.go(i, self.m_z(i, 1, yx), cond=self.h.middle)

    def m_dx(self, i):
        b = self.bufs[self.items[i].cls]
        return self.rc(i, 1, self.mine(i, self.h.dg, slice(0, 2)), self.buf(i, b.rd, 0, slice(None)), self.h.xdev)

    def m_dy(self, i):
        b = self.bufs[self.items[i].cls]
        return self.rc(i, 2, self.mine(i, self.h.dg, slice(2, 4)), self.buf(i, b.rd, 1, slice(None)), self.h.ydev)

    def m_x(self, i):
        b = self.bufs[self.items[i].cls]
        return self.rc(i, 3, self.mine(i, self.h.nx, slice(None)), self.buf(i, b.rxy, 0, slice(None)), self.h.xdev)

    def m_y(self, i):
        b = self.bufs[self.items[i].cls]
        return self.rc(i, 4, self.mine(i, self.h.ny, slice(None)), self.buf(i, b.rxy, 1, slice(None)), self.h.ydev)

    def column1(self, i):
        r, dg = self.bufs[self.items[i].cls].r1, self.h.dg
        self.wait_halves(i)
        tiles(4, lambda j: self.add(self.mine(i, dg, j), self.buf(i, r, dg, j)))
        self.go(i, self.m_dx(i), self.m_dy(i))

        def near(j):
            a, q = lax.rem(dg + 1 + lax.div(j, 4), 4), lax.rem(j, 4)
            self.add(self.mine(i, a, q), self.buf(i, r, a, q))

        tiles(12, near)

    def column2(self, i):
        rd, nx, ny = self.bufs[self.items[i].cls].rd, self.h.nx, self.h.ny
        self.m_dx(i).wait_recv()
        tiles(2, lambda j: self.add(self.mine(i, ny, j), self.buf(i, rd, 0, j)))
        self.go(i, self.m_y(i))
        self.m_dy(i).wait_recv()
        tiles(2, lambda j: self.add(self.mine(i, nx, 2 + j), self.buf(i, rd, 1, j)))
        self.go(i, self.m_x(i))

    def column3(self, i):
        rxy, dp = self.bufs[self.items[i].cls].rxy, self.h.dp
        self.m_x(i).wait_recv()
        self.m_y(i).wait_recv()
        tiles(4, lambda j: self.add(self.mine(i, dp, j), self.buf(i, rxy, 0, j), self.buf(i, rxy, 1, j)))
        self.send_z(i)

    def column4(self, i):
        self.relay_z(i)

    def column5(self, i):
        it, b, s, w = self.views(i)
        cols = pl.ds(it.c0, w)
        self.m_z(i, 1, None).wait_recv()
        it.out[:, cols] = self.mine(i, self.h.dp, self.h.z)[...].astype(f32) + self.buf(i, b.rz, 1)[...].astype(f32)
        for k, cond in self.from_z:
            if cond is not None:

                def more(k=k):
                    self.m_z(i, k, None).wait_recv()
                    it.out[:, cols] += self.buf(i, b.rz, k)[...].astype(f32)

                pl.when(cond)(more)
        self.last(i)

    def plane1(self, i):
        r = self.bufs[self.items[i].cls].r1
        self.wait_halves(i)

        def both(j):
            a, q = lax.div(j, 4), lax.rem(j, 4)
            self.add(self.mine(i, a, q), self.buf(i, r, a, q))

        tiles(16, both)
        self.send_z(i, slice(None))

    def plane2(self, i):
        self.relay_z(i, slice(None))

    def p_d(self, i, n):
        b, h = self.bufs[self.items[i].cls], self.h
        rows = self.items[i].out.shape[0] // 2
        src = self.mine(i, h.dg, h.z, pl.ds(n * rows, rows))
        return self.rc(i, 1 + n, src, self.buf(i, b.rd, n), (h.xdev, h.ydev)[n])

    def p_xy(self, i, n):
        b, h = self.bufs[self.items[i].cls], self.h
        return self.rc(
            i, 3 + n, self.mine(i, (h.nx, h.ny)[n], h.z), self.buf(i, b.rxy, n), (h.xdev, h.ydev)[n]
        )

    def plane3(self, i):
        b, z = self.bufs[self.items[i].cls], self.h.z
        for k, cond in self.from_z:

            def more(k=k):
                self.m_z(i, k, slice(None)).wait_recv()
                tiles(4, lambda j: self.add(self.mine(i, j, z), self.buf(i, b.rz, k, j)))

            where_true(cond, more)
        self.go(i, self.p_d(i, 0), self.p_d(i, 1))

    def plane4(self, i):
        b, h = self.bufs[self.items[i].cls], self.h
        rows = self.items[i].out.shape[0] // 2
        for n, other in ((0, h.ny), (1, h.nx)):
            self.p_d(i, n).wait_recv()
            self.add(self.mine(i, other, h.z, pl.ds(n * rows, rows)), self.buf(i, b.rd, n))
            self.go(i, self.p_xy(i, 1 - n))

    def plane5(self, i):
        it, b, s, w = self.views(i)
        self.p_xy(i, 0).wait_recv()
        self.p_xy(i, 1).wait_recv()
        total = self.mine(i, self.h.dp, self.h.z)[...].astype(f32)
        it.out[:, pl.ds(it.c0, w)] = total + self.buf(i, b.rxy, 0)[...].astype(f32) + self.buf(i, b.rxy, 1)[...].astype(f32)
        self.last(i)

    def timed_steps(self):
        steps = []
        for i, it in enumerate(self.items):
            u = it.w * it.out.shape[0] / (32 * 1024)
            first = (self.step0, -i - 1, 1.5 * u, 0.2)
            if it.cls == PLANE_RING:
                steps.append([
                    first, (self.plane1, 2, 10.0 * u, 0.5 * u + 0.2), (self.plane2, 2, 8.0 * u, 0.1 * u + 0.1),
                    (self.plane3, 1, 0.8 * u, 0.2 * u + 0.2), (self.plane4, 1, 1.5 * u, 0.2),
                    (self.plane5, None, 0.0, 0.2),
                ])
            else:
                steps.append([
                    first, (self.column1, 1, 2.9 * u, 0.4 * u + 0.2), (self.column2, 1, 5.8 * u, 0.2 * u + 0.2),
                    (self.column3, 2, 2.5 * u, 0.2 * u + 0.2), (self.column4, 2, 2.0 * u, 0.1),
                    (self.column5, None, 0.0, 0.2),
                ])
        return steps

    def after(self):
        return [set() if it.before is None else {it.before} for it in self.items]


DOWN_RING, IN_RING, PLANE_RING, GAIN_RING = range(4)


def scatter_plan(specs, ring):
    items, by_class = [], {}
    for m, c0, w, g0, cls in specs:
        mine = by_class.setdefault(cls, [])
        it = SimpleNamespace(m=m, c0=c0, w=w, g0=g0, cls=cls, slot=len(mine) % ring[cls], before=None, reused=False)
        if len(mine) >= ring[cls]:
            it.before = mine[-ring[cls]]
            items[it.before].reused = True
        mine.append(len(items))
        items.append(it)
    return items


def scatter_scratch(cls, slots, r, w, dt):
    held, planes = cls == GAIN_RING, cls == PLANE_RING
    return dict(
        g=pltpu.VMEM((slots, 4, 4, 2, r, w) if held else (8, 128), dt),
        p=pltpu.VMEM((8, 128) if held else (slots, 4, 4, r, w), dt),
        r1=pltpu.VMEM((slots, 4, 4, r, w), dt),
        rd=pltpu.VMEM((slots, 2, r // 2, w) if planes else (slots, 2, 2, r, w), dt),
        rxy=pltpu.VMEM((slots, 2, r, w) if planes else (slots, 2, 4, r, w), dt),
        rz=pltpu.VMEM((slots, 4, 4, r, w) if planes else (slots, 4, r, w), dt),
    )


def ring_buffers(rings):
    bufs = [SimpleNamespace(**b) for b in rings]
    for cls, b in enumerate(bufs):
        if cls == GAIN_RING:
            b.p = None
        else:
            b.g = None
    return bufs


def column_parts(width, part):
    return [(c0, min(part, width - c0)) for c0 in range(0, width, part)]


def dot_nn(a, b):
    return jnp.dot(a, b, preferred_element_type=f32)


def dot_nt(a, b):
    return lax.dot_general(a, b, (((1,), (1,)), ((), ())), preferred_element_type=f32)


def dot_tn(a, b):
    return lax.dot_general(a, b, (((0,), (0,)), ((), ())), preferred_element_type=f32)


def tiles(count, body):
    def step(i, carry):
        body(i)
        return carry

    lax.fori_loop(0, count, step, 0)


def rows_of(i, size):
    return pl.ds(pl.multiple_of(i * size, size), size)


def rms_inv(values):
    return lax.rsqrt(jnp.mean(values * values, axis=-1, keepdims=True) + epsilon)


QUAD = 4 * HEAD_DIM


def quad_mask():
    shape = (QUAD, QUAD)
    row = lax.div(lax.broadcasted_iota(jnp.int32, shape, 0), HEAD_DIM)
    return row == lax.div(lax.broadcasted_iota(jnp.int32, shape, 1), HEAD_DIM)


def spread_heads(rows, mask):
    tall = jnp.concatenate([rows] * 4, axis=0)
    return jnp.where(mask, tall, jnp.zeros_like(tall))


def per_head(values, reduce, fill):
    halves = []
    for k in range(2):
        part = values[:, 128 * k : 128 * (k + 1)]
        low = lax.broadcasted_iota(jnp.int32, part.shape, 1) < HEAD_DIM
        first = reduce(jnp.where(low, part, fill), axis=-1, keepdims=True)
        second = reduce(jnp.where(low, fill, part), axis=-1, keepdims=True)
        halves.append(jnp.where(low, first, second))
    return jnp.concatenate(halves, axis=1)


def attend_blocks(b, q, k, v, probs, mix):
    mask = quad_mask()
    place = lax.broadcasted_iota(jnp.int32, (BLOCK, QUAD), 0)
    causal = place >= lax.rem(lax.broadcasted_iota(jnp.int32, (BLOCK, QUAD), 1), HEAD_DIM)
    at = [
        (rows_of(2 * b + n, BLOCK), slice(QUAD * g, QUAD * (g + 1))) for n in range(2) for g in range(HEADS // 4)
    ]
    scores = [
        jnp.where(causal, dot_nt(q[i], spread_heads(k[i], mask)) * HEAD_DIM ** (-0.5), masked_score) for i in at
    ]
    tops = [per_head(s, jnp.max, masked_score) for s in scores]
    terms = [jnp.exp(s - m) for s, m in zip(scores, tops)]
    totals = [per_head(t, jnp.sum, 0.0) for t in terms]
    lows = [(t / n).astype(bf16) for t, n in zip(terms, totals)]
    mixes = [dot_nn(p, spread_heads(v[i], mask)) for i, p in zip(at, lows)]
    for i, p, m in zip(at, lows, mixes):
        probs[i] = p
        mix[i] = m


def attend_blocks_back(b, q, k, v, probs, grad_mix, dq, dk, dv):
    mask = quad_mask()
    scale = HEAD_DIM ** (-0.5)
    low = lax.broadcasted_iota(jnp.int32, (BLOCK, 128), 1) < HEAD_DIM

    def own_head(wide):
        return jnp.concatenate(
            [
                jnp.where(low, wide[0:64, 0:128], wide[64:128, 0:128]),
                jnp.where(low, wide[128:192, 128:256], wide[192:256, 128:256]),
            ],
            axis=1,
        )

    at = [
        (rows_of(2 * b + n, BLOCK), slice(QUAD * g, QUAD * (g + 1))) for n in range(2) for g in range(HEADS // 4)
    ]
    dps = [dot_nt(grad_mix[i], spread_heads(v[i], mask)) for i in at]
    dvs = [own_head(dot_tn(probs[i], grad_mix[i])) for i in at]
    ps = [probs[i].astype(f32) for i in at]
    means = [per_head(dp * p, jnp.sum, 0.0) for dp, p in zip(dps, ps)]
    dss = [(p * (dp - m)).astype(bf16) for p, dp, m in zip(ps, dps, means)]
    dqs = [dot_nn(ds, spread_heads(k[i], mask)) * scale for i, ds in zip(at, dss)]
    dks = [own_head(dot_tn(ds, q[i])) * scale for i, ds in zip(at, dss)]
    for i, a, c, d in zip(at, dqs, dks, dvs):
        dq[i] = a.astype(bf16)
        dk[i] = c.astype(bf16)
        dv[i] = d.astype(bf16)


class Saves:
    def __init__(self, sems):
        self.sems, self.count, self.open = sems, 0, {}

    def start(self, name, src, dst):
        m = pltpu.make_async_copy(src, dst, self.sems.at[self.count])
        self.count += 1
        m.start()
        self.open[name] = m

    def wait(self, *names):
        for name in names:
            if name in self.open:
                self.open.pop(name).wait()

    def finish(self):
        self.wait(*list(self.open))


FORWARD_COPIES = 64
FORWARD_MODEL = SimpleNamespace(latency=(4.15, 0.96, 4.12), work=1.21, core=1.91, link=1.05, slack=0.0)
X, DF, A1, Q, K, V, PB, GP, H, O, Y, A2, GAINS, SLABS, INV = range(10, 25)


def forward_kernel(items, groups, trees, *refs):
    ref = bind(trees, refs)
    rows, width = ref.tokens.shape
    ff = ref.shards[FIRST].shape[1]
    parts = column_parts(ff, width)
    x, a1, q, k, v, pb, h, a2, e0, e1, e2, df = [ref.page.at[i] for i in range(12)]
    weight = [ref.weight.at[i] for i in range(4)]
    hidden, first, second = (e0, e1, e2), (q, k, v), (pb, h, x)
    wide = ref.wide
    gate_rows, mix_rows, mid_rows = [pl.ds(rows * i, rows) for i in range(3)]
    gp, o, y = wide.at[gate_rows], wide.at[mix_rows], wide.at[mid_rows]
    here = Place()
    ag = Gather(here, items, ref.shards, ref.full, ref.ssem, ref.rsem, ref.lsem)
    cp = Saves(ref.csem)
    size = 128
    lane = lax.broadcasted_iota(jnp.int32, (size, 128), 1)
    live_len = ref.lengths[0]

    def live(i, n):
        return lax.broadcasted_iota(jnp.int32, (n, 1), 0) + i * n < live_len

    def spread(values):
        return jnp.broadcast_to(values, (values.shape[0], 128))

    cp.start(X, ref.tokens, x)
    cp.start(DF, ref.cotangent, df)
    here.barrier()

    def norm_in():
        cp.wait(X)

        def tile(i):
            r = rows_of(i, size)
            t = x[r, :].astype(f32)
            inv = rms_inv(t)
            a1[r, :] = (t * inv).astype(bf16)
            ref.inv[r, :] = spread(inv)

        tiles(rows // size, tile)
        cp.start(A1, a1, ref.save_a1)

    def mask_df():
        cp.wait(DF)

        def tile(i):
            r = rows_of(i, size)
            df[r, :] = jnp.where(live(i, size), df[r, :], jnp.zeros((), bf16))

        tiles(rows // size, tile)

    def load(slot, m, c0=0, w=None):
        src = ref.full[m]
        w = src.shape[-1] if w is None else w
        cp.start(slot, src.at[:, :, :, :, pl.ds(c0, w)], weight[slot].at[:, :, :, :, pl.ds(0, w)])

    def matrix(slot, w=None):
        w = width if w is None else w
        return weight[slot][:, :, :, :, 0:w].reshape(width, w)

    half_rows = rows // 2

    def projected(half, slot, dst, name=None, kept=None):
        def run():
            cp.wait(slot)
            r = pl.ds(half * half_rows, half_rows)
            dst[r, :] = dot_nn(a1[r, :], matrix(slot)).astype(dst.dtype)
            if kept is not None and half:
                cp.start(name, dst, kept)

        return run

    def gate_low():
        def tile(i):
            r = rows_of(i, size)
            e0[r, :] = gp[r, :].astype(bf16)

        tiles(rows // size, tile)
        cp.start(GP, e0, ref.save_gp)

    def attention(n, count):
        def run():
            tiles(count, lambda b: attend_blocks(b + n * count, q, k, v, pb, o))

        return run

    def mixed():
        cp.start(PB, pb, ref.save_pb)
        cp.wait(GAINS)
        gains = ref.gain
        gain = jnp.concatenate(
            [
                sum(gains[g, j, cc, 0:1, :].astype(f32) for j in (2 * half, 2 * half + 1) for cc in range(2))
                for g in range(4)
                for half in range(2)
            ],
            axis=1,
        )

        def tile(i):
            r = rows_of(i, size)
            t, z = o[r, :], gp[r, :]
            inv = rms_inv(t)
            h[r, :] = (t * inv * gain * (z * jax.nn.sigmoid(z))).astype(bf16)
            e1[r, :] = t.astype(bf16)
            ref.inv[r, :] = jnp.where(lane == 1, inv, ref.inv[r, :])

        tiles(rows // size, tile)
        cp.start(H, h, ref.save_h)
        cp.start(O, e1, ref.save_o)

    def middle(half, slot):
        def run():
            cp.wait(slot)
            r = pl.ds(half * half_rows, half_rows)
            y[r, :] = dot_nn(h[r, :], matrix(slot))

        return run

    def norm_middle():
        def tile(i):
            r = rows_of(i, size)
            t = x[r, :].astype(f32) + jnp.where(live(i, size), y[r, :], 0.0)
            inv = rms_inv(t)
            y[r, :] = t
            a2[r, :] = (t * inv).astype(bf16)
            ref.inv[r, :] = jnp.where(lane == 2, inv, ref.inv[r, :])

        tiles(rows // size, tile)
        cp.start(Y, y, ref.save_y)
        cp.start(A2, a2, ref.save_a2)

    def gated(j, s1, s2, part, count):
        c0, w = parts[j]
        saved = ((first[j], ref.save_g1), (second[j], ref.save_g2), (hidden[j], ref.save_e))

        def run():
            if part == 0:
                cp.wait(s1, s2, Q, K, V, PB, H, GP, O)
            r = pl.ds(part * (rows // count), rows // count)
            up = dot_nn(a2[r, :], matrix(s1, w))
            first[j][r, 0:w] = up.astype(bf16)
            other = dot_nn(a2[r, :], matrix(s2, w))
            second[j][r, 0:w] = other.astype(bf16)
            hidden[j][r, 0:w] = (up * other).astype(bf16)
            if part == count - 1:
                for n, (page, kept) in enumerate(saved):
                    cp.start((j, n), page.at[:, 0:w], kept.at[:, pl.ds(c0, w)])

        return run

    def down_grad(j, c0, w):
        def run():
            if j == 2:
                cp.wait(Y)
            wide[pl.ds(parts[j][0] + c0, w), :] = dot_tn(hidden[j][:, c0 : c0 + w], df[...])

        return run

    def down_slabs():
        slabs = ref.slabs
        n = slabs.shape[1]

        def tile(d):
            slabs[d] = wide[pl.ds(pl.multiple_of(d * n, 8), n), :].astype(bf16)

        tiles(slabs.shape[0], tile)
        cp.start(SLABS, slabs, ref.down_partial)

    work = []

    def piece(cost, f, needs=()):
        work.append((f, cost, needs, ()))

    piece(1.5, norm_in)
    piece(0.5, mask_df)
    for n in range(2):
        piece(1.15, projected(n, 0, q, Q, ref.save_q), (0,))
    for n in range(2):
        piece(1.15, projected(n, 1, k, K, ref.save_k), (1,))
    for n in range(2):
        piece(1.15, projected(n, 2, v, V, ref.save_v), (2,))
    for n in range(rows // BLOCK // 2):
        piece(1.0, attention(n, 1))
    for n in range(2):
        piece(1.15, projected(n, 3, gp), (3,))
    piece(0.5, gate_low)
    piece(1.5, mixed, (4,))
    for n in range(2):
        piece(1.1, middle(n, 0), (5,))
    piece(1.0, norm_middle)
    slots = ((1, 2), (3, 0), (1, 2))
    for j, (s1, s2) in enumerate(slots):
        for n in range(4):
            piece(1.3 * parts[j][1] / width, gated(j, s1, s2, n, 4), (6 + 2 * j, 7 + 2 * j))
    for j, (c0, w) in enumerate(parts):
        step = 512 if w % 512 == 0 else w // 2
        for n in range(w // step):
            piece(1.2, down_grad(j, n * step, step))
    piece(1.0, down_slabs)
    loads = {0: (0, QUERY), 1: (1, KEY), 2: (2, VALUE), 3: (3, GATE), 5: (0, OUT)}
    for j, (s1, s2) in enumerate(slots):
        loads[6 + 2 * j] = (s1, FIRST) + parts[j]
        loads[7 + 2 * j] = (s2, SECOND) + parts[j]
    readers = [sum(g in p[2] for p in work) for g in range(len(items))]
    ready, waiting, held = set(), [], {}

    def try_loads():
        while waiting:
            i = waiting[0]
            slot = loads[i][0]
            if slot in held and readers[held[slot]]:
                return
            held[slot] = i
            load(*loads[i])
            ready.add(i)
            waiting.pop(0)

    left = [sum(g == n for g in groups) for n in range(len(items))]

    def ended(i):
        group = groups[i]
        left[group] -= 1
        if left[group]:
            return
        if group in loads:
            waiting.append(group)
            try_loads()
        elif group == 4:
            cp.start(GAINS, ref.full[GAIN], ref.gain)
            ready.add(group)

    def reading(f, needs):
        def run():
            f()
            for i in needs:
                readers[i] -= 1
            try_loads()

        return run

    work = [(reading(f, needs), cost, needs, gives) for f, cost, needs, gives in work]
    Timeline(
        ag.timed_steps(), work, 3, range(len(items)), FORWARD_MODEL,
        can_run=lambda needs: all(i in ready for i in needs), ended=ended,
    ).run()
    ag.finish()
    cp.start(INV, ref.inv, ref.save_inv)
    cp.finish()


def forward(tokens, lengths, cotangent, shards):
    rows, width = tokens.shape
    ff = shards[FIRST].shape[1]
    parts = column_parts(ff, width)
    whole = [(m, 0, width) for m in (QUERY, KEY, VALUE, GATE)] + [(GAIN, 0, shards[GAIN].shape[1]), (OUT, 0, width)]
    whole += [(m, c0, w) for c0, w in parts for m in (FIRST, SECOND)]
    pieces = [(m, c0 + d, w, g) for g, (m, c0, n) in enumerate(whole) for d, w in column_parts(n, 512)]
    pieces.sort(key=lambda p: (p[3] if p[3] < 6 else 6 + (p[3] - 6) // 2, p[1]))
    pieces += [(DOWN, c0, w, len(whole)) for c0, w in column_parts(width, 256)]
    items = [(m, c0, w, n % 6 == 0 and m not in (GAIN, DOWN)) for n, (m, c0, w, _) in enumerate(pieces)]
    groups = [p[3] for p in pieces]
    n = len(items)
    page, row = jax.ShapeDtypeStruct((rows, width), bf16), jax.ShapeDtypeStruct((rows, 128), f32)
    wide = jax.ShapeDtypeStruct((rows, ff), bf16)
    saves = dict(
        save_a1=page, save_q=page, save_k=page, save_v=page, save_pb=page, save_gp=page, save_o=page, save_h=page,
        save_a2=page, save_g1=wide, save_g2=wide, save_e=wide, save_y=jax.ShapeDtypeStruct((rows, width), f32),
        save_inv=row,
    )
    slab = (32,) + shards[DOWN].shape
    saves[DOWN_PARTIAL] = jax.ShapeDtypeStruct(slab, bf16)
    outs = dict(full=[jax.ShapeDtypeStruct((4, 4, 2) + s.shape, bf16) for s in shards])
    scratch = dict(
        page=pltpu.VMEM((12, rows, width), bf16),
        weight=pltpu.VMEM((4, 4, 4, 2, shards[QUERY].shape[0], width), bf16),
        wide=pltpu.VMEM((3 * rows, width), f32),
        slabs=pltpu.VMEM(slab, bf16),
        gain=pltpu.VMEM((4, 4, 2) + shards[GAIN].shape, bf16),
        inv=pltpu.VMEM((rows, 128), f32),
        ssem=pltpu.SemaphoreType.DMA((n, 12)),
        rsem=pltpu.SemaphoreType.DMA((n, 12)),
        lsem=pltpu.SemaphoreType.DMA((n,)),
        csem=pltpu.SemaphoreType.DMA((FORWARD_COPIES,)),
    )
    ins = dict(cotangent=cotangent, shards=list(shards), tokens=tokens)
    hbm, vmem = pl.BlockSpec(memory_space=pl.ANY), pl.BlockSpec(memory_space=pltpu.VMEM)
    leaves = jax.tree.leaves
    got = pl.pallas_call(
        functools.partial(forward_kernel, items, groups, (dict(lengths=0), ins, outs, saves, scratch)),
        out_shape=leaves(outs) + leaves(saves),
        in_specs=[pl.BlockSpec(memory_space=pltpu.SMEM), hbm] + [vmem] * len(shards) + [hbm],
        out_specs=[hbm] * len(leaves(outs) + leaves(saves)),
        scratch_shapes=leaves(scratch),
        compiler_params=pltpu.CompilerParams(
            collective_id=0, has_side_effects=True, vmem_limit_bytes=62 * 2**20
        ),
    )(lengths, *leaves(ins))
    full = got[: len(shards)]
    return full, jax.tree.unflatten(jax.tree.structure(saves), got[len(shards) :])


class Timeline:
    def __init__(self, steps, work, window, given, model, after=None, can_run=None, ended=None):
        self.steps, self.work, self.window, self.model = steps, list(work), window, model
        self.after = after or [set()] * len(steps)
        self.can_run = can_run or (lambda needs: all(n in self.done for n in needs))
        self.ended = ended or (lambda i: None)
        self.made = set(given)
        self.at = [0] * len(steps)
        self.when = [0.0] * len(steps)
        self.free = {}
        self.now = 3.0
        self.done = set()

    def next_steps(self):
        started = 0
        for i, at in enumerate(self.at):
            if at == 0:
                if i in self.made and started < self.window and self.after[i] <= self.done:
                    yield i
                return
            if at < len(self.steps[i]):
                started += at < 2
                yield i

    def step(self, i):
        run, link, link_us, core_us = self.steps[i][self.at[i]]
        self.now = max(self.now, self.when[i])
        run(i)
        self.now += core_us * self.model.core
        self.when[i] = self.now
        if link:
            sent = max(self.now, self.free.get(link, 0.0)) + link_us * self.model.link
            self.free[link] = sent
            self.when[i] = sent + self.model.latency[link - 1 if link in (1, 2) else 2]
        self.at[i] += 1
        if self.at[i] == len(self.steps[i]):
            self.done.add(i)
            self.ended(i)

    def run(self):
        while True:
            steps = list(self.next_steps())
            ready = [i for i in steps if self.when[i] <= self.now + self.model.slack]
            if ready:
                self.step(ready[0])
            elif self.work and self.can_run(self.work[0][2]):
                run, core_us, _, gives = self.work.pop(0)
                run()
                self.now += core_us * self.model.work
                for i in gives:
                    self.made.add(i)
                    self.when[i] = self.now + self.model.latency[2]
            elif steps:
                self.step(min(steps, key=lambda i: self.when[i]))
            else:
                return


BACKWARD_COPIES = 64
BACKWARD_MODEL = SimpleNamespace(latency=(4.71, 4.18, 2.15), work=1.15, core=1.38, link=1.14, slack=0.0)
PAGES = 9


def backward_kernel(items, trees, *refs):
    ref = bind(trees, refs)
    rows, width = ref.cotangent.shape
    ff = ref.full[FIRST].shape[1]
    parts = column_parts(ff, width)
    page = [ref.page.at[i] for i in range(PAGES)]
    acc, other = ref.wide.at[0], ref.wide.at[1]
    here = Place()
    bufs = ring_buffers(ref.rings)
    cp = Saves(ref.csem)
    made = sorted({(it.m, it.g0) for it in items if it.m not in (DOWN, GAIN)})
    items = [
        SimpleNamespace(
            **vars(it), out=ref.grads[it.m], s0=it.c0 - it.g0,
            src=ref.partials[made.index((it.m, it.g0))] if (it.m, it.g0) in made else ref.down_partial,
        )
        for it in items
    ]
    rs = Scatter(here, items, bufs, lambda i: cp.wait((items[i].m, items[i].g0)), ref.ssem, ref.rsem, ref.lsem, ref.free)
    size, half_rows = 128, rows // 2
    live_len = ref.lengths[0]

    def live(first, n):
        return lax.broadcasted_iota(jnp.int32, (n, 1), 0) + first < live_len

    def load(n, src, c0=None, w=None, by_row=False):
        dst = page[n]
        if c0 is not None:
            if by_row:
                src, dst = src.at[pl.ds(c0, w)], dst.at[pl.ds(0, w)]
            else:
                src, dst = src.at[:, pl.ds(c0, w)], dst.at[:, pl.ds(0, w)]
        cp.start(n, src, dst)

    def halves(f):
        return [functools.partial(f, pl.ds(half_rows * n, half_rows)) for n in range(2)]

    work = []

    def piece(cost, f, needs=(), gives=()):
        work.append((f, cost, needs, gives))

    staged = []

    def grad_item(m, c0, w, left, right):
        name = (m, c0)
        slot = len(staged) % 2
        used = staged[-2] if len(staged) > 1 else None
        staged.append(name)
        stage = ref.stage.at[slot]
        gives = [i for i, it in enumerate(items) if (it.m, it.g0) == name]

        def half(n):
            def run():
                if n == 0:
                    cp.wait(*[k for k in range(PAGES) if page[k] is left or page[k] is right], used)
                cols = slice(n * (width // 2), (n + 1) * (width // 2))
                got = dot_tn(left[:, cols], right[:, 0:w]).astype(bf16)
                stage[2 * n : 2 * n + 2, :, :, :, 0:w] = got.reshape((2,) + stage.shape[1:4] + (w,))
                if n == 1:
                    to = ref.partials[made.index(name)]
                    cp.start(name, stage.at[:, :, :, :, 0:w], to.at[:, :, :, :, 0:w])

            return run

        piece(1.15 * w / width, half(0))
        piece(1.15 * w / width, half(1), (), gives)

    load(0, ref.cotangent)
    load(2, ref.full[DOWN], *parts[0], by_row=True)
    load(4, ref.save_g2, *parts[0])
    load(3, ref.save_g1, *parts[0])
    cp.start(12, ref.save_inv, ref.inv)
    cp.start(15, ref.full_gain, ref.gain)

    here.barrier()

    def hidden_back(j, n):
        c0, w = parts[j]

        def run():
            cp.wait(0, 2, 3, 4)
            if n == 0 and j == 0:
                load(1, ref.save_a2)
                load(5, ref.full[FIRST], *parts[0])
                load(6, ref.full[SECOND], *parts[0])
            r = pl.ds(half_rows * n, half_rows)
            de = dot_nt(page[0][r, :], page[2][0:w, :])
            de = jnp.where(live(half_rows * n, half_rows), de, 0.0)
            page[7][r, 0:w] = (de * page[4][r, 0:w].astype(f32)).astype(bf16)
            page[8][r, 0:w] = (de * page[3][r, 0:w].astype(f32)).astype(bf16)
            if n == 1:
                if j + 1 < len(parts):
                    load(2, ref.full[DOWN], *parts[j + 1], by_row=True)
                    load(3, ref.save_g1, *parts[j + 1])
                    load(4, ref.save_g2, *parts[j + 1])
                else:
                    load(3, ref.save_o)
                    load(4, ref.save_gp)

        return run

    def mid_back(j, n, second):
        c0, w = parts[j]

        def run():
            up, weight = (8, 6) if second else (7, 5)
            cp.wait(weight)
            r = pl.ds(half_rows * n, half_rows)
            part = dot_nt(page[up][r, 0:w], page[weight][:, 0:w])
            acc[r, :] = part if j == 0 and not second else acc[r, :] + part
            if n == 1 and second:
                if j + 1 < len(parts):
                    load(5, ref.full[FIRST], *parts[j + 1])
                    load(6, ref.full[SECOND], *parts[j + 1])
                else:
                    load(5, ref.save_h)
                    load(6, ref.full[OUT])
                    load(7, ref.save_q)
                    load(8, ref.save_k)

        return run

    for j, (c0, w) in enumerate(parts):
        for n in range(2):
            piece(1.5 * w / width, hidden_back(j, n))
        grad_item(FIRST, c0, w, page[1], page[7])
        grad_item(SECOND, c0, w, page[1], page[8])
        for second in range(2):
            for n in range(2):
                piece(1.1 * w / width, mid_back(j, n, second))

    def middle_back():
        cp.wait(12, 1, 0)

        def tile(i):
            r = rows_of(i, size)
            up, n2 = acc[r, :], page[1][r, :].astype(f32)
            mean = jnp.mean(up * n2, axis=-1, keepdims=True)
            dy = page[0][r, :].astype(f32) + ref.inv[r, 2:3] * (up - n2 * mean)
            acc[r, :] = dy
            page[2][r, :] = jnp.where(live(i * size, size), dy, 0.0).astype(bf16)

        tiles(rows // size, tile)
        load(1, ref.save_a1)
        load(0, ref.save_v)

    piece(1.5, middle_back)
    grad_item(OUT, 0, width, page[5], page[2])

    def branch_back(n):
        def run():
            if n == 0:
                cp.wait(6)
                load(5, ref.save_pb)
            r = pl.ds(half_rows * n, half_rows)
            other[r, :] = dot_nt(page[2][r, :], page[6][...])

        return run

    for n in range(2):
        piece(1.1, branch_back(n))

    def mix_back(first, count):
        def run():
            cp.wait(15, 3, 4)
            gains = ref.gain
            gain = jnp.concatenate(
                [
                    sum(gains[g, j, cc, 0:1, :].astype(f32) for j in (2 * half, 2 * half + 1) for cc in range(2))
                    for g in range(4)
                    for half in range(2)
                ],
                axis=1,
            )
            terms = ref.gain_terms
            if first == 0:
                terms[...] = jnp.zeros_like(terms)

            def tile(i):
                r = rows_of(i + first, size)
                inv = ref.inv[r, 1:2]
                up, z = other[r, :], page[4][r, :].astype(f32)
                normed = page[3][r, :].astype(f32) * inv
                sig = jax.nn.sigmoid(z)
                upu = up * (z * sig)
                terms[...] += (upu * normed).reshape(size // 8, 8, width).sum(axis=0)
                page[4][r, :] = (up * normed * gain * sig * (1.0 + z * (1.0 - sig))).astype(bf16)
                dm = upu * gain
                mean = jnp.mean(dm * normed, axis=-1, keepdims=True)
                page[3][r, :] = (inv * (dm - normed * mean)).astype(bf16)

            tiles(count, tile)

        return run

    for n in range(2):
        piece(1.2, mix_back(n * (rows // size // 2), rows // size // 2))

    def gain_item():
        g, terms = bufs[GAIN_RING].g, ref.gain_terms
        for yx in range(4):
            for z in range(4):
                for c in range(2):
                    at = 128 * (2 * yx + z // 2)
                    g[0, yx, z, c] = terms[:, at : at + 128]

    piece(0.3, gain_item, (), [i for i, it in enumerate(items) if it.m == GAIN])
    grad_item(GATE, 0, width, page[1], page[4])

    def attention_back(n, count):
        def run():
            cp.wait(7, 8, 0, 5)
            q, k, v, pb, do, dq, dk, dv = [page[m] for m in (7, 8, 0, 5, 3, 3, 6, 2)]
            tiles(count, lambda b: attend_blocks_back(b + n * count, q, k, v, pb, do, dq, dk, dv))
            if n == rows // BLOCK // 2 - 1:
                load(5, ref.full[GATE])
                load(7, ref.full[QUERY])
                load(8, ref.full[KEY])
                load(0, ref.full[VALUE])

        return run

    for n in range(rows // BLOCK // 2):
        piece(1.6, attention_back(n, 1))
    grad_item(QUERY, 0, width, page[1], page[3])
    grad_item(KEY, 0, width, page[1], page[6])
    grad_item(VALUE, 0, width, page[1], page[2])

    def input_part(n, up, w, first, loads):
        def run():
            if n == 0:
                cp.wait(w)
            r = pl.ds(half_rows * n, half_rows)
            part = dot_nt(page[up][r, :], page[w][...])
            other[r, :] = part if first else other[r, :] + part
            if n == 1:
                for to, src, at in loads:
                    load(to, src, *parts[at], by_row=src is ref.full[DOWN])

        return run

    down, hidden = ref.full[DOWN], ref.save_e
    products = (
        (4, 5, True, [(5, hidden, 0)]), (3, 7, False, [(7, down, 0), (3, hidden, 1)]),
        (6, 8, False, [(8, down, 1), (6, hidden, 2)]), (2, 0, False, [(0, down, 2)]),
    )
    for product in products:
        for n in range(2):
            piece(1.1, input_part(n, *product))

    def input_back():
        cp.wait(1)

        def tile(i):
            r = rows_of(i, size)
            up, n1 = other[r, :], page[1][r, :].astype(f32)
            mean = jnp.mean(up * n1, axis=-1, keepdims=True)
            page[4][r, :] = (acc[r, :] + ref.inv[r, 0:1] * (up - n1 * mean)).astype(bf16)

        tiles(rows // size, tile)
        cp.start(4, page[4], ref.input_grad)
        cp.start(16, ref.save_y, acc)

    piece(1.5, input_back)

    def output_part(n, j, e, w):
        def run():
            if n == 0:
                cp.wait(e, w)
            count = parts[j][1]
            r = pl.ds(half_rows * n, half_rows)
            part = dot_nn(page[e][r, 0:count], page[w][0:count, :])
            other[r, :] = part if j == 0 else other[r, :] + part

        return run

    for j, (e, w) in enumerate(((5, 7), (3, 8), (6, 0))):
        for n in range(2):
            piece(1.1 * parts[j][1] / width, output_part(n, j, e, w))

    def output():
        cp.wait(16)

        def tile(i):
            r = rows_of(i, size)
            page[2][r, :] = (acc[r, :] + jnp.where(live(i * size, size), other[r, :], 0.0)).astype(bf16)

        tiles(rows // size, tile)
        cp.start(2, page[2], ref.layer_out)

    piece(1.0, output)

    given = [i for i, it in enumerate(items) if it.m == DOWN]
    Timeline(rs.timed_steps(), work, 6, given, BACKWARD_MODEL, rs.after()).run()
    rs.finish()
    cp.finish()


def backward(cotangent, lengths, full, got):
    rows, width = cotangent.shape
    flat = [w.reshape(-1, w.shape[-1]) for w in full]
    ff = flat[FIRST].shape[1]
    r_in, r_down = full[QUERY].shape[3], full[DOWN].shape[3]
    parts = column_parts(ff, width)
    made = [(m, c0, w) for c0, w in parts for m in (FIRST, SECOND)] + [(OUT, 0, width)]
    made += [(m, 0, width) for m in (GATE, QUERY, KEY, VALUE)]
    specs = [(DOWN, c0, w, 0, DOWN_RING) for c0, w in column_parts(width, 256)]
    for n, (m, c0, w) in enumerate(made):
        if m == GATE:
            specs.append((GAIN, 0, 128, 0, GAIN_RING))
        if n in (1, 3, 8):
            specs += [(m, c0, w // 2, c0, PLANE_RING), (m, c0 + w // 2, w // 2, c0, IN_RING)]
        else:
            specs.append((m, c0, w, c0, IN_RING))
    slots = (4, 5, 2, 1)
    items = scatter_plan(specs, slots)
    n = len(items)
    ins = dict(cotangent=cotangent, full=flat, full_gain=full[GAIN])
    ins |= {k: a for k, a in got.items() if k != DOWN_PARTIAL}
    ins |= dict(down_partial=got[DOWN_PARTIAL].reshape(full[DOWN].shape))
    shapes = [(r_down if m == DOWN else r_in, flat[m].shape[1]) for m in range(len(full))]
    shapes[GAIN] = (8, 128)
    page = jax.ShapeDtypeStruct((rows, width), bf16)
    outs = dict(layer_out=page, input_grad=page)
    partial = jax.ShapeDtypeStruct(full[QUERY].shape, bf16)
    outs |= dict(partials=[partial] * len(made))
    grads = dict(grads=[jax.ShapeDtypeStruct(s, f32) for s in shapes])
    scratch = dict(
        rings=[
            scatter_scratch(DOWN_RING, slots[DOWN_RING], r_down, 256, bf16),
            scatter_scratch(IN_RING, slots[IN_RING], r_in, width, bf16),
            scatter_scratch(PLANE_RING, slots[PLANE_RING], r_in, 512, bf16),
            scatter_scratch(GAIN_RING, slots[GAIN_RING], 8, 128, f32),
        ],
        stage=pltpu.VMEM((2,) + full[QUERY].shape, bf16),
        page=pltpu.VMEM((PAGES, rows, width), bf16),
        wide=pltpu.VMEM((2, rows, width), f32),
        inv=pltpu.VMEM((rows, 128), f32),
        gain=pltpu.VMEM(full[GAIN].shape, bf16),
        gain_terms=pltpu.VMEM((8, width), f32),
        ssem=pltpu.SemaphoreType.DMA((n, 9)),
        rsem=pltpu.SemaphoreType.DMA((n, 9)),
        lsem=pltpu.SemaphoreType.DMA((n,)),
        csem=pltpu.SemaphoreType.DMA((BACKWARD_COPIES,)),
        free=pltpu.SemaphoreType.REGULAR((len(slots), 6)),
    )
    hbm, vmem = pl.BlockSpec(memory_space=pl.ANY), pl.BlockSpec(memory_space=pltpu.VMEM)
    leaves = jax.tree.leaves
    out = pl.pallas_call(
        functools.partial(backward_kernel, items, (dict(lengths=0), ins, outs, grads, scratch)),
        out_shape=leaves(outs) + leaves(grads),
        in_specs=[pl.BlockSpec(memory_space=pltpu.SMEM)] + [hbm] * len(leaves(ins)),
        out_specs=[hbm] * len(leaves(outs)) + [vmem] * len(leaves(grads)),
        scratch_shapes=leaves(scratch),
        compiler_params=pltpu.CompilerParams(
            collective_id=1, has_side_effects=True, vmem_limit_bytes=63 * 2**20
        ),
    )(lengths, *leaves(ins))
    return bind((outs, grads), out)


def finish_kernel(count, *refs):
    ins, terms, outs, gain = refs[:count], refs[count], refs[count + 1 : 2 * count + 1], refs[2 * count + 1]
    held, (sems,) = refs[2 * count + 2 : -1], refs[-1:]
    reads = [pltpu.make_async_copy(ins[k], held[k], sems.at[0, k]) for k in range(count)]
    writes = [pltpu.make_async_copy(held[k], outs[k], sems.at[1, k]) for k in range(count)]
    for m in reads:
        m.start()
    part = lax.rem(lax.axis_index(AXES[1]), 4)
    row = jnp.sum(terms[...], axis=0, keepdims=True)
    gain[...] = sum(jnp.where(part == k, row[:, 32 * k : 32 * (k + 1)], 0.0) for k in range(4))
    for r, w in zip(reads, writes):
        r.wait()
        w.start()
    for w in writes:
        w.wait()


def finish(arrays, terms):
    count = len(arrays)
    hbm, vmem = pl.BlockSpec(memory_space=pl.ANY), pl.BlockSpec(memory_space=pltpu.VMEM)
    return pl.pallas_call(
        functools.partial(finish_kernel, count),
        out_shape=[jax.ShapeDtypeStruct(a.shape, a.dtype) for a in arrays] + [jax.ShapeDtypeStruct((1, 32), f32)],
        in_specs=[hbm] * count + [vmem],
        out_specs=[hbm] * count + [vmem],
        scratch_shapes=[pltpu.VMEM(a.shape, a.dtype) for a in arrays] + [pltpu.SemaphoreType.DMA((2, count))],
        compiler_params=pltpu.CompilerParams(vmem_limit_bytes=62 * 2**20),
    )(*arrays, terms)


def slice_body(
    tokens, lengths, cotangent, w_query, w_key, w_value, w_gate, w_out, out_gain, w_first, w_second, w_down,
):
    rows, width = tokens.shape[0] * tokens.shape[1], tokens.shape[2]
    me = lax.axis_index(AXES[0]) * 8 + lax.axis_index(AXES[1])
    lane = lax.broadcasted_iota(jnp.int32, (16, 128), 1)
    gain_block = jnp.where(lax.div(lane, 32) == lax.rem(me, 4), jnp.tile(out_gain, 4)[None, :], 0)
    flat_cotangent = cotangent.reshape(rows, width)
    shards = (w_query, w_key, w_value, w_gate, gain_block, w_out, w_first, w_second, w_down)
    full, got = forward(tokens.reshape(rows, width), lengths, flat_cotangent, shards)
    back = backward(flat_cotangent, lengths, full, got)
    kept = [m for m in range(9) if m != GAIN]
    *whole, gain = finish([back.layer_out, back.input_grad] + [back.grads[m] for m in kept], back.grads[GAIN])
    grads = dict(zip(kept, whole[2:]))
    return (
        whole[0].reshape(tokens.shape), whole[1].reshape(tokens.shape),
        *[grads[m] for m in (QUERY, KEY, VALUE, GATE, OUT)], gain.reshape(32),
        *[grads[m] for m in (FIRST, SECOND, DOWN)],
    )


def solution(mesh):
    fits = (mesh.shape[AXES[0]], mesh.shape[AXES[1]]) == (4, 8)
    return jax.shard_map(
        slice_body if fits else general_body,
        mesh=mesh,
        in_specs=(
            P(AXES, None, None),
            P(AXES),
            P(AXES, None, None),
            P(AXES, None),
            P(AXES, None),
            P(AXES, None),
            P(AXES, None),
            P(AXES, None),
            P(AXES),
            P(AXES, None),
            P(AXES, None),
            P(AXES, None),
        ),
        out_specs=(
            P(AXES, None, None),
            P(AXES, None, None),
            P(AXES, None),
            P(AXES, None),
            P(AXES, None),
            P(AXES, None),
            P(AXES, None),
            P(AXES),
            P(AXES, None),
            P(AXES, None),
            P(AXES, None),
        ),
        check_vma=False,
    )
```

```python
import functools
from types import SimpleNamespace

import jax
import jax.numpy as jnp
from jax import lax
from jax.experimental import pallas as pl
from jax.experimental.pallas import tpu as pltpu
from jax.sharding import PartitionSpec as P

AXES = ("dp", "fsdp")
HEADS = 16
HEAD_DIM = 64
BLOCK = 64


epsilon = 1e-06
masked_score = -1e30


def normalize(values):
    inv_rms = lax.rsqrt(jnp.mean(values * values, axis=-1, keepdims=True) + epsilon)
    return (values * inv_rms, inv_rms)


def norm_back(normed, inv_rms, upstream):
    return inv_rms * (upstream - normed * jnp.mean(upstream * normed, axis=-1, keepdims=True))


def project(left_rows, right_rows):
    return jnp.dot(left_rows, right_rows, preferred_element_type=jnp.float32)


def project_back(upstream, weight):
    return lax.dot_general(
        upstream, weight, (((1,), (1,)), ((), ())), preferred_element_type=jnp.float32
    )


def weight_grad(inputs, upstream):
    return lax.dot_general(
        inputs, upstream, (((0,), (0,)), ((), ())), preferred_element_type=jnp.float32
    )


def split_heads(row_block):
    row_count = row_block.shape[0]
    return row_block.reshape(row_count // BLOCK, BLOCK, HEADS, HEAD_DIM)


def block_scores(query_blocks, key_blocks):
    scores = jnp.einsum(
        "bihd,bjhd->bhij", query_blocks, key_blocks, preferred_element_type=jnp.float32
    ) * HEAD_DIM ** (-0.5)
    causal = lax.broadcasted_iota(jnp.int32, (BLOCK, BLOCK), 0) >= lax.broadcasted_iota(
        jnp.int32, (BLOCK, BLOCK), 1
    )
    return jnp.where(causal, scores, masked_score)


def attend(query_rows, key_rows, value_rows):
    scores = block_scores(split_heads(query_rows), split_heads(key_rows))
    row_max = jnp.max(scores, axis=-1, keepdims=True)
    exp_scores = jnp.exp(scores - row_max)
    row_total = jnp.sum(exp_scores, axis=-1, keepdims=True)
    probs_low = (exp_scores / row_total).astype(jnp.bfloat16)
    head_mix = jnp.einsum(
        "bhij,bjhd->bihd", probs_low, split_heads(value_rows), preferred_element_type=jnp.float32
    )
    return (head_mix.reshape(query_rows.shape[0], -1), row_max + jnp.log(row_total))


def attend_back(query_rows, key_rows, value_rows, logsum, grad_mix):
    query_blocks = split_heads(query_rows)
    key_blocks = split_heads(key_rows)
    value_blocks = split_heads(value_rows)
    grad_blocks = split_heads(grad_mix)
    probs = jnp.exp(block_scores(query_blocks, key_blocks) - logsum)
    probs_low = probs.astype(jnp.bfloat16)
    grad_probs = jnp.einsum(
        "bihd,bjhd->bhij", grad_blocks, value_blocks, preferred_element_type=jnp.float32
    )
    grad_values = jnp.einsum(
        "bhij,bihd->bjhd", probs_low, grad_blocks, preferred_element_type=jnp.float32
    )
    grad_scores = (
        probs * (grad_probs - jnp.sum(grad_probs * probs, axis=-1, keepdims=True))
    ).astype(jnp.bfloat16)
    scale_factor = HEAD_DIM ** (-0.5)
    grad_queries = (
        jnp.einsum("bhij,bjhd->bihd", grad_scores, key_blocks, preferred_element_type=jnp.float32)
        * scale_factor
    )
    grad_keys = (
        jnp.einsum("bhij,bihd->bjhd", grad_scores, query_blocks, preferred_element_type=jnp.float32)
        * scale_factor
    )
    row_count = query_rows.shape[0]
    return (
        grad_queries.reshape(row_count, -1).astype(jnp.bfloat16),
        grad_keys.reshape(row_count, -1).astype(jnp.bfloat16),
        grad_values.reshape(row_count, -1).astype(jnp.bfloat16),
    )


def ffn_sums(second_in, hidden, grad_first_proj, grad_second_proj, grad_branch):
    both_proj = jnp.concatenate([grad_first_proj, grad_second_proj], axis=1)
    inner_shard = lax.psum_scatter(
        weight_grad(second_in, both_proj), AXES, scatter_dimension=0, tiled=True
    )
    down_shard = lax.psum_scatter(
        weight_grad(hidden, grad_branch), AXES, scatter_dimension=0, tiled=True
    )
    ff_width = grad_first_proj.shape[1]
    return (inner_shard[:, :ff_width], inner_shard[:, ff_width:], down_shard)


def general_body(
    tokens,
    lengths,
    cotangent,
    w_query,
    w_key,
    w_value,
    w_gate,
    w_out,
    out_gain,
    w_first,
    w_second,
    w_down,
):
    slot_count, slot_len, feature_width = tokens.shape
    row_count = slot_count * slot_len
    places = lax.broadcasted_iota(jnp.int32, (slot_count, slot_len), 1)
    live_rows = (places < lengths[:, None]).astype(jnp.float32).reshape(row_count, 1)
    attn_full = (
        lax.all_gather(w_query, AXES, axis=0, tiled=True),
        lax.all_gather(w_key, AXES, axis=0, tiled=True),
        lax.all_gather(w_value, AXES, axis=0, tiled=True),
        lax.all_gather(w_gate, AXES, axis=0, tiled=True),
        lax.all_gather(w_out, AXES, axis=0, tiled=True),
        lax.all_gather(out_gain, AXES, axis=0, tiled=True),
    )
    ffn_full = (
        lax.all_gather(w_first, AXES, axis=0, tiled=True),
        lax.all_gather(w_second, AXES, axis=0, tiled=True),
        lax.all_gather(w_down, AXES, axis=0, tiled=True),
    )
    query_full, key_full, value_full, gate_full, out_full, gain_full = attn_full
    first_full, second_full, down_full = ffn_full
    inputs = tokens.reshape(row_count, feature_width).astype(jnp.float32)
    normed_in, inv_in = normalize(inputs)
    first_in = normed_in.astype(jnp.bfloat16)
    query_rows = project(first_in, query_full).astype(jnp.bfloat16)
    key_rows = project(first_in, key_full).astype(jnp.bfloat16)
    value_rows = project(first_in, value_full).astype(jnp.bfloat16)
    gate_pre = project(first_in, gate_full)
    head_mix, logsum = attend(query_rows, key_rows, value_rows)
    normed_mix, inv_mix = normalize(head_mix)
    gain_rows = gain_full.astype(jnp.float32)
    gate_act = jax.nn.silu(gate_pre)
    scaled_mix = normed_mix * gain_rows
    branch_in = (scaled_mix * gate_act).astype(jnp.bfloat16)
    middle = inputs + live_rows * project(branch_in, out_full)
    normed_mid, inv_mid = normalize(middle)
    second_in = normed_mid.astype(jnp.bfloat16)
    first_proj = project(second_in, first_full)
    second_proj = project(second_in, second_full)
    hidden = (first_proj * second_proj).astype(jnp.bfloat16)
    final_rows = middle + live_rows * project(hidden, down_full)
    layer_out = final_rows.astype(jnp.bfloat16).reshape(tokens.shape)
    first_back, second_back, down_back = (
        lax.all_gather(w_first, AXES, axis=0, tiled=True),
        lax.all_gather(w_second, AXES, axis=0, tiled=True),
        lax.all_gather(w_down, AXES, axis=0, tiled=True),
    )
    query_back, key_back, value_back, gate_back, out_back, gain_back = (
        lax.all_gather(w_query, AXES, axis=0, tiled=True),
        lax.all_gather(w_key, AXES, axis=0, tiled=True),
        lax.all_gather(w_value, AXES, axis=0, tiled=True),
        lax.all_gather(w_gate, AXES, axis=0, tiled=True),
        lax.all_gather(w_out, AXES, axis=0, tiled=True),
        lax.all_gather(out_gain, AXES, axis=0, tiled=True),
    )
    gain_used = gain_back.astype(jnp.float32)
    grad_final = cotangent.reshape(row_count, feature_width).astype(jnp.float32)
    grad_branch = (live_rows * grad_final).astype(jnp.bfloat16)
    grad_hidden = project_back(grad_branch, down_back)
    grad_first_proj = (grad_hidden * second_proj).astype(jnp.bfloat16)
    grad_second_proj = (grad_hidden * first_proj).astype(jnp.bfloat16)
    grad_normed_mid = project_back(grad_first_proj, first_back) + project_back(
        grad_second_proj, second_back
    )
    grad_middle = grad_final + norm_back(normed_mid, inv_mid, grad_normed_mid)
    grad_attn_out = (live_rows * grad_middle).astype(jnp.bfloat16)
    grad_branch_in = project_back(grad_attn_out, out_back)
    gain_terms = grad_branch_in * gate_act * normed_mix
    sigmoid_gate = jax.nn.sigmoid(gate_pre)
    grad_gate_pre = (
        grad_branch_in * scaled_mix * sigmoid_gate * (1.0 + gate_pre * (1.0 - sigmoid_gate))
    ).astype(jnp.bfloat16)
    grad_scaled = grad_branch_in * gate_act * gain_used
    grad_mix = norm_back(normed_mix, inv_mix, grad_scaled).astype(jnp.bfloat16)
    grad_queries, grad_keys, grad_values = attend_back(
        query_rows, key_rows, value_rows, logsum, grad_mix
    )
    grad_normed_in = (
        project_back(grad_queries, query_back)
        + project_back(grad_keys, key_back)
        + project_back(grad_values, value_back)
        + project_back(grad_gate_pre, gate_back)
    )
    grad_inputs = grad_middle + norm_back(normed_in, inv_in, grad_normed_in)
    input_grad = grad_inputs.astype(jnp.bfloat16).reshape(tokens.shape)
    ffn_shards = ffn_sums(second_in, hidden, grad_first_proj, grad_second_proj, grad_branch)
    four_grads = jnp.concatenate([grad_queries, grad_keys, grad_values, grad_gate_pre], axis=1)
    from_input = weight_grad(first_in, four_grads)
    from_branch = weight_grad(branch_in, grad_attn_out)
    gain_part = jnp.sum(gain_terms, axis=0)[:, None]
    attn_shard = lax.psum_scatter(
        jnp.concatenate([from_input, from_branch, gain_part], axis=1),
        AXES,
        scatter_dimension=0,
        tiled=True,
    )
    shard_query = attn_shard[:, 0:feature_width]
    shard_key = attn_shard[:, feature_width : 2 * feature_width]
    shard_value = attn_shard[:, 2 * feature_width : 3 * feature_width]
    shard_gate = attn_shard[:, 3 * feature_width : 4 * feature_width]
    shard_out = attn_shard[:, 4 * feature_width : 5 * feature_width]
    shard_gain = attn_shard[:, 5 * feature_width]
    shard_first, shard_second, shard_down = ffn_shards
    return (
        layer_out,
        input_grad,
        shard_query,
        shard_key,
        shard_value,
        shard_gate,
        shard_out,
        shard_gain,
        shard_first,
        shard_second,
        shard_down,
    )


MESH = pl.DeviceIdType.MESH
f32 = jnp.float32
bf16 = jnp.bfloat16
QUERY, KEY, VALUE, GATE, GAIN, OUT, FIRST, SECOND, DOWN = range(9)
DOWN_PARTIAL = "down_partial"


def bind(trees, refs):
    fields = {}
    for tree in trees:
        leaves, form = jax.tree.flatten(tree)
        fields |= jax.tree.unflatten(form, refs[: len(leaves)])
        refs = refs[len(leaves) :]
    return SimpleNamespace(**fields)


class Place:
    def __init__(self):
        dp, fs = lax.axis_index(AXES[0]), lax.axis_index(AXES[1])
        z, c = lax.div(fs, 2), lax.rem(fs, 2)
        self.dp, self.fs, self.z, self.c = dp, fs, z, c
        self.nx = dp + 1 - 2 * lax.rem(dp, 2)
        self.ny = lax.rem(dp + 2, 4)
        self.dg = lax.rem(self.nx + 2, 4)
        self.zp = [lax.rem(z + k, 4) for k in (1, 2, 3)]
        self.sib = (dp, z * 2 + 1 - c)
        self.zdev = [(dp, zz * 2 + c) for zz in self.zp]
        self.xdev, self.ydev = (self.nx, fs), (self.ny, fs)
        self.peers = [self.sib, self.xdev, self.ydev] + self.zdev
        self.above, self.below, self.always = z < 3, z > 0, None
        self.end = (z == 0) | (z == 3)
        self.middle = (z == 1) | (z == 2)
        self.inward = z + 1 - 2 * lax.rem(z, 2)
        self.inward_dev = (dp, self.inward * 2 + c)

    def barrier(self):
        bar = pltpu.get_barrier_semaphore()
        for d in self.peers:
            pl.semaphore_signal(bar, inc=1, device_id=d, device_id_type=MESH)
        pl.semaphore_wait(bar, 6)


def where_true(cond, run):
    if cond is None:
        run()
    else:
        pl.when(cond)(run)


class Moves:
    def __init__(self, here, ssem, rsem):
        self.h, self.ssem, self.rsem, self.sends = here, ssem, rsem, {}
        self.along_z = ((0, here.above), (1, None), (2, here.below))
        self.from_z = ((0, here.below), (1, None), (2, here.above))

    def rc(self, i, k, src, dst, dev):
        return pltpu.make_async_remote_copy(
            src_ref=src, dst_ref=dst, send_sem=self.ssem.at[i, k], recv_sem=self.rsem.at[i, k],
            device_id=dev, device_id_type=MESH,
        )

    def go(self, i, *moves, cond=None):
        for m in moves:
            where_true(cond, m.start)
            self.sends.setdefault(i, []).append((cond, m))

    def release(self, i):
        for cond, m in self.sends.pop(i, ()):
            where_true(cond, m.wait_send)

    def finish(self):
        for i in list(self.sends):
            self.release(i)


class Gather(Moves):
    def __init__(self, here, items, shards, outs, ssem, rsem, lsem):
        super().__init__(here, ssem, rsem)
        self.items, self.shards, self.outs, self.lsem = items, shards, outs, lsem

    def block(self, i, yx, z, rows=slice(None)):
        m, c0, w, _ = self.items[i]
        return self.outs[m].at[yx, z, self.h.c, rows, pl.ds(c0, w)]

    def shard(self, i):
        m, c0, w, _ = self.items[i]
        return self.shards[m].at[:, pl.ds(c0, w)]

    def same(self, i, k, ref, dev):
        return self.rc(i, k, ref, ref, dev)

    def own(self, i):
        return pltpu.make_async_copy(self.shard(i), self.block(i, self.h.dp, self.h.z), self.lsem.at[i])

    def zmsg(self, i, k, planes):
        h = self.h
        if planes:
            return self.same(i, k, self.block(i, slice(None), h.z), h.zdev[k])
        return self.rc(i, k, self.shard(i), self.block(i, h.dp, h.z), h.zdev[k])

    def relay(self, i, planes):
        h = self.h
        return self.same(i, 11, self.block(i, slice(None) if planes else h.dp, h.zp[1]), h.inward_dev)

    def send_z(self, i, planes):
        for k, cond in self.along_z:
            self.go(i, self.zmsg(i, k, planes), cond=cond)

    def relay_z(self, i, planes):
        self.zmsg(i, 1, planes).wait_recv()
        self.go(i, self.relay(i, planes), cond=self.h.middle)

    def wait_z(self, i, planes):
        where_true(self.h.below, self.zmsg(i, 0, planes).wait_recv)
        where_true(self.h.above, self.zmsg(i, 2, planes).wait_recv)
        where_true(self.h.end, self.relay(i, planes).wait_recv)

    def col(self, i, k, yx, dev):
        return self.same(i, k, self.block(i, yx, slice(None)), dev)

    def half(self, i, k, yx, lo, dev):
        return self.same(i, k, self.block(i, yx, slice(lo, lo + 2)), dev)

    def part(self, i, k, yx, lo, dev):
        n = self.shards[self.items[i][0]].shape[0] // 2
        return self.same(i, k, self.block(i, yx, self.h.z, pl.ds(lo * n, n)), dev)

    def column0(self, i):
        self.own(i).start()
        self.send_z(i, False)

    def column1(self, i):
        self.relay_z(i, False)

    def column2(self, i):
        h = self.h
        self.own(i).wait()
        self.wait_z(i, False)
        self.go(i, self.col(i, 3, h.dp, h.xdev), self.col(i, 4, h.dp, h.ydev), self.col(i, 7, h.dp, h.sib))

    def column3(self, i):
        h = self.h
        self.col(i, 3, h.dp, h.xdev).wait_recv()
        self.go(i, self.half(i, 6, h.nx, 2, h.ydev), self.col(i, 8, h.nx, h.sib))
        self.col(i, 4, h.dp, h.ydev).wait_recv()
        self.go(i, self.half(i, 5, h.ny, 0, h.xdev), self.col(i, 9, h.ny, h.sib))

    def column4(self, i):
        h = self.h
        self.half(i, 5, h.ny, 0, h.xdev).wait_recv()
        self.half(i, 6, h.nx, 2, h.ydev).wait_recv()
        self.go(i, self.col(i, 10, h.dg, h.sib))

    def column5(self, i):
        h = self.h
        for k in (7, 8, 9, 10):
            self.col(i, k, h.dp, h.sib).wait_recv()

    def plane0(self, i):
        h = self.h
        self.own(i).start()
        self.go(
            i, self.rc(i, 3, self.shard(i), self.block(i, h.dp, h.z), h.xdev),
            self.rc(i, 4, self.shard(i), self.block(i, h.dp, h.z), h.ydev),
        )

    def plane1(self, i):
        h = self.h
        self.same(i, 3, self.block(i, h.nx, h.z), h.xdev).wait_recv()
        self.go(i, self.part(i, 6, h.nx, 1, h.ydev))
        self.same(i, 4, self.block(i, h.ny, h.z), h.ydev).wait_recv()
        self.go(i, self.part(i, 5, h.ny, 0, h.xdev))

    def plane2(self, i):
        h = self.h
        self.own(i).wait()
        self.part(i, 5, h.dg, 0, h.xdev).wait_recv()
        self.part(i, 6, h.dg, 1, h.ydev).wait_recv()
        self.send_z(i, True)
        self.go(i, self.same(i, 7, self.block(i, slice(None), h.z), h.sib))

    def plane3(self, i):
        self.relay_z(i, True)

    def plane4(self, i):
        h = self.h
        self.wait_z(i, True)
        self.go(i, *[self.same(i, 8 + k, self.block(i, slice(None), h.zp[k]), h.sib) for k in range(3)])

    def plane5(self, i):
        h = self.h
        for k in (7, 8, 9, 10):
            self.same(i, k, self.block(i, slice(None), h.z), h.sib).wait_recv()

    def timed_steps(self):
        steps = []
        for m, _, w, planes in self.items:
            u = w * self.shards[m].shape[0] / (32 * 1024)
            if planes:
                steps.append([
                    (self.plane0, 1, 1.5 * u, 0.2), (self.plane1, 1, 0.8 * u, 0.2), (self.plane2, 2, 10.0 * u, 0.2),
                    (self.plane3, 2, 8.0 * u, 0.1), (self.plane4, 3, 1.0 * u, 0.1), (self.plane5, None, 0.0, 0.1),
                ])
            else:
                steps.append([
                    (self.column0, 2, 2.5 * u, 0.2), (self.column1, 2, 2.0 * u, 0.1), (self.column2, 1, 5.8 * u, 0.2),
                    (self.column3, 1, 2.9 * u, 0.2), (self.column4, 3, 1.0 * u, 0.1), (self.column5, None, 0.0, 0.1),
                ])
        return steps


class Scatter(Moves):
    def __init__(self, here, items, bufs, before, ssem, rsem, lsem, free):
        super().__init__(here, ssem, rsem)
        self.items, self.bufs, self.before, self.lsem, self.free = items, bufs, before, lsem, free

    def views(self, i):
        it = self.items[i]
        return it, self.bufs[it.cls], it.slot, it.w

    def mine(self, i, yx, z, rows=slice(None)):
        it, b, s, w = self.views(i)
        if b.p is not None:
            return b.p.at[s, yx, z, rows, 0:w]
        return b.g.at[s, yx, z, self.h.c, rows, 0:w]

    def buf(self, i, ref, *at):
        return ref.at[(self.items[i].slot,) + at + (slice(None), slice(0, self.items[i].w))]

    def m_sib(self, i):
        it, b, s, w = self.views(i)
        if b.p is not None:
            src = it.src.at[:, :, 1 - self.h.c, :, pl.ds(it.s0, w)]
        else:
            src = b.g.at[s, :, :, 1 - self.h.c, :, 0:w]
        return self.rc(i, 0, src, self.buf(i, b.r1, slice(None), slice(None)), self.h.sib)

    def m_load(self, i):
        it, b, s, w = self.views(i)
        src = it.src.at[:, :, self.h.c, :, pl.ds(it.s0, w)]
        return pltpu.make_async_copy(src, self.buf(i, b.p, slice(None), slice(None)), self.lsem.at[i])

    def add(self, to, *terms):
        total = to[...].astype(f32)
        for t in terms:
            total = total + t[...].astype(f32)
        to[...] = total.astype(to.dtype)

    def step0(self, i):
        it, b, s, w = self.views(i)
        if it.before is not None:
            self.release(it.before)
            for k in range(6):
                pl.semaphore_wait(self.free.at[it.cls, k], 1)
        self.before(i)
        if b.p is not None:
            self.m_load(i).start()
        self.go(i, self.m_sib(i))

    def wait_halves(self, i):
        if self.bufs[self.items[i].cls].p is not None:
            self.m_load(i).wait()
        self.m_sib(i).wait_recv()

    def last(self, i):
        it = self.items[i]
        if it.reused:
            for k, d in enumerate(self.h.peers):
                pl.semaphore_signal(
                    self.free.at[it.cls, k if k < 3 else 8 - k], inc=1, device_id=d, device_id_type=MESH
                )

    def m_z(self, i, k, yx):
        b = self.bufs[self.items[i].cls]
        more = () if yx is None else (slice(None),)
        yx = self.h.dp if yx is None else yx
        return self.rc(i, 5 + k, self.mine(i, yx, self.h.zp[k]), self.buf(i, b.rz, k, *more), self.h.zdev[k])

    def m_relay(self, i, yx):
        b = self.bufs[self.items[i].cls]
        more = () if yx is None else (slice(None),)
        yx = self.h.dp if yx is None else yx
        return self.rc(i, 8, self.mine(i, yx, 3 - self.h.z), self.buf(i, b.rz, 3, *more), self.h.inward_dev)

    def send_z(self, i, yx=None):
        self.go(i, self.m_relay(i, yx), cond=self.h.end)
        self.go(i, self.m_z(i, 1, yx), cond=self.h.end)
        self.go(i, self.m_z(i, 0, yx), cond=self.h.above)
        self.go(i, self.m_z(i, 2, yx), cond=self.h.below)

    def relay_z(self, i, yx=None):
        def run():
            b = self.bufs[self.items[i].cls]
            self.m_relay(i, yx).wait_recv()
            if yx is None:
                self.add(self.mine(i, self.h.dp, self.h.zp[1]), self.buf(i, b.rz, 3))
            else:
                tiles(4, lambda j: self.add(self.mine(i, j, self.h.zp[1]), self.buf(i, b.rz, 3, j)))

        where_true(self.h.middle, run)
        self.go(i, self.m_z(i, 1, yx), cond=self.h.middle)

    def m_dx(self, i):
        b = self.bufs[self.items[i].cls]
        return self.rc(i, 1, self.mine(i, self.h.dg, slice(0, 2)), self.buf(i, b.rd, 0, slice(None)), self.h.xdev)

    def m_dy(self, i):
        b = self.bufs[self.items[i].cls]
        return self.rc(i, 2, self.mine(i, self.h.dg, slice(2, 4)), self.buf(i, b.rd, 1, slice(None)), self.h.ydev)

    def m_x(self, i):
        b = self.bufs[self.items[i].cls]
        return self.rc(i, 3, self.mine(i, self.h.nx, slice(None)), self.buf(i, b.rxy, 0, slice(None)), self.h.xdev)

    def m_y(self, i):
        b = self.bufs[self.items[i].cls]
        return self.rc(i, 4, self.mine(i, self.h.ny, slice(None)), self.buf(i, b.rxy, 1, slice(None)), self.h.ydev)

    def column1(self, i):
        r, dg = self.bufs[self.items[i].cls].r1, self.h.dg
        self.wait_halves(i)
        tiles(4, lambda j: self.add(self.mine(i, dg, j), self.buf(i, r, dg, j)))
        self.go(i, self.m_dx(i), self.m_dy(i))

        def near(j):
            a, q = lax.rem(dg + 1 + lax.div(j, 4), 4), lax.rem(j, 4)
            self.add(self.mine(i, a, q), self.buf(i, r, a, q))

        tiles(12, near)

    def column2(self, i):
        rd, nx, ny = self.bufs[self.items[i].cls].rd, self.h.nx, self.h.ny
        self.m_dx(i).wait_recv()
        tiles(2, lambda j: self.add(self.mine(i, ny, j), self.buf(i, rd, 0, j)))
        self.go(i, self.m_y(i))
        self.m_dy(i).wait_recv()
        tiles(2, lambda j: self.add(self.mine(i, nx, 2 + j), self.buf(i, rd, 1, j)))
        self.go(i, self.m_x(i))

    def column3(self, i):
        rxy, dp = self.bufs[self.items[i].cls].rxy, self.h.dp
        self.m_x(i).wait_recv()
        self.m_y(i).wait_recv()
        tiles(4, lambda j: self.add(self.mine(i, dp, j), self.buf(i, rxy, 0, j), self.buf(i, rxy, 1, j)))
        self.send_z(i)

    def column4(self, i):
        self.relay_z(i)

    def column5(self, i):
        it, b, s, w = self.views(i)
        cols = pl.ds(it.c0, w)
        self.m_z(i, 1, None).wait_recv()
        it.out[:, cols] = self.mine(i, self.h.dp, self.h.z)[...].astype(f32) + self.buf(i, b.rz, 1)[...].astype(f32)
        for k, cond in self.from_z:
            if cond is not None:

                def more(k=k):
                    self.m_z(i, k, None).wait_recv()
                    it.out[:, cols] += self.buf(i, b.rz, k)[...].astype(f32)

                pl.when(cond)(more)
        self.last(i)

    def plane1(self, i):
        r = self.bufs[self.items[i].cls].r1
        self.wait_halves(i)

        def both(j):
            a, q = lax.div(j, 4), lax.rem(j, 4)
            self.add(self.mine(i, a, q), self.buf(i, r, a, q))

        tiles(16, both)
        self.send_z(i, slice(None))

    def plane2(self, i):
        self.relay_z(i, slice(None))

    def p_d(self, i, n):
        b, h = self.bufs[self.items[i].cls], self.h
        rows = self.items[i].out.shape[0] // 2
        src = self.mine(i, h.dg, h.z, pl.ds(n * rows, rows))
        return self.rc(i, 1 + n, src, self.buf(i, b.rd, n), (h.xdev, h.ydev)[n])

    def p_xy(self, i, n):
        b, h = self.bufs[self.items[i].cls], self.h
        return self.rc(
            i, 3 + n, self.mine(i, (h.nx, h.ny)[n], h.z), self.buf(i, b.rxy, n), (h.xdev, h.ydev)[n]
        )

    def plane3(self, i):
        b, z = self.bufs[self.items[i].cls], self.h.z
        for k, cond in self.from_z:

            def more(k=k):
                self.m_z(i, k, slice(None)).wait_recv()
                tiles(4, lambda j: self.add(self.mine(i, j, z), self.buf(i, b.rz, k, j)))

            where_true(cond, more)
        self.go(i, self.p_d(i, 0), self.p_d(i, 1))

    def plane4(self, i):
        b, h = self.bufs[self.items[i].cls], self.h
        rows = self.items[i].out.shape[0] // 2
        for n, other in ((0, h.ny), (1, h.nx)):
            self.p_d(i, n).wait_recv()
            self.add(self.mine(i, other, h.z, pl.ds(n * rows, rows)), self.buf(i, b.rd, n))
            self.go(i, self.p_xy(i, 1 - n))

    def plane5(self, i):
        it, b, s, w = self.views(i)
        self.p_xy(i, 0).wait_recv()
        self.p_xy(i, 1).wait_recv()
        total = self.mine(i, self.h.dp, self.h.z)[...].astype(f32)
        it.out[:, pl.ds(it.c0, w)] = total + self.buf(i, b.rxy, 0)[...].astype(f32) + self.buf(i, b.rxy, 1)[...].astype(f32)
        self.last(i)

    def timed_steps(self):
        steps = []
        for i, it in enumerate(self.items):
            u = it.w * it.out.shape[0] / (32 * 1024)
            first = (self.step0, -i - 1, 1.5 * u, 0.2)
            if it.cls == PLANE_RING:
                steps.append([
                    first, (self.plane1, 2, 10.0 * u, 0.5 * u + 0.2), (self.plane2, 2, 8.0 * u, 0.1 * u + 0.1),
                    (self.plane3, 1, 0.8 * u, 0.2 * u + 0.2), (self.plane4, 1, 1.5 * u, 0.2),
                    (self.plane5, None, 0.0, 0.2),
                ])
            else:
                steps.append([
                    first, (self.column1, 1, 2.9 * u, 0.4 * u + 0.2), (self.column2, 1, 5.8 * u, 0.2 * u + 0.2),
                    (self.column3, 2, 2.5 * u, 0.2 * u + 0.2), (self.column4, 2, 2.0 * u, 0.1),
                    (self.column5, None, 0.0, 0.2),
                ])
        return steps

    def after(self):
        return [set() if it.before is None else {it.before} for it in self.items]


DOWN_RING, IN_RING, PLANE_RING, GAIN_RING = range(4)


def scatter_plan(specs, ring):
    items, by_class = [], {}
    for m, c0, w, g0, cls in specs:
        mine = by_class.setdefault(cls, [])
        it = SimpleNamespace(m=m, c0=c0, w=w, g0=g0, cls=cls, slot=len(mine) % ring[cls], before=None, reused=False)
        if len(mine) >= ring[cls]:
            it.before = mine[-ring[cls]]
            items[it.before].reused = True
        mine.append(len(items))
        items.append(it)
    return items


def scatter_scratch(cls, slots, r, w, dt):
    held, planes = cls == GAIN_RING, cls == PLANE_RING
    return dict(
        g=pltpu.VMEM((slots, 4, 4, 2, r, w) if held else (8, 128), dt),
        p=pltpu.VMEM((8, 128) if held else (slots, 4, 4, r, w), dt),
        r1=pltpu.VMEM((slots, 4, 4, r, w), dt),
        rd=pltpu.VMEM((slots, 2, r // 2, w) if planes else (slots, 2, 2, r, w), dt),
        rxy=pltpu.VMEM((slots, 2, r, w) if planes else (slots, 2, 4, r, w), dt),
        rz=pltpu.VMEM((slots, 4, 4, r, w) if planes else (slots, 4, r, w), dt),
    )


def ring_buffers(rings):
    bufs = [SimpleNamespace(**b) for b in rings]
    for cls, b in enumerate(bufs):
        if cls == GAIN_RING:
            b.p = None
        else:
            b.g = None
    return bufs


def column_parts(width, part):
    return [(c0, min(part, width - c0)) for c0 in range(0, width, part)]


def dot_nn(a, b):
    return jnp.dot(a, b, preferred_element_type=f32)


def dot_nt(a, b):
    return lax.dot_general(a, b, (((1,), (1,)), ((), ())), preferred_element_type=f32)


def dot_tn(a, b):
    return lax.dot_general(a, b, (((0,), (0,)), ((), ())), preferred_element_type=f32)


def tiles(count, body):
    def step(i, carry):
        body(i)
        return carry

    lax.fori_loop(0, count, step, 0)


def rows_of(i, size):
    return pl.ds(pl.multiple_of(i * size, size), size)


def rms_inv(values):
    return lax.rsqrt(jnp.mean(values * values, axis=-1, keepdims=True) + epsilon)


QUAD = 4 * HEAD_DIM


def quad_mask():
    shape = (QUAD, QUAD)
    row = lax.div(lax.broadcasted_iota(jnp.int32, shape, 0), HEAD_DIM)
    return row == lax.div(lax.broadcasted_iota(jnp.int32, shape, 1), HEAD_DIM)


def spread_heads(rows, mask):
    tall = jnp.concatenate([rows] * 4, axis=0)
    return jnp.where(mask, tall, jnp.zeros_like(tall))


def per_head(values, reduce, fill):
    halves = []
    for k in range(2):
        part = values[:, 128 * k : 128 * (k + 1)]
        low = lax.broadcasted_iota(jnp.int32, part.shape, 1) < HEAD_DIM
        first = reduce(jnp.where(low, part, fill), axis=-1, keepdims=True)
        second = reduce(jnp.where(low, fill, part), axis=-1, keepdims=True)
        halves.append(jnp.where(low, first, second))
    return jnp.concatenate(halves, axis=1)


def attend_blocks(b, q, k, v, probs, mix):
    mask = quad_mask()
    place = lax.broadcasted_iota(jnp.int32, (BLOCK, QUAD), 0)
    causal = place >= lax.rem(lax.broadcasted_iota(jnp.int32, (BLOCK, QUAD), 1), HEAD_DIM)
    at = [
        (rows_of(2 * b + n, BLOCK), slice(QUAD * g, QUAD * (g + 1))) for n in range(2) for g in range(HEADS // 4)
    ]
    scores = [
        jnp.where(causal, dot_nt(q[i], spread_heads(k[i], mask)) * HEAD_DIM ** (-0.5), masked_score) for i in at
    ]
    tops = [per_head(s, jnp.max, masked_score) for s in scores]
    terms = [jnp.exp(s - m) for s, m in zip(scores, tops)]
    totals = [per_head(t, jnp.sum, 0.0) for t in terms]
    lows = [(t / n).astype(bf16) for t, n in zip(terms, totals)]
    mixes = [dot_nn(p, spread_heads(v[i], mask)) for i, p in zip(at, lows)]
    for i, p, m in zip(at, lows, mixes):
        probs[i] = p
        mix[i] = m


def attend_blocks_back(b, q, k, v, probs, grad_mix, dq, dk, dv):
    mask = quad_mask()
    scale = HEAD_DIM ** (-0.5)
    low = lax.broadcasted_iota(jnp.int32, (BLOCK, 128), 1) < HEAD_DIM

    def own_head(wide):
        return jnp.concatenate(
            [
                jnp.where(low, wide[0:64, 0:128], wide[64:128, 0:128]),
                jnp.where(low, wide[128:192, 128:256], wide[192:256, 128:256]),
            ],
            axis=1,
        )

    at = [
        (rows_of(2 * b + n, BLOCK), slice(QUAD * g, QUAD * (g + 1))) for n in range(2) for g in range(HEADS // 4)
    ]
    dps = [dot_nt(grad_mix[i], spread_heads(v[i], mask)) for i in at]
    dvs = [own_head(dot_tn(probs[i], grad_mix[i])) for i in at]
    ps = [probs[i].astype(f32) for i in at]
    means = [per_head(dp * p, jnp.sum, 0.0) for dp, p in zip(dps, ps)]
    dss = [(p * (dp - m)).astype(bf16) for p, dp, m in zip(ps, dps, means)]
    dqs = [dot_nn(ds, spread_heads(k[i], mask)) * scale for i, ds in zip(at, dss)]
    dks = [own_head(dot_tn(ds, q[i])) * scale for i, ds in zip(at, dss)]
    for i, a, c, d in zip(at, dqs, dks, dvs):
        dq[i] = a.astype(bf16)
        dk[i] = c.astype(bf16)
        dv[i] = d.astype(bf16)


class Saves:
    def __init__(self, sems):
        self.sems, self.count, self.open = sems, 0, {}

    def start(self, name, src, dst):
        m = pltpu.make_async_copy(src, dst, self.sems.at[self.count])
        self.count += 1
        m.start()
        self.open[name] = m

    def wait(self, *names):
        for name in names:
            if name in self.open:
                self.open.pop(name).wait()

    def finish(self):
        self.wait(*list(self.open))


FORWARD_COPIES = 64
FORWARD_MODEL = SimpleNamespace(latency=(4.15, 0.96, 4.12), work=1.21, core=1.91, link=1.05, slack=0.0)
X, DF, A1, Q, K, V, PB, GP, H, O, Y, A2, GAINS, SLABS, INV = range(10, 25)


def forward_kernel(items, groups, trees, *refs):
    ref = bind(trees, refs)
    rows, width = ref.tokens.shape
    ff = ref.shards[FIRST].shape[1]
    parts = column_parts(ff, width)
    x, a1, q, k, v, pb, h, a2, e0, e1, e2, df = [ref.page.at[i] for i in range(12)]
    weight = [ref.weight.at[i] for i in range(4)]
    hidden, first, second = (e0, e1, e2), (q, k, v), (pb, h, x)
    wide = ref.wide
    gate_rows, mix_rows, mid_rows = [pl.ds(rows * i, rows) for i in range(3)]
    gp, o, y = wide.at[gate_rows], wide.at[mix_rows], wide.at[mid_rows]
    here = Place()
    ag = Gather(here, items, ref.shards, ref.full, ref.ssem, ref.rsem, ref.lsem)
    cp = Saves(ref.csem)
    size = 128
    lane = lax.broadcasted_iota(jnp.int32, (size, 128), 1)
    live_len = ref.lengths[0]

    def live(i, n):
        return lax.broadcasted_iota(jnp.int32, (n, 1), 0) + i * n < live_len

    def spread(values):
        return jnp.broadcast_to(values, (values.shape[0], 128))

    cp.start(X, ref.tokens, x)
    cp.start(DF, ref.cotangent, df)
    own_gain, place = ref.shards[GAIN][...].astype(f32), lax.rem(here.fs, 4)
    spots = jnp.concatenate([jnp.where(place == k, own_gain, 0.0) for k in range(4)], axis=1)
    ref.gain_block[...] = jnp.broadcast_to(spots, ref.gain_block.shape).astype(bf16)
    ref.shards[GAIN] = ref.gain_block
    here.barrier()

    def norm_in():
        cp.wait(X)

        def tile(i):
            r = rows_of(i, size)
            t = x[r, :].astype(f32)
            inv = rms_inv(t)
            a1[r, :] = (t * inv).astype(bf16)
            ref.inv[r, :] = spread(inv)

        tiles(rows // size, tile)
        cp.start(A1, a1, ref.save_a1)

    def mask_df():
        cp.wait(DF)

        def tile(i):
            r = rows_of(i, size)
            df[r, :] = jnp.where(live(i, size), df[r, :], jnp.zeros((), bf16))

        tiles(rows // size, tile)

    def load(slot, m, c0=0, w=None):
        src = ref.full[m]
        w = src.shape[-1] if w is None else w
        cp.start(slot, src.at[:, :, :, :, pl.ds(c0, w)], weight[slot].at[:, :, :, :, pl.ds(0, w)])

    def matrix(slot, w=None):
        w = width if w is None else w
        return weight[slot][:, :, :, :, 0:w].reshape(width, w)

    half_rows = rows // 2

    def projected(half, slot, dst, name=None, kept=None):
        def run():
            cp.wait(slot)
            r = pl.ds(half * half_rows, half_rows)
            dst[r, :] = dot_nn(a1[r, :], matrix(slot)).astype(dst.dtype)
            if kept is not None and half:
                cp.start(name, dst, kept)

        return run

    def gate_low():
        def tile(i):
            r = rows_of(i, size)
            e0[r, :] = gp[r, :].astype(bf16)

        tiles(rows // size, tile)
        cp.start(GP, e0, ref.save_gp)

    def attention(n, count):
        def run():
            tiles(count, lambda b: attend_blocks(b + n * count, q, k, v, pb, o))

        return run

    def mixed():
        cp.start(PB, pb, ref.save_pb)
        cp.wait(GAINS)
        gains = ref.gain
        gain = jnp.concatenate(
            [
                sum(gains[g, j, cc, 0:1, :].astype(f32) for j in (2 * half, 2 * half + 1) for cc in range(2))
                for g in range(4)
                for half in range(2)
            ],
            axis=1,
        )

        def tile(i):
            r = rows_of(i, size)
            t, z = o[r, :], gp[r, :]
            inv = rms_inv(t)
            h[r, :] = (t * inv * gain * (z * jax.nn.sigmoid(z))).astype(bf16)
            e1[r, :] = t.astype(bf16)
            ref.inv[r, :] = jnp.where(lane == 1, inv, ref.inv[r, :])

        tiles(rows // size, tile)
        cp.start(H, h, ref.save_h)
        cp.start(O, e1, ref.save_o)

    def middle(half, slot):
        def run():
            cp.wait(slot)
            r = pl.ds(half * half_rows, half_rows)
            y[r, :] = dot_nn(h[r, :], matrix(slot))

        return run

    def norm_middle():
        def tile(i):
            r = rows_of(i, size)
            t = x[r, :].astype(f32) + jnp.where(live(i, size), y[r, :], 0.0)
            inv = rms_inv(t)
            y[r, :] = t
            a2[r, :] = (t * inv).astype(bf16)
            ref.inv[r, :] = jnp.where(lane == 2, inv, ref.inv[r, :])

        tiles(rows // size, tile)
        cp.start(Y, y, ref.save_y)
        cp.start(A2, a2, ref.save_a2)

    def gated(j, s1, s2, part, count):
        c0, w = parts[j]
        saved = ((first[j], ref.save_g1), (second[j], ref.save_g2), (hidden[j], ref.save_e))

        def run():
            if part == 0:
                cp.wait(s1, s2, Q, K, V, PB, H, GP, O)
            r = pl.ds(part * (rows // count), rows // count)
            up = dot_nn(a2[r, :], matrix(s1, w))
            first[j][r, 0:w] = up.astype(bf16)
            other = dot_nn(a2[r, :], matrix(s2, w))
            second[j][r, 0:w] = other.astype(bf16)
            hidden[j][r, 0:w] = (up * other).astype(bf16)
            if part == count - 1:
                for n, (page, kept) in enumerate(saved):
                    cp.start((j, n), page.at[:, 0:w], kept.at[:, pl.ds(c0, w)])

        return run

    def down_grad(j, c0, w):
        def run():
            if j == 2:
                cp.wait(Y)
            wide[pl.ds(parts[j][0] + c0, w), :] = dot_tn(hidden[j][:, c0 : c0 + w], df[...])

        return run

    def down_slabs():
        slabs = ref.slabs
        n = slabs.shape[1]

        def tile(d):
            slabs[d] = wide[pl.ds(pl.multiple_of(d * n, 8), n), :].astype(bf16)

        tiles(slabs.shape[0], tile)
        cp.start(SLABS, slabs, ref.down_partial)

    work = []

    def piece(cost, f, needs=()):
        work.append((f, cost, needs, ()))

    piece(1.5, norm_in)
    piece(0.5, mask_df)
    for n in range(2):
        piece(1.15, projected(n, 0, q, Q, ref.save_q), (0,))
    for n in range(2):
        piece(1.15, projected(n, 1, k, K, ref.save_k), (1,))
    for n in range(2):
        piece(1.15, projected(n, 2, v, V, ref.save_v), (2,))
    for n in range(rows // BLOCK // 2):
        piece(1.0, attention(n, 1))
    for n in range(2):
        piece(1.15, projected(n, 3, gp), (3,))
    piece(0.5, gate_low)
    piece(1.5, mixed, (4,))
    for n in range(2):
        piece(1.1, middle(n, 0), (5,))
    piece(1.0, norm_middle)
    slots = ((1, 2), (3, 0), (1, 2))
    for j, (s1, s2) in enumerate(slots):
        for n in range(4):
            piece(1.3 * parts[j][1] / width, gated(j, s1, s2, n, 4), (6 + 2 * j, 7 + 2 * j))
    for j, (c0, w) in enumerate(parts):
        step = 512 if w % 512 == 0 else w // 2
        for n in range(w // step):
            piece(1.2, down_grad(j, n * step, step))
    piece(1.0, down_slabs)
    loads = {0: (0, QUERY), 1: (1, KEY), 2: (2, VALUE), 3: (3, GATE), 5: (0, OUT)}
    for j, (s1, s2) in enumerate(slots):
        loads[6 + 2 * j] = (s1, FIRST) + parts[j]
        loads[7 + 2 * j] = (s2, SECOND) + parts[j]
    readers = [sum(g in p[2] for p in work) for g in range(len(items))]
    ready, waiting, held = set(), [], {}

    def try_loads():
        while waiting:
            i = waiting[0]
            slot = loads[i][0]
            if slot in held and readers[held[slot]]:
                return
            held[slot] = i
            load(*loads[i])
            ready.add(i)
            waiting.pop(0)

    left = [sum(g == n for g in groups) for n in range(len(items))]

    def ended(i):
        group = groups[i]
        left[group] -= 1
        if left[group]:
            return
        if group in loads:
            waiting.append(group)
            try_loads()
        elif group == 4:
            cp.start(GAINS, ref.full[GAIN], ref.gain)
            ready.add(group)

    def reading(f, needs):
        def run():
            f()
            for i in needs:
                readers[i] -= 1
            try_loads()

        return run

    work = [(reading(f, needs), cost, needs, gives) for f, cost, needs, gives in work]
    Timeline(
        ag.timed_steps(), work, 3, range(len(items)), FORWARD_MODEL,
        can_run=lambda needs: all(i in ready for i in needs), ended=ended,
    ).run()
    ag.finish()
    cp.start(INV, ref.inv, ref.save_inv)
    cp.finish()


def forward(tokens, lengths, cotangent, shards):
    rows, width = tokens.shape
    operands = list(shards)
    shards = [jax.ShapeDtypeStruct((16, 128), bf16) if m == GAIN else w for m, w in enumerate(shards)]
    ff = shards[FIRST].shape[1]
    parts = column_parts(ff, width)
    whole = [(m, 0, width) for m in (QUERY, KEY, VALUE, GATE)] + [(GAIN, 0, shards[GAIN].shape[1]), (OUT, 0, width)]
    whole += [(m, c0, w) for c0, w in parts for m in (FIRST, SECOND)]
    pieces = [(m, c0 + d, w, g) for g, (m, c0, n) in enumerate(whole) for d, w in column_parts(n, 512)]
    pieces.sort(key=lambda p: (p[3] if p[3] < 6 else 6 + (p[3] - 6) // 2, p[1]))
    pieces += [(DOWN, c0, w, len(whole)) for c0, w in column_parts(width, 256)]
    items = [(m, c0, w, n % 6 == 0 and m not in (GAIN, DOWN)) for n, (m, c0, w, _) in enumerate(pieces)]
    groups = [p[3] for p in pieces]
    n = len(items)
    page, row = jax.ShapeDtypeStruct((rows, width), bf16), jax.ShapeDtypeStruct((rows, 128), f32)
    wide = jax.ShapeDtypeStruct((rows, ff), bf16)
    saves = dict(
        save_a1=page, save_q=page, save_k=page, save_v=page, save_pb=page, save_gp=page, save_o=page, save_h=page,
        save_a2=page, save_g1=wide, save_g2=wide, save_e=wide, save_y=jax.ShapeDtypeStruct((rows, width), f32),
        save_inv=row,
    )
    slab = (32,) + shards[DOWN].shape
    saves[DOWN_PARTIAL] = jax.ShapeDtypeStruct(slab, bf16)
    outs = dict(full=[jax.ShapeDtypeStruct((4, 4, 2) + s.shape, bf16) for s in shards])
    scratch = dict(
        page=pltpu.VMEM((12, rows, width), bf16),
        weight=pltpu.VMEM((4, 4, 4, 2, shards[QUERY].shape[0], width), bf16),
        wide=pltpu.VMEM((3 * rows, width), f32),
        slabs=pltpu.VMEM(slab, bf16),
        gain=pltpu.VMEM((4, 4, 2) + shards[GAIN].shape, bf16),
        gain_block=pltpu.VMEM(shards[GAIN].shape, bf16),
        inv=pltpu.VMEM((rows, 128), f32),
        ssem=pltpu.SemaphoreType.DMA((n, 12)),
        rsem=pltpu.SemaphoreType.DMA((n, 12)),
        lsem=pltpu.SemaphoreType.DMA((n,)),
        csem=pltpu.SemaphoreType.DMA((FORWARD_COPIES,)),
    )
    ins = dict(cotangent=cotangent, shards=operands, tokens=tokens)
    hbm, vmem = pl.BlockSpec(memory_space=pl.ANY), pl.BlockSpec(memory_space=pltpu.VMEM)
    leaves = jax.tree.leaves
    got = pl.pallas_call(
        functools.partial(forward_kernel, items, groups, (dict(lengths=0), ins, outs, saves, scratch)),
        out_shape=leaves(outs) + leaves(saves),
        in_specs=[pl.BlockSpec(memory_space=pltpu.SMEM), hbm] + [vmem] * len(shards) + [hbm],
        out_specs=[hbm] * len(leaves(outs) + leaves(saves)),
        scratch_shapes=leaves(scratch),
        compiler_params=pltpu.CompilerParams(
            collective_id=0, has_side_effects=True, vmem_limit_bytes=62 * 2**20
        ),
    )(lengths, *leaves(ins))
    full = got[: len(shards)]
    return full, jax.tree.unflatten(jax.tree.structure(saves), got[len(shards) :])


class Timeline:
    def __init__(self, steps, work, window, given, model, after=None, can_run=None, ended=None):
        self.steps, self.work, self.window, self.model = steps, list(work), window, model
        self.after = after or [set()] * len(steps)
        self.can_run = can_run or (lambda needs: all(n in self.done for n in needs))
        self.ended = ended or (lambda i: None)
        self.made = set(given)
        self.at = [0] * len(steps)
        self.when = [0.0] * len(steps)
        self.free = {}
        self.now = 3.0
        self.done = set()

    def next_steps(self):
        started = 0
        for i, at in enumerate(self.at):
            if at == 0:
                if i in self.made and started < self.window and self.after[i] <= self.done:
                    yield i
                return
            if at < len(self.steps[i]):
                started += at < 2
                yield i

    def step(self, i):
        run, link, link_us, core_us = self.steps[i][self.at[i]]
        self.now = max(self.now, self.when[i])
        run(i)
        self.now += core_us * self.model.core
        self.when[i] = self.now
        if link:
            sent = max(self.now, self.free.get(link, 0.0)) + link_us * self.model.link
            self.free[link] = sent
            self.when[i] = sent + self.model.latency[link - 1 if link in (1, 2) else 2]
        self.at[i] += 1
        if self.at[i] == len(self.steps[i]):
            self.done.add(i)
            self.ended(i)

    def run(self):
        while True:
            steps = list(self.next_steps())
            ready = [i for i in steps if self.when[i] <= self.now + self.model.slack]
            if ready:
                self.step(ready[0])
            elif self.work and self.can_run(self.work[0][2]):
                run, core_us, _, gives = self.work.pop(0)
                run()
                self.now += core_us * self.model.work
                for i in gives:
                    self.made.add(i)
                    self.when[i] = self.now + self.model.latency[2]
            elif steps:
                self.step(min(steps, key=lambda i: self.when[i]))
            else:
                return


BACKWARD_COPIES = 64
BACKWARD_MODEL = SimpleNamespace(latency=(4.71, 4.18, 2.15), work=1.15, core=1.38, link=1.14, slack=0.0)
PAGES = 9


def backward_kernel(items, trees, *refs):
    ref = bind(trees, refs)
    rows, width = ref.cotangent.shape
    ff = ref.full[FIRST].shape[1]
    parts = column_parts(ff, width)
    page = [ref.page.at[i] for i in range(PAGES)]
    acc, other = ref.wide.at[0], ref.wide.at[1]
    here = Place()
    bufs = ring_buffers(ref.rings)
    cp = Saves(ref.csem)
    made = sorted({(it.m, it.g0) for it in items if it.m not in (DOWN, GAIN)})
    items = [
        SimpleNamespace(
            **vars(it), out=ref.grads[it.m], s0=it.c0 - it.g0,
            src=ref.partials[made.index((it.m, it.g0))] if (it.m, it.g0) in made else ref.down_partial,
        )
        for it in items
    ]
    rs = Scatter(here, items, bufs, lambda i: cp.wait((items[i].m, items[i].g0)), ref.ssem, ref.rsem, ref.lsem, ref.free)
    size, half_rows = 128, rows // 2
    live_len = ref.lengths[0]

    def live(first, n):
        return lax.broadcasted_iota(jnp.int32, (n, 1), 0) + first < live_len

    def load(n, src, c0=None, w=None, by_row=False):
        dst = page[n]
        if c0 is not None:
            if by_row:
                src, dst = src.at[pl.ds(c0, w)], dst.at[pl.ds(0, w)]
            else:
                src, dst = src.at[:, pl.ds(c0, w)], dst.at[:, pl.ds(0, w)]
        cp.start(n, src, dst)

    def halves(f):
        return [functools.partial(f, pl.ds(half_rows * n, half_rows)) for n in range(2)]

    work = []

    def piece(cost, f, needs=(), gives=()):
        work.append((f, cost, needs, gives))

    staged = []

    def grad_item(m, c0, w, left, right):
        name = (m, c0)
        slot = len(staged) % 2
        used = staged[-2] if len(staged) > 1 else None
        staged.append(name)
        stage = ref.stage.at[slot]
        gives = [i for i, it in enumerate(items) if (it.m, it.g0) == name]

        def half(n):
            def run():
                if n == 0:
                    cp.wait(*[k for k in range(PAGES) if page[k] is left or page[k] is right], used)
                cols = slice(n * (width // 2), (n + 1) * (width // 2))
                got = dot_tn(left[:, cols], right[:, 0:w]).astype(bf16)
                stage[2 * n : 2 * n + 2, :, :, :, 0:w] = got.reshape((2,) + stage.shape[1:4] + (w,))
                if n == 1:
                    to = ref.partials[made.index(name)]
                    cp.start(name, stage.at[:, :, :, :, 0:w], to.at[:, :, :, :, 0:w])

            return run

        piece(1.15 * w / width, half(0))
        piece(1.15 * w / width, half(1), (), gives)

    load(0, ref.cotangent)
    load(2, ref.full[DOWN], *parts[0], by_row=True)
    load(4, ref.save_g2, *parts[0])
    load(3, ref.save_g1, *parts[0])
    cp.start(12, ref.save_inv, ref.inv)
    cp.start(15, ref.full_gain, ref.gain)

    here.barrier()

    def hidden_back(j, n):
        c0, w = parts[j]

        def run():
            cp.wait(0, 2, 3, 4)
            if n == 0 and j == 0:
                load(1, ref.save_a2)
                load(5, ref.full[FIRST], *parts[0])
                load(6, ref.full[SECOND], *parts[0])
            r = pl.ds(half_rows * n, half_rows)
            de = dot_nt(page[0][r, :], page[2][0:w, :])
            de = jnp.where(live(half_rows * n, half_rows), de, 0.0)
            page[7][r, 0:w] = (de * page[4][r, 0:w].astype(f32)).astype(bf16)
            page[8][r, 0:w] = (de * page[3][r, 0:w].astype(f32)).astype(bf16)
            if n == 1:
                if j + 1 < len(parts):
                    load(2, ref.full[DOWN], *parts[j + 1], by_row=True)
                    load(3, ref.save_g1, *parts[j + 1])
                    load(4, ref.save_g2, *parts[j + 1])
                else:
                    load(3, ref.save_o)
                    load(4, ref.save_gp)

        return run

    def mid_back(j, n, second):
        c0, w = parts[j]

        def run():
            up, weight = (8, 6) if second else (7, 5)
            cp.wait(weight)
            r = pl.ds(half_rows * n, half_rows)
            part = dot_nt(page[up][r, 0:w], page[weight][:, 0:w])
            acc[r, :] = part if j == 0 and not second else acc[r, :] + part
            if n == 1 and second:
                if j + 1 < len(parts):
                    load(5, ref.full[FIRST], *parts[j + 1])
                    load(6, ref.full[SECOND], *parts[j + 1])
                else:
                    load(5, ref.save_h)
                    load(6, ref.full[OUT])
                    load(7, ref.save_q)
                    load(8, ref.save_k)

        return run

    for j, (c0, w) in enumerate(parts):
        for n in range(2):
            piece(1.5 * w / width, hidden_back(j, n))
        grad_item(FIRST, c0, w, page[1], page[7])
        grad_item(SECOND, c0, w, page[1], page[8])
        for second in range(2):
            for n in range(2):
                piece(1.1 * w / width, mid_back(j, n, second))

    def middle_back():
        cp.wait(12, 1, 0)

        def tile(i):
            r = rows_of(i, size)
            up, n2 = acc[r, :], page[1][r, :].astype(f32)
            mean = jnp.mean(up * n2, axis=-1, keepdims=True)
            dy = page[0][r, :].astype(f32) + ref.inv[r, 2:3] * (up - n2 * mean)
            acc[r, :] = dy
            page[2][r, :] = jnp.where(live(i * size, size), dy, 0.0).astype(bf16)

        tiles(rows // size, tile)
        load(1, ref.save_a1)
        load(0, ref.save_v)

    piece(1.5, middle_back)
    grad_item(OUT, 0, width, page[5], page[2])

    def branch_back(n):
        def run():
            if n == 0:
                cp.wait(6)
                load(5, ref.save_pb)
            r = pl.ds(half_rows * n, half_rows)
            other[r, :] = dot_nt(page[2][r, :], page[6][...])

        return run

    for n in range(2):
        piece(1.1, branch_back(n))

    def mix_back(first, count):
        def run():
            cp.wait(15, 3, 4)
            gains = ref.gain
            gain = jnp.concatenate(
                [
                    sum(gains[g, j, cc, 0:1, :].astype(f32) for j in (2 * half, 2 * half + 1) for cc in range(2))
                    for g in range(4)
                    for half in range(2)
                ],
                axis=1,
            )
            terms = ref.gain_terms
            if first == 0:
                terms[...] = jnp.zeros_like(terms)

            def tile(i):
                r = rows_of(i + first, size)
                inv = ref.inv[r, 1:2]
                up, z = other[r, :], page[4][r, :].astype(f32)
                normed = page[3][r, :].astype(f32) * inv
                sig = jax.nn.sigmoid(z)
                upu = up * (z * sig)
                terms[...] += (upu * normed).reshape(size // 8, 8, width).sum(axis=0)
                page[4][r, :] = (up * normed * gain * sig * (1.0 + z * (1.0 - sig))).astype(bf16)
                dm = upu * gain
                mean = jnp.mean(dm * normed, axis=-1, keepdims=True)
                page[3][r, :] = (inv * (dm - normed * mean)).astype(bf16)

            tiles(count, tile)

        return run

    for n in range(2):
        piece(1.2, mix_back(n * (rows // size // 2), rows // size // 2))

    def gain_item():
        g, terms = bufs[GAIN_RING].g, ref.gain_terms
        for yx in range(4):
            for z in range(4):
                for c in range(2):
                    at = 128 * (2 * yx + z // 2)
                    g[0, yx, z, c] = terms[:, at : at + 128]

    piece(0.3, gain_item, (), [i for i, it in enumerate(items) if it.m == GAIN])
    grad_item(GATE, 0, width, page[1], page[4])

    def attention_back(n, count):
        def run():
            cp.wait(7, 8, 0, 5)
            q, k, v, pb, do, dq, dk, dv = [page[m] for m in (7, 8, 0, 5, 3, 3, 6, 2)]
            tiles(count, lambda b: attend_blocks_back(b + n * count, q, k, v, pb, do, dq, dk, dv))
            if n == rows // BLOCK // 2 - 1:
                load(5, ref.full[GATE])
                load(7, ref.full[QUERY])
                load(8, ref.full[KEY])
                load(0, ref.full[VALUE])

        return run

    for n in range(rows // BLOCK // 2):
        piece(1.6, attention_back(n, 1))
    grad_item(QUERY, 0, width, page[1], page[3])
    grad_item(KEY, 0, width, page[1], page[6])
    grad_item(VALUE, 0, width, page[1], page[2])

    def input_part(n, up, w, first, loads):
        def run():
            if n == 0:
                cp.wait(w)
            r = pl.ds(half_rows * n, half_rows)
            part = dot_nt(page[up][r, :], page[w][...])
            other[r, :] = part if first else other[r, :] + part
            if n == 1:
                for to, src, at in loads:
                    load(to, src, *parts[at], by_row=src is ref.full[DOWN])

        return run

    down, hidden = ref.full[DOWN], ref.save_e
    products = (
        (4, 5, True, [(5, hidden, 0)]), (3, 7, False, [(7, down, 0), (3, hidden, 1)]),
        (6, 8, False, [(8, down, 1), (6, hidden, 2)]), (2, 0, False, [(0, down, 2)]),
    )
    for product in products:
        for n in range(2):
            piece(1.1, input_part(n, *product))

    def input_back():
        cp.wait(1)

        def tile(i):
            r = rows_of(i, size)
            up, n1 = other[r, :], page[1][r, :].astype(f32)
            mean = jnp.mean(up * n1, axis=-1, keepdims=True)
            page[4][r, :] = (acc[r, :] + ref.inv[r, 0:1] * (up - n1 * mean)).astype(bf16)

        tiles(rows // size, tile)
        cp.start(4, page[4], ref.input_grad)
        cp.start(16, ref.save_y, acc)

    piece(1.5, input_back)

    def output_part(n, j, e, w):
        def run():
            if n == 0:
                cp.wait(e, w)
            count = parts[j][1]
            r = pl.ds(half_rows * n, half_rows)
            part = dot_nn(page[e][r, 0:count], page[w][0:count, :])
            other[r, :] = part if j == 0 else other[r, :] + part

        return run

    for j, (e, w) in enumerate(((5, 7), (3, 8), (6, 0))):
        for n in range(2):
            piece(1.1 * parts[j][1] / width, output_part(n, j, e, w))

    def output():
        cp.wait(16)

        def tile(i):
            r = rows_of(i, size)
            page[2][r, :] = (acc[r, :] + jnp.where(live(i * size, size), other[r, :], 0.0)).astype(bf16)

        tiles(rows // size, tile)
        cp.start(2, page[2], ref.layer_out)

    piece(1.0, output)

    given = [i for i, it in enumerate(items) if it.m == DOWN]
    Timeline(rs.timed_steps(), work, 6, given, BACKWARD_MODEL, rs.after()).run()
    rs.finish()
    cp.finish()


def backward(cotangent, lengths, full, got):
    rows, width = cotangent.shape
    flat = [w.reshape(-1, w.shape[-1]) for w in full]
    ff = flat[FIRST].shape[1]
    r_in, r_down = full[QUERY].shape[3], full[DOWN].shape[3]
    parts = column_parts(ff, width)
    made = [(m, c0, w) for c0, w in parts for m in (FIRST, SECOND)] + [(OUT, 0, width)]
    made += [(m, 0, width) for m in (GATE, QUERY, KEY, VALUE)]
    specs = [(DOWN, c0, w, 0, DOWN_RING) for c0, w in column_parts(width, 256)]
    for n, (m, c0, w) in enumerate(made):
        if m == GATE:
            specs.append((GAIN, 0, 128, 0, GAIN_RING))
        if n in (1, 3, 8):
            specs += [(m, c0, w // 2, c0, PLANE_RING), (m, c0 + w // 2, w // 2, c0, IN_RING)]
        else:
            specs.append((m, c0, w, c0, IN_RING))
    slots = (4, 5, 2, 1)
    items = scatter_plan(specs, slots)
    n = len(items)
    ins = dict(cotangent=cotangent, full=flat, full_gain=full[GAIN])
    ins |= {k: a for k, a in got.items() if k != DOWN_PARTIAL}
    ins |= dict(down_partial=got[DOWN_PARTIAL].reshape(full[DOWN].shape))
    shapes = [(r_down if m == DOWN else r_in, flat[m].shape[1]) for m in range(len(full))]
    shapes[GAIN] = (8, 128)
    page = jax.ShapeDtypeStruct((rows, width), bf16)
    outs = dict(layer_out=page, input_grad=page)
    partial = jax.ShapeDtypeStruct(full[QUERY].shape, bf16)
    outs |= dict(partials=[partial] * len(made))
    grads = dict(grads=[jax.ShapeDtypeStruct(s, f32) for s in shapes])
    scratch = dict(
        rings=[
            scatter_scratch(DOWN_RING, slots[DOWN_RING], r_down, 256, bf16),
            scatter_scratch(IN_RING, slots[IN_RING], r_in, width, bf16),
            scatter_scratch(PLANE_RING, slots[PLANE_RING], r_in, 512, bf16),
            scatter_scratch(GAIN_RING, slots[GAIN_RING], 8, 128, f32),
        ],
        stage=pltpu.VMEM((2,) + full[QUERY].shape, bf16),
        page=pltpu.VMEM((PAGES, rows, width), bf16),
        wide=pltpu.VMEM((2, rows, width), f32),
        inv=pltpu.VMEM((rows, 128), f32),
        gain=pltpu.VMEM(full[GAIN].shape, bf16),
        gain_terms=pltpu.VMEM((8, width), f32),
        ssem=pltpu.SemaphoreType.DMA((n, 9)),
        rsem=pltpu.SemaphoreType.DMA((n, 9)),
        lsem=pltpu.SemaphoreType.DMA((n,)),
        csem=pltpu.SemaphoreType.DMA((BACKWARD_COPIES,)),
        free=pltpu.SemaphoreType.REGULAR((len(slots), 6)),
    )
    hbm, vmem = pl.BlockSpec(memory_space=pl.ANY), pl.BlockSpec(memory_space=pltpu.VMEM)
    leaves = jax.tree.leaves
    out = pl.pallas_call(
        functools.partial(backward_kernel, items, (dict(lengths=0), ins, outs, grads, scratch)),
        out_shape=leaves(outs) + leaves(grads),
        in_specs=[pl.BlockSpec(memory_space=pltpu.SMEM)] + [hbm] * len(leaves(ins)),
        out_specs=[hbm] * len(leaves(outs)) + [vmem] * len(leaves(grads)),
        scratch_shapes=leaves(scratch),
        compiler_params=pltpu.CompilerParams(
            collective_id=1, has_side_effects=True, vmem_limit_bytes=63 * 2**20
        ),
    )(lengths, *leaves(ins))
    return bind((outs, grads), out)


def finish_kernel(count, *refs):
    ins, terms, outs, gain = refs[:count], refs[count], refs[count + 1 : 2 * count + 1], refs[2 * count + 1]
    held, (sems,) = refs[2 * count + 2 : -1], refs[-1:]
    reads = [pltpu.make_async_copy(ins[k], held[k], sems.at[0, k]) for k in range(count)]
    writes = [pltpu.make_async_copy(held[k], outs[k], sems.at[1, k]) for k in range(count)]
    for m in reads:
        m.start()
    part = lax.rem(lax.axis_index(AXES[1]), 4)
    row = jnp.sum(terms[...], axis=0, keepdims=True)
    gain[...] = sum(jnp.where(part == k, row[:, 32 * k : 32 * (k + 1)], 0.0) for k in range(4))
    for r, w in zip(reads, writes):
        r.wait()
        w.start()
    for w in writes:
        w.wait()


def finish(arrays, terms):
    count = len(arrays)
    hbm, vmem = pl.BlockSpec(memory_space=pl.ANY), pl.BlockSpec(memory_space=pltpu.VMEM)
    return pl.pallas_call(
        functools.partial(finish_kernel, count),
        out_shape=[jax.ShapeDtypeStruct(a.shape, a.dtype) for a in arrays] + [jax.ShapeDtypeStruct((1, 32), f32)],
        in_specs=[hbm] * count + [vmem],
        out_specs=[hbm] * count + [vmem],
        scratch_shapes=[pltpu.VMEM(a.shape, a.dtype) for a in arrays] + [pltpu.SemaphoreType.DMA((2, count))],
        compiler_params=pltpu.CompilerParams(vmem_limit_bytes=62 * 2**20),
    )(*arrays, terms)


def slice_body(
    tokens, lengths, cotangent, w_query, w_key, w_value, w_gate, w_out, out_gain, w_first, w_second, w_down,
):
    rows, width = tokens.shape[0] * tokens.shape[1], tokens.shape[2]
    flat_cotangent = cotangent.reshape(rows, width)
    shards = (w_query, w_key, w_value, w_gate, out_gain.reshape(1, -1), w_out, w_first, w_second, w_down)
    full, got = forward(tokens.reshape(rows, width), lengths, flat_cotangent, shards)
    back = backward(flat_cotangent, lengths, full, got)
    kept = [m for m in range(9) if m != GAIN]
    *whole, gain = finish([back.layer_out, back.input_grad] + [back.grads[m] for m in kept], back.grads[GAIN])
    grads = dict(zip(kept, whole[2:]))
    return (
        whole[0].reshape(tokens.shape), whole[1].reshape(tokens.shape),
        *[grads[m] for m in (QUERY, KEY, VALUE, GATE, OUT)], gain.reshape(32),
        *[grads[m] for m in (FIRST, SECOND, DOWN)],
    )


def solution(mesh):
    fits = (mesh.shape[AXES[0]], mesh.shape[AXES[1]]) == (4, 8)
    return jax.shard_map(
        slice_body if fits else general_body,
        mesh=mesh,
        in_specs=(
            P(AXES, None, None),
            P(AXES),
            P(AXES, None, None),
            P(AXES, None),
            P(AXES, None),
            P(AXES, None),
            P(AXES, None),
            P(AXES, None),
            P(AXES),
            P(AXES, None),
            P(AXES, None),
            P(AXES, None),
        ),
        out_specs=(
            P(AXES, None, None),
            P(AXES, None, None),
            P(AXES, None),
            P(AXES, None),
            P(AXES, None),
            P(AXES, None),
            P(AXES, None),
            P(AXES),
            P(AXES, None),
            P(AXES, None),
            P(AXES, None),
        ),
        check_vma=False,
    )
```
